512 devices in a mesh: member: 16 (over z), space: 32 (over y, x, core).
Axes of the slice: x: 4, y: 4, z: 16, core: 2. Of those that a mesh axis runs over, the one named last changes fastest.
Arguments:
- coarse_state: float32 [16, 3, 2048, 512], P('member', None, 'space'), may hold values from -6 to 6
- coarse_seabed: float32 [2048, 512], P('space'), may hold values from 0.2 to 1
- open_faces: int32 [2, 2048, 512], P(None, 'space'), may hold values 0 or 1
- fine_state: float32 [16, 3, 192, 128, 128], P('member', None, 'space'), may hold values from -6 to 6
- fine_seabed: float32 [192, 128, 128], P('space'), may hold values from 0.2 to 1
- slot_patch: int32 [192], replicated, may hold values from -1 to 63, as said below
- patch_anchor: int32 [64, 2], replicated, may hold values from 1 to 479, as said below
- gauge_cells: int32 [128], replicated, may hold values from 0 to 1048575
Outputs:
- coarse_out: float32 [16, 3, 2048, 512], P('member', None, 'space')
- fine_out: float32 [16, 3, 192, 128, 128], P('member', None, 'space')
- gauge_spread: float32 [16, 128], P('member')
The draws below stay inside these ranges and needn't reach their ends.
Inputs may be any that keep to these rules, and one draw needn't show every extreme that they name: `slot_patch`: every patch stands in exactly one slot; occupied slots of an owner come first; a quarter of the owners hold 6 patches, half hold one and a quarter none; no owner holds two patches with the same parent slab; empty slots hold -1. `patch_anchor`: entry [p, 0] lies in 1 .. 31; entry [p, 1] lies in 1 .. 223 for even p and in 257 .. 479 for odd p.
All inputs are finite; a program needn't handle non-finite values. No bound on the sum of `open_faces` on one device may be relied on, other than what follows from the above.
Results may differ from the reference program's by a relative error of at most 0.0003.
Values sent between devices are 32-bit elements; how exact they have to be, the bound alone decides.
A program may use at most 64 MiB of HBM per device.

```python
import jax
import jax.numpy as jnp
from jax import lax

CROWS = 64
CCOLS = 512
F = 128
REFINE = 4
PPD = 2
STEPS = 2
G = 128
B = 32
NR = 2048
MEMBERS = 16
NPATCH = 64
TOTAL_SLOTS = 192
N_SPACE = 32


def draw_slot_patch(key, part):
    key = jax.random.fold_in(key, 11)
    first_key, second_key = jax.random.split(key)
    parent_order = jax.random.permutation(first_key, N_SPACE).astype(jnp.int32)
    owner_order = jax.random.permutation(second_key, N_SPACE).astype(jnp.int32)
    position = jnp.arange(2 * N_SPACE, dtype=jnp.int32)
    group_index = position // 8
    within = position % 8
    rank_in_group = jnp.where(within < 6, 0, within - 5)
    slot_index = jnp.where(within < 6, within, 0)
    owner_index = owner_order[4 * group_index + rank_in_group]
    half_span = N_SPACE // 2
    parent_index = jnp.where(position < N_SPACE, parent_order[position % N_SPACE], parent_order[(position - N_SPACE + half_span) % N_SPACE])
    side_index = jnp.where(position < N_SPACE, 0, 1)
    patch_ids = parent_index * 2 + side_index
    slot_table = jnp.full((N_SPACE, 6), -1, jnp.int32).at[owner_index, slot_index].set(patch_ids)
    return slot_table.reshape(-1)


def draw_patch_anchor(key, part):
    key = jax.random.fold_in(key, 12)
    first_key, second_key = jax.random.split(key)
    row_first = jax.random.randint(first_key, (NPATCH,), 1, CROWS - B)
    half_cols = CCOLS // 2
    col_first = jax.random.randint(second_key, (NPATCH,), 1, half_cols - B) + jnp.arange(NPATCH) % 2 * half_cols
    return jnp.stack([row_first, col_first], axis=1).astype(jnp.int32)


def set_ends(values, stream_key, low, high):
    longest = values.shape.index(max(values.shape))
    spots = []
    for shift in (0, 1):
        where = [jax.random.randint(jax.random.fold_in(stream_key, axis), (), 0, length) for axis, length in enumerate(values.shape)]
        where[longest] = (where[longest] + shift) % values.shape[longest]
        spots.append(tuple(where))
    return values.at[spots[0]].set(low).at[spots[1]].set(high)


def levels(rng, dims, cuts, low, top_value):
    gain, own = 1.0, jax.random.fold_in(rng, 6)
    for dim, blocks in cuts:
        draws = jnp.exp(jax.random.uniform(jax.random.fold_in(own, dim), (blocks,), jnp.float32, low / len(cuts), top_value / len(cuts)))
        gain = gain * jnp.repeat(draws, dims[dim] // blocks).reshape([-1 if axis == dim else 1 for axis in range(len(dims))])
    return gain


def centred(rng, shape, width, limit, cuts=(), held_as=jnp.bfloat16):
    entries = jax.random.normal(rng, shape, jnp.float32) * width
    if len(cuts) > 0:
        entries = levels(rng, shape, cuts, -0.22, 0.18) * entries
    return jnp.clip(entries, min=-limit, max=limit).astype(held_as)


def setup_inputs(seed: int = 0) -> dict:
    key_of = jax.random.split(jax.random.key(seed), 9)
    return {
        "coarse_state": centred(key_of[0], (MEMBERS, 3, NR, CCOLS), 1.0, 6.0, ((0, 16), (2, 32)), jnp.float32),
        "coarse_seabed": jnp.clip(0.2 + 0.8 * jax.random.uniform(key_of[1], (NR, CCOLS), jnp.float32) ** levels(key_of[1], (NR, CCOLS), ((0, 32),), -0.2, 0.2), 0.2, 1.0),
        "open_faces": set_ends((jax.random.randint(key_of[2], (2, NR, CCOLS), 0, 10) < 9).astype(jnp.int32), jax.random.fold_in(key_of[2], 1), 0, 1),
        "fine_state": centred(key_of[3], (MEMBERS, 3, TOTAL_SLOTS, F, F), 1.0, 6.0, ((0, 16), (2, 32)), jnp.float32),
        "fine_seabed": jnp.clip(0.2 + 0.8 * jax.random.uniform(key_of[4], (TOTAL_SLOTS, F, F), jnp.float32) ** levels(key_of[4], (TOTAL_SLOTS, F, F), ((0, 32),), -0.2, 0.2), 0.2, 1.0),
        "slot_patch": draw_slot_patch(jax.random.fold_in(key_of[8], 71), 0),
        "patch_anchor": draw_patch_anchor(jax.random.fold_in(key_of[8], 71), 0),
        "gauge_cells": set_ends(jax.random.randint(key_of[7], (G,), 0, NR * CCOLS), jax.random.fold_in(key_of[7], 1), 0, (NR * CCOLS) - 1).astype(jnp.int32),
    }


courant = 0.5


def coarse_advance(fields, seabed, open_faces):
    height = fields[:, 0]
    east_flux = fields[:, 1]
    north_flux = fields[:, 2]
    zero_column = jnp.zeros_like(height[..., :1])
    zero_row = jnp.zeros_like(height[:, :1, :])
    west_flux = jnp.concatenate([zero_column, east_flux[..., :-1]], axis=-1)
    south_flux = jnp.concatenate([zero_row, north_flux[:, :-1, :]], axis=1)
    height_new = height - courant * (east_flux - west_flux + north_flux - south_flux)
    height_up = jnp.concatenate([height_new[:, 1:, :], zero_row], axis=1)
    height_right = jnp.concatenate([height_new[..., 1:], zero_column], axis=-1)
    open_east = open_faces[0].astype(jnp.float32)
    open_north = open_faces[1].astype(jnp.float32)
    east_new = open_east * (east_flux - courant * seabed * (height_right - height_new))
    north_new = open_north * (north_flux - courant * seabed * (height_up - height_new))
    return jnp.stack([height_new, east_new, north_new], axis=1)


def cycle_values(both_times, row_start, col_start, block_len):
    members = both_times.shape[0]
    anchor = jnp.zeros((), jnp.int32)
    row_first = (row_start - 1).astype(jnp.int32)
    col_first = (col_start - 1).astype(jnp.int32)
    region = lax.dynamic_slice(both_times, (anchor, anchor, anchor, row_first, col_first), (members, 2, 3, block_len + 2, block_len + 2))
    west_side = region[:, :, 1, 1:block_len + 1, 0]
    south_side = region[:, :, 2, 0, 1:block_len + 1]
    east_side = region[:, :, 0, 1:block_len + 1, block_len + 1]
    north_side = region[:, :, 0, block_len + 1, 1:block_len + 1]
    return jnp.concatenate([west_side, south_side, east_side, north_side], axis=-1)


def fine_advance(fine_fields, fine_seabed, ghosts, refine):
    height = fine_fields[:, 0]
    east_flux = fine_fields[:, 1]
    north_flux = fine_fields[:, 2]
    fine_len = height.shape[-1]
    spread = jnp.repeat(ghosts, refine, axis=-1)
    old_edges = spread[:, :, 0]
    new_edges = spread[:, :, 1]
    for substep in range(refine):
        flux_weight = (2 * substep + 1) / (2.0 * refine)
        level_weight = (substep + 1) / float(refine)
        flux_edge = old_edges + flux_weight * (new_edges - old_edges)
        level_edge = old_edges + level_weight * (new_edges - old_edges)
        west_edge = flux_edge[..., 0:fine_len]
        south_edge = flux_edge[..., fine_len:2 * fine_len]
        east_edge = level_edge[..., 2 * fine_len:3 * fine_len]
        north_edge = level_edge[..., 3 * fine_len:4 * fine_len]
        west_flux = jnp.concatenate([west_edge[..., :, None], east_flux[..., :-1]], axis=-1)
        south_flux = jnp.concatenate([south_edge[..., None, :], north_flux[..., :-1, :]], axis=-2)
        height = height - courant * (east_flux - west_flux + north_flux - south_flux)
        height_right = jnp.concatenate([height[..., 1:], east_edge[..., :, None]], axis=-1)
        height_up = jnp.concatenate([height[..., 1:, :], north_edge[..., None, :]], axis=-2)
        east_flux = east_flux - courant * fine_seabed * (height_right - height)
        north_flux = north_flux - courant * fine_seabed * (height_up - height)
    return jnp.stack([height, east_flux, north_flux], axis=1)


def block_average(fine_fields, block_len, refine):
    members = fine_fields.shape[0]
    slot_count = fine_fields.shape[2]
    height_means = fine_fields[:, 0].reshape(members, slot_count, block_len, refine, block_len, refine).mean(axis=(3, 5))
    east_means = fine_fields[:, 1][..., refine - 1::refine].reshape(members, slot_count, block_len, refine, block_len).mean(axis=3)
    north_means = fine_fields[:, 2][..., refine - 1::refine, :].reshape(members, slot_count, block_len, block_len, refine).mean(axis=4)
    return jnp.stack([height_means, east_means, north_means], axis=1)


def reference(coarse_state, coarse_seabed, open_faces, fine_state, fine_seabed, slot_patch, patch_anchor, gauge_cells):
    occupied = (slot_patch >= 0).astype(jnp.float32)
    parent_rows = ((jnp.arange(NPATCH, dtype=jnp.int32) // PPD) * CROWS + patch_anchor[:, 0]).astype(jnp.int32)
    col_starts = patch_anchor[:, 1].astype(jnp.int32)
    safe_patch = jnp.clip(slot_patch, 0, NPATCH - 1).astype(jnp.int32)
    slot_of = jnp.zeros((NPATCH,), jnp.int32).at[jnp.where(slot_patch >= 0, slot_patch, NPATCH).astype(jnp.int32)].set(
        jnp.arange(TOTAL_SLOTS, dtype=jnp.int32), mode="drop")

    def one_member(member_pair):
        fields = member_pair[0][None]
        fine_fields = member_pair[1][None] * occupied[None, None, :, None, None]
        for step_index in range(STEPS):
            advanced = coarse_advance(fields, coarse_seabed, open_faces)
            both_times = jnp.stack([fields, advanced], axis=1)
            cycle_stack = jax.vmap(lambda row_first, col_first: cycle_values(both_times, row_first, col_first, B))(parent_rows, col_starts)
            ghosts = cycle_stack[safe_patch] * occupied[:, None, None, None]
            ghosts = jnp.transpose(ghosts, (1, 0, 2, 3))
            fine_fields = fine_advance(fine_fields, fine_seabed, ghosts, REFINE) * occupied[None, None, :, None, None]
            averages = block_average(fine_fields, B, REFINE)
            patch_means = averages[:, :, slot_of]

            def place_block(patch_index, current):
                which = jnp.asarray(patch_index).astype(jnp.int32)
                anchor = jnp.zeros((), jnp.int32)
                block_piece = lax.dynamic_index_in_dim(patch_means, which, 2, keepdims=False)
                return lax.dynamic_update_slice(current, block_piece, (anchor, anchor, parent_rows[which], col_starts[which]))

            fields = lax.fori_loop(0, NPATCH, place_block, advanced)
        readings = fields[0, 0].reshape(-1)[gauge_cells]
        return fields[0], fine_fields[0], readings

    coarse_out, fine_out, readings = lax.map(one_member, (coarse_state, fine_state))
    weights = 1.0 + 2.0 * jnp.arange(MEMBERS, dtype=jnp.float32) / (MEMBERS - 1)
    weights = weights / jnp.sum(weights)
    center = jnp.sum(weights[:, None] * readings, axis=0)
    return coarse_out, fine_out, readings - center
```

```python
import functools

import jax
import jax.numpy as jnp
from jax import lax
from jax.experimental import pallas as pl
from jax.experimental.pallas import tpu as pltpu
from jax.sharding import PartitionSpec as P

REFINE = 4
C = 0.5
MESH = pl.DeviceIdType.MESH
f32 = jnp.float32
NT = (((1,), (1,)), ((), ()))
NN = (((1,), (0,)), ((), ()))


def dot(a, b, dims=NN):
    return lax.dot_general(
        a, b, dims, precision=lax.Precision.HIGHEST, preferred_element_type=f32
    )


def iota(shape, dim):
    return lax.broadcasted_iota(jnp.int32, shape, dim)


def roll(x, shift, axis):
    return pltpu.roll(x, shift, axis)


def kernel(
    ns, nm, slots,
    slot, anchor, gauge, coarse, seabed, faces, fine, fseabed,
    coarse_out, fine_out, spread_out,
    cs, sd, op, t1, t2, ex, ce, cn, fh, fu, fv, fd,
    up_s, dn_s, up_r, dn_r, rs, pay_s, pay_r, xb, gx, ycol, yrow, red, tp,
    m1_p, m1_s, m1_r, a2_p, a2_s, a2_r, pz, cout, z_s, z_r, g_s, g_r, sidx,
    in_sem, out_sem, send_sem, recv_sem,
):
    me = lax.axis_index("space")
    mem = lax.axis_index("member")
    rows, cols = sd.shape
    fl = fu.shape[-1]
    bl = fl // REFINE
    nb = slots * 8

    loads = [
        pltpu.make_async_copy(coarse.at[0], cs, in_sem.at[0]),
        pltpu.make_async_copy(seabed, sd, in_sem.at[1]),
        pltpu.make_async_copy(faces, op, in_sem.at[2]),
        pltpu.make_async_copy(fine.at[0, 0], fh.at[:, pl.ds(8, fl), :], in_sem.at[3]),
        pltpu.make_async_copy(fine.at[0, 1], fu, in_sem.at[4]),
        pltpu.make_async_copy(fine.at[0, 2], fv.at[:, pl.ds(8, fl), :], in_sem.at[5]),
        pltpu.make_async_copy(fseabed, fd, in_sem.at[6]),
    ]
    for load in loads:
        load.start()

    barrier = pltpu.get_barrier_semaphore()

    def greet_space(k, carry):
        pl.semaphore_signal(
            barrier, inc=1, device_id=(mem, lax.rem(me + k, ns)), device_id_type=MESH
        )
        return carry

    def greet_member(k, carry):
        pl.semaphore_signal(
            barrier, inc=1, device_id=(lax.rem(mem + k, nm), me), device_id_type=MESH
        )
        return carry

    lax.fori_loop(1, ns, greet_space, 0)
    lax.fori_loop(1, nm, greet_member, 0)

    my_patch = [slot[me * slots + s] for s in range(slots)]
    held_parent = [p >> 1 for p in my_patch]

    def find_slot(k, carry):
        d = lax.rem(me + k + 1, ns)
        which = jnp.int32(0)
        for s in range(1, slots):
            which = jnp.where(held_parent[s] == d, s, which)
        sidx[k] = which
        return carry

    lax.fori_loop(0, ns, find_slot, 0)

    def find_owner(i, carry):
        p = slot[i]
        return tuple(
            jnp.where(p == 2 * me + j, i, carry[j]) for j in range(2)
        )

    where_held = lax.fori_loop(0, ns * slots, find_owner, (jnp.int32(0), jnp.int32(0)))
    owner_at = [lax.rem(me - w // slots - 1 + 2 * ns, ns) for w in where_held]
    r0 = [jnp.clip(anchor[0, 2 * me + j], 1, rows - bl - 1) for j in range(2)]
    c0 = [jnp.clip(anchor[1, 2 * me + j], 1, cols - bl - 1) for j in range(2)]

    lane = iota((1, 128), 1)
    row8 = iota((8, 128), 0)
    lane8 = iota((8, 128), 1)
    rowc = iota((rows, cols), 0)
    lanec = iota((rows, cols), 1)
    lane1 = iota((1, cols), 1)
    block = None
    for j in range(2):
        inside = (
            (rowc >= r0[j]) & (rowc < r0[j] + bl) & (lanec >= c0[j]) & (lanec < c0[j] + bl)
        )
        block = inside if block is None else block | inside

    def west(x):
        first = iota(x.shape, 1) == 0
        return jnp.where(first, 0.0, roll(x, 1, 1))

    def east(x):
        last = iota(x.shape, 1) == cols - 1
        return jnp.where(last, 0.0, roll(x, cols - 1, 1))

    def south(x, below):
        return jnp.where(rowc == 0, below, roll(x, 1, 0))

    def north(x, above):
        return jnp.where(rowc == rows - 1, above, roll(x, rows - 1, 0))

    for load in loads[:3]:
        load.wait()
    h0, u0, v0 = cs[0], cs[1], cs[2]
    oe = op[0].astype(f32)
    on = op[1].astype(f32)
    cd = C * sd[...]
    ce[...] = cd * oe
    cn[...] = cd * on
    h1 = h0 - C * (u0 - west(u0) + v0 - south(v0, 0.0))
    t1[0] = h1
    up_s[0:1, :] = h1[rows - 1 : rows]
    up_s[1:2, :] = v0[rows - 1 : rows]
    up_s[2:3, :] = on[rows - 1 : rows]
    up_s[3:4, :] = cn[rows - 1 : rows, :]
    up_s[4:8, :] = jnp.zeros((4, cols), f32)
    dn_s[0:1, :] = h1[0:1]
    dn_s[1:2, :] = u0[0:1]
    dn_s[2:3, :] = v0[0:1]
    dn_s[3:4, :] = h1[1:2]
    dn_s[4:5, :] = oe[0:1]
    dn_s[5:6, :] = ce[0:1, :]
    dn_s[6:7, :] = on[0:1]
    dn_s[7:8, :] = cn[0:1, :]

    pl.semaphore_wait(barrier, ns + nm - 2)

    up = pltpu.make_async_remote_copy(
        src_ref=up_s, dst_ref=up_r, send_sem=send_sem.at[0], recv_sem=recv_sem.at[0],
        device_id=(mem, lax.rem(me + 1, ns)), device_id_type=MESH,
    )
    down = pltpu.make_async_remote_copy(
        src_ref=dn_s, dst_ref=dn_r, send_sem=send_sem.at[1], recv_sem=recv_sem.at[1],
        device_id=(mem, lax.rem(me + ns - 1, ns)), device_id_type=MESH,
    )
    up.start()
    down.start()

    xb[...] = jnp.zeros(xb.shape, f32)
    gx[...] = jnp.zeros(gx.shape, f32)
    tp[...] = jnp.zeros(tp.shape, f32)
    pz[...] = jnp.zeros(pz.shape, f32)
    rs[...] = jnp.zeros(rs.shape, f32)

    up.wait()
    down.wait()

    low = me > 0
    high = me < ns - 1
    h1_m = up_r[0:1, :]
    v0_m = jnp.where(low, up_r[1:2, :], 0.0)
    h1 = jnp.where(rowc == 0, h1 + C * v0_m, h1)
    h1_p = jnp.where(high, dn_r[0:1, :] + C * v0[rows - 1 : rows], 0.0)
    u1 = oe * u0 - ce[...] * (east(h1) - h1)
    v1 = on * v0 - cn[...] * (north(h1, h1_p) - h1)
    u1_p = dn_r[4:5, :] * dn_r[1:2, :] - dn_r[5:6, :] * (east(h1_p) - h1_p)
    v1_p = dn_r[6:7, :] * dn_r[2:3, :] - dn_r[7:8, :] * (dn_r[3:4, :] - h1_p)
    v1_m = jnp.where(
        low, up_r[2:3, :] * v0_m - up_r[3:4, :] * (h1[0:1] - h1_m), 0.0
    )
    h2_p = jnp.where(
        high, h1_p - C * (u1_p - west(u1_p) + v1_p - v1[rows - 1 : rows]), 0.0
    )
    h1 = jnp.where(block, 0.0, h1)
    u1 = jnp.where(block, 0.0, u1)
    v1 = jnp.where(block, 0.0, v1)
    h2 = h1 - C * (u1 - west(u1) + v1 - south(v1, v1_m))
    t1[0], t1[1], t1[2] = h1, u1, v1
    t2[...] = h2
    u2 = oe * u1 - ce[...] * (east(h2) - h2)
    v2 = on * v1 - cn[...] * (north(h2, h2_p) - h2)
    for f, held in enumerate((h0, h1, h2, u0, u1, u2, ce, v0, v1, v2, cn)):
        for tile in range(cols // 128):
            ex[f, tile] = held[:, 128 * tile : 128 * tile + 128]

    payload = None
    for j in range(2):
        cw = c0[j] - 1
        ch = c0[j] + bl
        tw = cw >> 7
        te = ch >> 7
        span = pl.ds(r0[j], bl)
        west_stack = jnp.concatenate(
            [ex[3 + t, tw, span, :] for t in range(4)], axis=0
        )
        east_stack = jnp.concatenate(
            [ex[t, te, span, :] for t in range(3)] + [jnp.full((bl, 128), -1.0, f32)],
            axis=0,
        )
        pick_w = jnp.where((row8 == 1) & (lane8 == (cw & 127)), 1.0, 0.0)
        pick_e = jnp.where((row8 == 0) & (lane8 == (ch & 127)), 1.0, 0.0)
        sides = dot(pick_w, west_stack, NT) + dot(pick_e, east_stack, NT)
        first = c0[j] >> 7
        second = jnp.minimum(first + 1, cols // 128 - 1)
        north_row = pl.ds(r0[j] + bl, 1)
        south_row = pl.ds(r0[j] - 1, 1)
        for t in range(4):
            moved = []
            for half, tile in enumerate((first, second)):
                if t < 3:
                    rs[j, t, half, 2:3, :] = ex[t, tile, north_row, :]
                else:
                    rs[j, t, half, 2:3, :] = jnp.full((1, 128), -1.0, f32)
                rs[j, t, half, 3:4, :] = ex[7 + t, tile, south_row, :]
                moved.append(roll(rs[j, t, half], (32 * t - c0[j]) & 127, 1))
            kept = lane8 - 32 * t < 128 - (c0[j] & 127)
            picked = jnp.where(kept, moved[0], moved[1])
            here = (row8 >= 2) & (row8 < 4) & (lane8 >= 32 * t) & (lane8 < 32 * t + 32)
            sides = jnp.where(here, picked, sides)
        sides = jnp.where(row8 < 4, sides, 0.0)
        payload = sides if j == 0 else payload + roll(sides, 4, 0)
    pay_s[...] = payload
    pay_r[ns - 1] = payload

    def spread_payload(k, carry):
        pltpu.make_async_remote_copy(
            src_ref=pay_s, dst_ref=pay_r.at[k], send_sem=send_sem.at[2],
            recv_sem=recv_sem.at[2], device_id=(mem, lax.rem(me + k + 1, ns)),
            device_id_type=MESH,
        ).start()
        return carry

    lax.fori_loop(0, ns - 1, spread_payload, 0)

    def all_of(ref, count, sem):
        part = ref.at[pl.ds(0, count)]
        pltpu.make_async_copy(part, part, sem).wait()

    rc_i = iota((fl, 128), 0)
    rc_l = iota((fl, 128), 1)
    spread_rows = jnp.where((rc_l & 31) == (rc_i >> 2), 1.0, 0.0)
    spread_lanes = jnp.where((rc_i & 31) == (rc_l >> 2), 1.0, 0.0)
    mean_h = jnp.where((rc_i >> 2) == rc_l, 0.25, 0.0)
    mean_u = jnp.where(rc_i == 4 * (rc_l - 32) + 3, 1.0, 0.0)
    mean_v = jnp.where((rc_i >> 2) == rc_l - 64, 0.25, 0.0)
    lane_nb = iota((nb, 128), 1)

    def expand(old, diff):
        both = jnp.concatenate([old, diff], axis=0)
        ycol[:, 0 : 2 * nb] = dot(spread_rows, both, NT)
        yrow[...] = dot(both, spread_lanes)

    def fine_steps(last):
        lane_f = iota((fl, 128), 1)

        def one_slot(s, carry):
            ego = roll(ycol[...], 127 - 8 * s, 1)
            egd = roll(ycol[...], lax.rem(255 - 8 * s - nb, 128), 1)
            n_old = yrow[pl.ds(8 * s + 2, 1), :]
            s_old = yrow[pl.ds(8 * s + 3, 1), :]
            n_dif = yrow[pl.ds(nb + 8 * s + 2, 1), :]
            s_dif = yrow[pl.ds(nb + 8 * s + 3, 1), :]
            cdf = C * fd[s]
            used = slot[me * slots + s] >= 0
            for k in range(REFINE):
                wf = (2 * k + 1) / (2.0 * REFINE)
                wl = (k + 1) / float(REFINE)
                edge = ego + jnp.where(lane == fl - 1, wl, wf) * egd
                u = fu[s]
                fv[s, 7:8, :] = s_old + wf * s_dif
                v = fv[s, 8 : 8 + fl, :]
                v_s = fv[s, 7 : 7 + fl, :]
                u_w = jnp.where(lane_f == 0, edge, roll(u, 1, 1))
                h = fh[s, 8 : 8 + fl, :] - C * (u - u_w + v - v_s)
                fh[s, 8 : 8 + fl, :] = h
                fh[s, 8 + fl : 9 + fl, :] = n_old + wl * n_dif
                h_e = jnp.where(lane_f == fl - 1, edge, roll(h, fl - 1, 1))
                h_n = fh[s, 9 : 9 + fl, :]
                u = u - cdf * (h_e - h)
                v = v - cdf * (h_n - h)
                if last and k == REFINE - 1:
                    fh[s, 8 : 8 + fl, :] = jnp.where(used, h, 0.0)
                    u = jnp.where(used, u, 0.0)
                    v = jnp.where(used, v, 0.0)
                fu[s] = u
                fv[s, 8 : 8 + fl, :] = v
            return carry

        lax.fori_loop(0, slots, one_slot, 0)

    def averages():
        for s in range(slots):
            span = slice(bl * s, bl * s + bl)
            parts = [fh[s, pl.ds(8 + i, bl, stride=4), :] for i in range(REFINE)]
            red[0, span, :] = 0.25 * ((parts[0] + parts[1]) + (parts[2] + parts[3]))
            parts = [fu[s, pl.ds(i, bl, stride=4), :] for i in range(REFINE)]
            red[1, span, :] = 0.25 * ((parts[0] + parts[1]) + (parts[2] + parts[3]))
            red[2, span, :] = fv[s, pl.ds(11, bl, stride=4), :]
        return dot(red[0], mean_h) + dot(red[1], mean_u) + dot(red[2], mean_v)

    for load in loads[3:]:
        load.wait()
    all_of(pay_r, ns - 1, recv_sem.at[2])

    for s in range(slots):
        p = jnp.maximum(my_patch[s], 0)
        at = lax.rem(me - (p >> 1) - 1 + 2 * ns, ns)
        got = pay_r[at, pl.ds((p & 1) * 4, 4), :]
        xb[8 * s : 8 * s + 4, :] = jnp.where(my_patch[s] >= 0, got, 0.0)

    x = xb[...]
    left = lane_nb < 32
    expand(
        jnp.where(left, x, 0.0), jnp.where(left, roll(x, 96, 1) - x, 0.0)
    )
    fine_steps(False)

    mean = averages()
    pick_i = iota((16, 128), 0)
    pick_l = iota((16, 128), 1)
    pick = jnp.where((pick_i == 0) & (pick_l == 63), C, 0.0)
    pick = pick + jnp.where((pick_i == 1) & (pick_l == 0), 1.0, 0.0)
    pick = pick - jnp.where((pick_i == 1) & ((pick_l == 32) | (pick_l == 64)), C, 0.0)
    pick = pick + jnp.where((pick_i == 9) & (pick_l == 64), C, 0.0)
    for s in range(slots):
        tp[s, 64:96, :] = mean[bl * s : bl * s + bl]
    for s in range(slots):
        side = dot(pick, tp[s], NT)
        side = side[0:8] + roll(side[8:16], 1, 1)
        gx[8 * s : 8 * s + 2, :] = side[0:2]
        top = tp[s, 95:96, :]
        low_row = tp[s, 64:65, :]
        gx[8 * s + 2 : 8 * s + 3, :] = C * top
        gx[8 * s + 3 : 8 * s + 4, :] = roll(low_row, 64, 1) - C * (
            roll(low_row, 32, 1) - jnp.where(lane > 64, roll(low_row, 33, 1), 0.0) + low_row
        )
    new = x - roll(x, 96, 1) * gx[...]
    mid = (lane_nb >= 64) & (lane_nb < 96)
    expand(
        jnp.where((lane_nb >= 32) & (lane_nb < 64), x, 0.0),
        jnp.where(mid, new - roll(x, 32, 1), 0.0),
    )
    packed = jnp.zeros((nb, 128), f32)
    row_nb = iota((nb, 128), 0) & 7
    for q in range(4):
        here = (row_nb == q) & (lane_nb >= 32 * q) & (lane_nb < 32 * q + 32)
        packed = jnp.where(here, roll(new, (32 * q + 64) % 128, 1), packed)
    for s in range(slots):
        m1_p[s] = jnp.sum(packed[8 * s : 8 * s + 8], axis=0, keepdims=True)

    def send_cycle(k, carry):
        m1_s[k] = m1_p[sidx[k]]
        pltpu.make_async_remote_copy(
            src_ref=m1_s.at[k], dst_ref=m1_r.at[k], send_sem=send_sem.at[3],
            recv_sem=recv_sem.at[3], device_id=(mem, lax.rem(me + k + 1, ns)),
            device_id_type=MESH,
        ).start()
        return carry

    lax.fori_loop(0, ns - 1, send_cycle, 0)
    m1_r[ns - 1] = m1_p[sidx[ns - 1]]

    fine_steps(True)
    stores = [
        pltpu.make_async_copy(fh.at[:, pl.ds(8, fl), :], fine_out.at[0, 0], out_sem.at[0]),
        pltpu.make_async_copy(fu, fine_out.at[0, 1], out_sem.at[1]),
        pltpu.make_async_copy(fv.at[:, pl.ds(8, fl), :], fine_out.at[0, 2], out_sem.at[2]),
    ]

    mean = averages()
    for s in range(slots):
        tail = mean[bl * s + 24 : bl * s + 32]
        for i in range(3):
            piece = mean[bl * s + 8 * i : bl * s + 8 * i + 8]
            a2_p[s, 8 * i : 8 * i + 8, :] = jnp.where(
                lane8 < 96, piece, roll(tail, 96 - 32 * i, 1)
            )

    def send_mean(k, carry):
        a2_s[k] = a2_p[sidx[k]]
        pltpu.make_async_remote_copy(
            src_ref=a2_s.at[k], dst_ref=a2_r.at[k], send_sem=send_sem.at[4],
            recv_sem=recv_sem.at[4], device_id=(mem, lax.rem(me + k + 1, ns)),
            device_id_type=MESH,
        ).start()
        return carry

    lax.fori_loop(0, ns - 1, send_mean, 0)
    a2_r[ns - 1] = a2_p[sidx[ns - 1]]
    for store in stores:
        store.start()

    all_of(m1_r, ns - 1, recv_sem.at[3])
    rowh = iota((rows, 128), 0)
    laneh = iota((rows, 128), 1)
    h2 = t2[...]
    fixes = []
    for j in range(2):
        got = m1_r[owner_at[j]]
        match = (laneh & 31) == rowh - r0[j]
        rows_in = (rowc >= r0[j]) & (rowc < r0[j] + bl)
        cols_in = (lanec >= c0[j]) & (lanec < c0[j] + bl)
        east_col = jnp.sum(
            jnp.where(match & (laneh < 32), got, 0.0), axis=1, keepdims=True
        )
        west_col = jnp.sum(
            jnp.where(match & (laneh >= 32) & (laneh < 64), got, 0.0), axis=1, keepdims=True
        )
        got8 = jnp.broadcast_to(got, (8, 128))
        north_row = roll(got8, (c0[j] - 64) & 127, 1)[0:1]
        south_row = roll(got8, (c0[j] - 96) & 127, 1)[0:1]
        north_row = jnp.concatenate([north_row] * (cols // 128), axis=1)
        south_row = jnp.concatenate([south_row] * (cols // 128), axis=1)
        h2 = jnp.where(rows_in & (lanec == c0[j] + bl), east_col, h2)
        h2 = jnp.where(cols_in & (rowc == r0[j] + bl), north_row, h2)
        fixes.append((rows_in & (lanec == c0[j] - 1), west_col,
                      cols_in & (rowc == r0[j] - 1), south_row))
    u1, v1 = t1[1], t1[2]
    u2 = oe * u1 - ce[...] * (east(h2) - h2)
    v2 = on * v1 - cn[...] * (north(h2, h2_p) - h2)
    for at_west, west_col, at_south, south_row in fixes:
        u2 = jnp.where(at_west, west_col, u2)
        v2 = jnp.where(at_south, south_row, v2)
    cout[0], cout[1], cout[2] = h2, u2, v2

    cell = gauge[...]
    grow = cell // cols
    gcol = cell - grow * cols
    own_row = grow - me * rows
    in_block = None
    for j in range(2):
        hit = (
            (own_row >= r0[j]) & (own_row < r0[j] + bl) & (gcol >= c0[j]) & (gcol < c0[j] + bl)
        )
        in_block = hit if in_block is None else in_block | hit
    pick_col = jnp.where(iota((cols, 128), 0) == gcol, 1.0, 0.0)
    found = dot(h2, pick_col)
    value = jnp.sum(
        jnp.where((rowh == own_row) & jnp.logical_not(in_block), found, 0.0),
        axis=0, keepdims=True,
    )
    rel_col = jnp.full((1, 128), -1, jnp.int32)
    rel_row = jnp.full((1, 128), -1, jnp.int32)
    for s in range(slots):
        p = jnp.maximum(my_patch[s], 0)
        first_row = (p >> 1) * rows + anchor[0, p]
        first_col = anchor[1, p]
        hit = (
            (grow >= first_row) & (grow < first_row + bl)
            & (gcol >= first_col) & (gcol < first_col + bl) & (my_patch[s] >= 0)
        )
        rel_col = jnp.where(hit, gcol - first_col, rel_col)
        rel_row = jnp.where(hit, grow - first_row + bl * s, rel_row)
    pick_col = jnp.where(rc_i == rel_col, 1.0, 0.0)
    found = dot(mean, pick_col)
    value = value + jnp.sum(
        jnp.where(iota((bl * slots, 128), 0) == rel_row, found, 0.0), axis=0, keepdims=True
    )
    z_s[0] = value

    def send_member(k, carry):
        pltpu.make_async_remote_copy(
            src_ref=z_s.at[0], dst_ref=z_r.at[k], send_sem=send_sem.at[5],
            recv_sem=recv_sem.at[5], device_id=(lax.rem(mem + k + 1, nm), me),
            device_id_type=MESH,
        ).start()
        return carry

    lax.fori_loop(0, nm - 1, send_member, 0)
    all_of(z_r, nm - 1, recv_sem.at[5])

    def weight(m):
        return (1.0 + 2.0 * m.astype(f32) / (nm - 1)) / (2.0 * nm)

    center = weight(mem) * value
    for k in range(nm - 1):
        center = center + weight(lax.rem(mem - k - 1 + nm, nm)) * z_r[k]
    g_s[0] = value - center

    def send_gauge(k, carry):
        pltpu.make_async_remote_copy(
            src_ref=g_s.at[0], dst_ref=g_r.at[k], send_sem=send_sem.at[6],
            recv_sem=recv_sem.at[6], device_id=(mem, lax.rem(me + k + 1, ns)),
            device_id_type=MESH,
        ).start()
        return carry

    lax.fori_loop(0, ns - 1, send_gauge, 0)

    all_of(a2_r, ns - 1, recv_sem.at[4])
    for j in range(2):
        at = owner_at[j]
        tail = jnp.zeros((8, 128), f32)
        for i in range(3):
            piece = a2_r[at, 8 * i : 8 * i + 8, :]
            pz[j, 32 + 8 * i : 40 + 8 * i, :] = piece
            here = (lane8 >= 32 * i) & (lane8 < 32 * i + 32)
            tail = jnp.where(here, roll(piece, 32 + 32 * i, 1), tail)
        pz[j, 56:64, :] = tail
        moved = pz[j, pl.ds(32 - r0[j], rows), :]
        inside = (
            (rowc >= r0[j]) & (rowc < r0[j] + bl) & (lanec >= c0[j]) & (lanec < c0[j] + bl)
        )
        for field in range(3):
            placed = roll(moved, (c0[j] - 32 * field) & 127, 1)
            placed = jnp.concatenate([placed] * (cols // 128), axis=1)
            cout[field] = jnp.where(inside, placed, cout[field])
    final = pltpu.make_async_copy(cout, coarse_out.at[0], out_sem.at[3])
    final.start()

    all_of(g_r, ns - 1, recv_sem.at[6])
    total = g_s[0]
    for k in range(ns - 1):
        total = total + g_r[k]
    spread_out[...] = total

    all_of(pay_r, ns - 1, send_sem.at[2])
    all_of(m1_r, ns - 1, send_sem.at[3])
    all_of(a2_r, ns - 1, send_sem.at[4])
    all_of(z_r, nm - 1, send_sem.at[5])
    all_of(g_r, ns - 1, send_sem.at[6])
    for store in stores:
        store.wait()
    final.wait()


def shards(
    coarse_state, coarse_seabed, open_faces, fine_state, fine_seabed, slot_patch, patch_anchor,
    gauge_cells,
):
    ns = lax.axis_size("space")
    nm = lax.axis_size("member")
    rows, cols = coarse_seabed.shape
    slots, fl = fine_seabed.shape[0], fine_seabed.shape[-1]
    nb = 8 * slots
    vmem, hbm, smem = (
        pl.BlockSpec(memory_space=space) for space in (pltpu.VMEM, pltpu.HBM, pltpu.SMEM)
    )

    def buf(*shape):
        return pltpu.VMEM(shape, f32)

    return pl.pallas_call(
        functools.partial(kernel, ns, nm, slots),
        out_shape=(
            jax.ShapeDtypeStruct(coarse_state.shape, f32),
            jax.ShapeDtypeStruct(fine_state.shape, f32),
            jax.ShapeDtypeStruct((1, gauge_cells.shape[0]), f32),
        ),
        in_specs=[smem, smem, vmem, hbm, hbm, hbm, hbm, hbm],
        out_specs=(hbm, hbm, vmem),
        scratch_shapes=[
            buf(3, rows, cols), buf(rows, cols), pltpu.VMEM((2, rows, cols), jnp.int32),
            buf(3, rows, cols), buf(rows, cols), buf(11, cols // 128, rows, 128),
            buf(rows, cols), buf(rows, cols),
            buf(slots, fl + 16, fl), buf(slots, fl, fl), buf(slots, fl + 16, fl),
            buf(slots, fl, fl),
            buf(8, cols), buf(8, cols), buf(8, cols), buf(8, cols),
            buf(2, 4, 2, 8, 128), buf(8, 128), buf(ns, 8, 128), buf(nb, 128), buf(nb, 128),
            buf(fl, 128), buf(2 * nb, 128), buf(3, slots * fl // REFINE, 128),
            buf(slots, 128, 128),
            buf(slots, 1, 128), buf(ns, 1, 128), buf(ns, 1, 128),
            buf(slots, 24, 128), buf(ns, 24, 128), buf(ns, 24, 128),
            buf(2, 128, 128), buf(3, rows, cols),
            buf(1, 1, 128), buf(nm, 1, 128), buf(1, 1, 128), buf(ns, 1, 128),
            pltpu.SMEM((ns,), jnp.int32),
            pltpu.SemaphoreType.DMA((7,)), pltpu.SemaphoreType.DMA((4,)),
            pltpu.SemaphoreType.DMA((7,)), pltpu.SemaphoreType.DMA((7,)),
        ],
        compiler_params=pltpu.CompilerParams(
            collective_id=0, has_side_effects=True, vmem_limit_bytes=40 * 1024 * 1024
        ),
    )(
        slot_patch, patch_anchor.T, gauge_cells.reshape(1, -1), coarse_state, coarse_seabed,
        open_faces, fine_state, fine_seabed,
    )


def solution(mesh):
    return jax.shard_map(
        shards,
        mesh=mesh,
        in_specs=(
            P("member", None, "space", None),
            P("space", None),
            P(None, "space", None),
            P("member", None, "space", None, None),
            P("space", None, None),
            P(),
            P(),
            P(),
        ),
        out_specs=(
            P("member", None, "space", None),
            P("member", None, "space", None, None),
            P("member", None),
        ),
        check_vma=False,
    )
```

```python
import functools

import jax
import jax.numpy as jnp
from jax import lax
from jax.experimental import pallas as pl
from jax.experimental.pallas import tpu as pltpu
from jax.sharding import PartitionSpec as P

REFINE = 4
C = 0.5
MESH = pl.DeviceIdType.MESH
f32 = jnp.float32
NT = (((1,), (1,)), ((), ()))
NN = (((1,), (0,)), ((), ()))


def dot(a, b, dims=NN):
    return lax.dot_general(
        a, b, dims, precision=lax.Precision.HIGHEST, preferred_element_type=f32
    )


def dot3(a, b):
    b = b.astype(jnp.bfloat16)
    total = None
    for _ in range(3):
        part = a.astype(jnp.bfloat16)
        a = a - part.astype(f32)
        term = lax.dot_general(part, b, NN, preferred_element_type=f32)
        total = term if total is None else total + term
    return total


def iota(shape, dim):
    return lax.broadcasted_iota(jnp.int32, shape, dim)


def roll(x, shift, axis):
    return pltpu.roll(x, shift, axis)


def kernel(
    ns, nm, slots,
    slot, anchor, gauge, coarse, seabed, faces, fine, fseabed,
    coarse_out, fine_out, spread_out,
    cs, sd, op, t1, t2, ex, ce, cn, fh, fu, fv, fd, eo, ed,
    up_s, dn_s, up_r, dn_r, rs, pay_s, pay_r, xb, gx, ycol, yrow, red, tp,
    m1_p, m1_s, m1_r, a2_p, a2_s, a2_r, pz, z_s, z_r, g_s, g_r, sidx,
    in_sem, send_sem, recv_sem,
):
    me = lax.axis_index("space")
    mem = lax.axis_index("member")
    rows, cols = sd.shape
    fl = fu.shape[-1]
    bl = fl // REFINE
    nb = slots * 8

    barrier = pltpu.get_barrier_semaphore()

    def greet_space(k, carry):
        pl.semaphore_signal(
            barrier, inc=1, device_id=(mem, lax.rem(me + k, ns)), device_id_type=MESH
        )
        return carry

    def greet_member(k, carry):
        pl.semaphore_signal(
            barrier, inc=1, device_id=(lax.rem(mem + k, nm), me), device_id_type=MESH
        )
        return carry

    lax.fori_loop(1, nm, greet_member, 0)
    lax.fori_loop(1, ns, greet_space, 0)

    loads = [
        pltpu.make_async_copy(coarse.at[0], cs, in_sem.at[0]),
        pltpu.make_async_copy(seabed, sd, in_sem.at[1]),
        pltpu.make_async_copy(faces, op, in_sem.at[2]),
        pltpu.make_async_copy(fine.at[0, 0], fh.at[:, pl.ds(8, fl), :], in_sem.at[3]),
        pltpu.make_async_copy(fine.at[0, 1], fu, in_sem.at[4]),
        pltpu.make_async_copy(fine.at[0, 2], fv.at[:, pl.ds(8, fl), :], in_sem.at[5]),
        pltpu.make_async_copy(fseabed, fd, in_sem.at[6]),
    ]
    for load in loads:
        load.start()

    r0 = [jnp.clip(anchor[0, 2 * me + j], 1, rows - bl - 1) for j in range(2)]
    c0 = [jnp.clip(anchor[1, 2 * me + j], 1, cols - bl - 1) for j in range(2)]

    lane = iota((1, 128), 1)
    row8 = iota((8, 128), 0)
    lane8 = iota((8, 128), 1)
    rowc = iota((rows, cols), 0)
    lanec = iota((rows, cols), 1)
    lane1 = iota((1, cols), 1)
    block = None
    for j in range(2):
        inside = (
            (rowc >= r0[j]) & (rowc < r0[j] + bl) & (lanec >= c0[j]) & (lanec < c0[j] + bl)
        )
        block = inside if block is None else block | inside

    def west(x):
        first = iota(x.shape, 1) == 0
        return jnp.where(first, 0.0, roll(x, 1, 1))

    def east(x):
        last = iota(x.shape, 1) == cols - 1
        return jnp.where(last, 0.0, roll(x, cols - 1, 1))

    def south(x, below):
        return jnp.where(rowc == 0, below, roll(x, 1, 0))

    def north(x, above):
        return jnp.where(rowc == rows - 1, above, roll(x, rows - 1, 0))

    for load in loads[:3]:
        load.wait()
    h0, u0, v0 = cs[0], cs[1], cs[2]
    oe = op[0].astype(f32)
    on = op[1].astype(f32)
    cd = C * sd[...]
    ce[...] = cd * oe
    cn[...] = cd * on
    h1 = h0 - C * (u0 - west(u0) + v0 - south(v0, 0.0))
    t1[0] = h1
    up_s[0:1, :] = h1[rows - 1 : rows]
    up_s[1:2, :] = v0[rows - 1 : rows]
    up_s[2:3, :] = on[rows - 1 : rows]
    up_s[3:4, :] = cn[rows - 1 : rows, :]
    up_s[4:8, :] = jnp.zeros((4, cols), f32)
    dn_s[0:1, :] = h1[0:1]
    dn_s[1:2, :] = u0[0:1]
    dn_s[2:3, :] = v0[0:1]
    dn_s[3:4, :] = h1[1:2]
    dn_s[4:5, :] = oe[0:1]
    dn_s[5:6, :] = ce[0:1, :]
    dn_s[6:7, :] = on[0:1]
    dn_s[7:8, :] = cn[0:1, :]

    pl.semaphore_wait(barrier, ns + nm - 2)

    up = pltpu.make_async_remote_copy(
        src_ref=up_s, dst_ref=up_r, send_sem=send_sem.at[0], recv_sem=recv_sem.at[0],
        device_id=(mem, lax.rem(me + 1, ns)), device_id_type=MESH,
    )
    down = pltpu.make_async_remote_copy(
        src_ref=dn_s, dst_ref=dn_r, send_sem=send_sem.at[1], recv_sem=recv_sem.at[1],
        device_id=(mem, lax.rem(me + ns - 1, ns)), device_id_type=MESH,
    )
    up.start()
    down.start()

    xb[...] = jnp.zeros(xb.shape, f32)
    gx[...] = jnp.zeros(gx.shape, f32)
    tp[...] = jnp.zeros(tp.shape, f32)
    pz[...] = jnp.zeros(pz.shape, f32)
    rs[...] = jnp.zeros(rs.shape, f32)

    up.wait()
    down.wait()

    low = me > 0
    high = me < ns - 1
    h1_m = up_r[0:1, :]
    v0_m = jnp.where(low, up_r[1:2, :], 0.0)
    h1 = jnp.where(rowc == 0, h1 + C * v0_m, h1)
    h1_p = jnp.where(high, dn_r[0:1, :] + C * v0[rows - 1 : rows], 0.0)
    u1 = oe * u0 - ce[...] * (east(h1) - h1)
    v1 = on * v0 - cn[...] * (north(h1, h1_p) - h1)
    u1_p = dn_r[4:5, :] * dn_r[1:2, :] - dn_r[5:6, :] * (east(h1_p) - h1_p)
    v1_p = dn_r[6:7, :] * dn_r[2:3, :] - dn_r[7:8, :] * (dn_r[3:4, :] - h1_p)
    v1_m = jnp.where(
        low, up_r[2:3, :] * v0_m - up_r[3:4, :] * (h1[0:1] - h1_m), 0.0
    )
    h2_p = jnp.where(
        high, h1_p - C * (u1_p - west(u1_p) + v1_p - v1[rows - 1 : rows]), 0.0
    )
    h1 = jnp.where(block, 0.0, h1)
    u1 = jnp.where(block, 0.0, u1)
    v1 = jnp.where(block, 0.0, v1)
    h2 = h1 - C * (u1 - west(u1) + v1 - south(v1, v1_m))
    t1[0], t1[1], t1[2] = h1, u1, v1
    t2[...] = h2
    u2 = oe * u1 - ce[...] * (east(h2) - h2)
    v2 = on * v1 - cn[...] * (north(h2, h2_p) - h2)
    for f, held in enumerate((h0, h1, h2, u0, u1, u2, ce, v0, v1, v2, cn)):
        for tile in range(cols // 128):
            ex[f, tile] = held[:, 128 * tile : 128 * tile + 128]

    payload = None
    for j in range(2):
        cw = c0[j] - 1
        ch = c0[j] + bl
        tw = cw >> 7
        te = ch >> 7
        span = pl.ds(r0[j], bl)
        west_stack = jnp.concatenate(
            [ex[3 + t, tw, span, :] for t in range(4)], axis=0
        )
        east_stack = jnp.concatenate(
            [ex[t, te, span, :] for t in range(3)] + [jnp.full((bl, 128), -1.0, f32)],
            axis=0,
        )
        pick_w = jnp.where((row8 == 1) & (lane8 == (cw & 127)), 1.0, 0.0)
        pick_e = jnp.where((row8 == 0) & (lane8 == (ch & 127)), 1.0, 0.0)
        sides = dot(pick_w, west_stack, NT) + dot(pick_e, east_stack, NT)
        first = c0[j] >> 7
        second = jnp.minimum(first + 1, cols // 128 - 1)
        north_row = pl.ds(r0[j] + bl, 1)
        south_row = pl.ds(r0[j] - 1, 1)
        for t in range(4):
            moved = []
            for half, tile in enumerate((first, second)):
                if t < 3:
                    rs[j, t, half, 2:3, :] = ex[t, tile, north_row, :]
                else:
                    rs[j, t, half, 2:3, :] = jnp.full((1, 128), -1.0, f32)
                rs[j, t, half, 3:4, :] = ex[7 + t, tile, south_row, :]
                moved.append(roll(rs[j, t, half], (32 * t - c0[j]) & 127, 1))
            kept = lane8 - 32 * t < 128 - (c0[j] & 127)
            picked = jnp.where(kept, moved[0], moved[1])
            here = (row8 >= 2) & (row8 < 4) & (lane8 >= 32 * t) & (lane8 < 32 * t + 32)
            sides = jnp.where(here, picked, sides)
        sides = jnp.where(row8 < 4, sides, 0.0)
        payload = sides if j == 0 else payload + roll(sides, 4, 0)
    pay_s[...] = payload
    pay_r[ns - 1] = payload

    def spread_payload(k, carry):
        pltpu.make_async_remote_copy(
            src_ref=pay_s, dst_ref=pay_r.at[k], send_sem=send_sem.at[2],
            recv_sem=recv_sem.at[2], device_id=(mem, lax.rem(me + k + 1, ns)),
            device_id_type=MESH,
        ).start()
        return carry

    lax.fori_loop(0, ns - 1, spread_payload, 0)

    my_patch = [slot[me * slots + s] for s in range(slots)]
    held_parent = [p >> 1 for p in my_patch]

    def find_slot(k, carry):
        d = lax.rem(me + k + 1, ns)
        which = jnp.int32(0)
        for s in range(1, slots):
            which = jnp.where(held_parent[s] == d, s, which)
        sidx[k] = which
        return carry

    lax.fori_loop(0, ns, find_slot, 0)

    def find_owner(i, carry):
        p = slot[i]
        return tuple(
            jnp.where(p == 2 * me + j, i, carry[j]) for j in range(2)
        )

    where_held = lax.fori_loop(0, ns * slots, find_owner, (jnp.int32(0), jnp.int32(0)))
    owner_at = [lax.rem(me - w // slots - 1 + 2 * ns, ns) for w in where_held]

    def all_of(ref, count, sem):
        part = ref.at[pl.ds(0, count)]
        pltpu.make_async_copy(part, part, sem).wait()

    rc_i = iota((fl, 128), 0)
    rc_l = iota((fl, 128), 1)
    spread_rows = jnp.where((rc_l & 31) == (rc_i >> 2), 1.0, 0.0)
    spread_lanes = jnp.where((rc_i & 31) == (rc_l >> 2), 1.0, 0.0)
    mean_h = jnp.where((rc_i >> 2) == rc_l, 0.25, 0.0)
    mean_u = jnp.where(rc_i == 4 * (rc_l - 32) + 3, 1.0, 0.0)
    mean_v = jnp.where((rc_i >> 2) == rc_l - 64, 0.25, 0.0)
    lane_nb = iota((nb, 128), 1)

    def expand(old, diff):
        both = jnp.concatenate([old, diff], axis=0)
        ycol[:, 0 : 2 * nb] = dot(spread_rows, both, NT)
        yrow[...] = dot(both, spread_lanes)
        for s in range(slots):
            eo[s] = roll(ycol[...], 127 - 8 * s, 1)
            ed[s] = roll(ycol[...], (255 - 8 * s - nb) % 128, 1)

    lane_f = iota((fl, 128), 1)
    every = range(slots)

    def update(k, final):
        kf = k.astype(f32)
        wf = (2.0 * kf + 1.0) / (2.0 * REFINE)
        wl = (kf + 1.0) / REFINE
        weight_of = jnp.where(lane == fl - 1, wl, wf)
        for s in every:
            n, o = 8 * s + 2, 8 * s + 3
            fv[s, 7:8, :] = yrow[o : o + 1, :] + wf * yrow[nb + o : nb + o + 1, :]
            fh[s, 8 + fl : 9 + fl, :] = yrow[n : n + 1, :] + wl * yrow[nb + n : nb + n + 1, :]
        held = []
        for s in every:
            edge = eo[s] + weight_of * ed[s]
            u = fu[s]
            v = fv[s, 8 : 8 + fl, :]
            v_s = fv[s, 7 : 7 + fl, :]
            u_w = jnp.where(lane_f == 0, edge, roll(u, 1, 1))
            h = fh[s, 8 : 8 + fl, :] - C * (u - u_w + v - v_s)
            held.append((h, u, v, edge))
        for s in every:
            fh[s, 8 : 8 + fl, :] = held[s][0]
        for s in every:
            h, u, v, edge = held[s]
            cdf = C * fd[s]
            h_e = jnp.where(lane_f == fl - 1, edge, roll(h, fl - 1, 1))
            h_n = fh[s, 9 : 9 + fl, :]
            u = u - cdf * (h_e - h)
            v = v - cdf * (h_n - h)
            if final:
                used = my_patch[s] >= 0
                fine_out[0, 0, s] = jnp.where(used, h, 0.0)
                fine_out[0, 1, s] = jnp.where(used, u, 0.0)
                fine_out[0, 2, s] = jnp.where(used, v, 0.0)
            else:
                fu[s] = u
                fv[s, 8 : 8 + fl, :] = v

    def fine_steps(last):
        def step(k, carry):
            update(k, False)
            return carry

        lax.fori_loop(0, REFINE - 1 if last else REFINE, step, 0)
        if last:
            update(jnp.int32(REFINE - 1), True)

    def averages(held):
        for s in range(slots):
            span = slice(bl * s, bl * s + bl)
            parts = [held(0, s, i) for i in range(REFINE)]
            red[0, span, :] = 0.25 * ((parts[0] + parts[1]) + (parts[2] + parts[3]))
            parts = [held(1, s, i) for i in range(REFINE)]
            red[1, span, :] = 0.25 * ((parts[0] + parts[1]) + (parts[2] + parts[3]))
            red[2, span, :] = held(2, s, REFINE - 1)
        return dot3(red[0], mean_h) + dot3(red[1], mean_u) + dot3(red[2], mean_v)

    def inner(f, s, i):
        if f == 1:
            return fu[s, pl.ds(i, bl, stride=REFINE), :]
        return (fh, None, fv)[f][s, pl.ds(8 + i, bl, stride=REFINE), :]

    def outer(f, s, i):
        return fine_out[0, f, s, pl.ds(i, bl, stride=REFINE), :]

    for load in loads[3:]:
        load.wait()
    all_of(pay_r, ns - 1, recv_sem.at[2])

    for s in range(slots):
        p = jnp.maximum(my_patch[s], 0)
        at = lax.rem(me - (p >> 1) - 1 + 2 * ns, ns)
        got = pay_r[at, pl.ds((p & 1) * 4, 4), :]
        xb[8 * s : 8 * s + 4, :] = jnp.where(my_patch[s] >= 0, got, 0.0)

    x = xb[...]
    left = lane_nb < 32
    expand(
        jnp.where(left, x, 0.0), jnp.where(left, roll(x, 96, 1) - x, 0.0)
    )
    fine_steps(False)

    mean = averages(inner)
    pick_i = iota((16, 128), 0)
    pick_l = iota((16, 128), 1)
    pick = jnp.where((pick_i == 0) & (pick_l == 63), C, 0.0)
    pick = pick + jnp.where((pick_i == 1) & (pick_l == 0), 1.0, 0.0)
    pick = pick - jnp.where((pick_i == 1) & ((pick_l == 32) | (pick_l == 64)), C, 0.0)
    pick = pick + jnp.where((pick_i == 9) & (pick_l == 64), C, 0.0)
    for s in range(slots):
        tp[s, 64:96, :] = mean[bl * s : bl * s + bl]
    for s in range(slots):
        side = dot(pick, tp[s], NT)
        side = side[0:8] + roll(side[8:16], 1, 1)
        gx[8 * s : 8 * s + 2, :] = side[0:2]
        top = tp[s, 95:96, :]
        low_row = tp[s, 64:65, :]
        gx[8 * s + 2 : 8 * s + 3, :] = C * top
        gx[8 * s + 3 : 8 * s + 4, :] = roll(low_row, 64, 1) - C * (
            roll(low_row, 32, 1) - jnp.where(lane > 64, roll(low_row, 33, 1), 0.0) + low_row
        )
    new = x - roll(x, 96, 1) * gx[...]
    mid = (lane_nb >= 64) & (lane_nb < 96)
    expand(
        jnp.where((lane_nb >= 32) & (lane_nb < 64), x, 0.0),
        jnp.where(mid, new - roll(x, 32, 1), 0.0),
    )
    packed = jnp.zeros((nb, 128), f32)
    row_nb = iota((nb, 128), 0) & 7
    for q in range(4):
        here = (row_nb == q) & (lane_nb >= 32 * q) & (lane_nb < 32 * q + 32)
        packed = jnp.where(here, roll(new, (32 * q + 64) % 128, 1), packed)
    for s in range(slots):
        m1_p[s] = jnp.sum(packed[8 * s : 8 * s + 8], axis=0, keepdims=True)

    def send_cycle(k, carry):
        m1_s[k] = m1_p[sidx[k]]
        pltpu.make_async_remote_copy(
            src_ref=m1_s.at[k], dst_ref=m1_r.at[k], send_sem=send_sem.at[3],
            recv_sem=recv_sem.at[3], device_id=(mem, lax.rem(me + k + 1, ns)),
            device_id_type=MESH,
        ).start()
        return carry

    lax.fori_loop(0, ns - 1, send_cycle, 0)
    m1_r[ns - 1] = m1_p[sidx[ns - 1]]

    fine_steps(True)
    mean = averages(outer)

    all_of(m1_r, ns - 1, recv_sem.at[3])
    rowh = iota((rows, 128), 0)
    laneh = iota((rows, 128), 1)
    h2 = t2[...]
    fixes = []
    for j in range(2):
        got = m1_r[owner_at[j]]
        match = (laneh & 31) == rowh - r0[j]
        rows_in = (rowc >= r0[j]) & (rowc < r0[j] + bl)
        cols_in = (lanec >= c0[j]) & (lanec < c0[j] + bl)
        east_col = jnp.sum(
            jnp.where(match & (laneh < 32), got, 0.0), axis=1, keepdims=True
        )
        west_col = jnp.sum(
            jnp.where(match & (laneh >= 32) & (laneh < 64), got, 0.0), axis=1, keepdims=True
        )
        got8 = jnp.broadcast_to(got, (8, 128))
        north_row = roll(got8, (c0[j] - 64) & 127, 1)[0:1]
        south_row = roll(got8, (c0[j] - 96) & 127, 1)[0:1]
        north_row = jnp.concatenate([north_row] * (cols // 128), axis=1)
        south_row = jnp.concatenate([south_row] * (cols // 128), axis=1)
        h2 = jnp.where(rows_in & (lanec == c0[j] + bl), east_col, h2)
        h2 = jnp.where(cols_in & (rowc == r0[j] + bl), north_row, h2)
        fixes.append((rows_in & (lanec == c0[j] - 1), west_col,
                      cols_in & (rowc == r0[j] - 1), south_row))
    u1, v1 = t1[1], t1[2]
    u2 = oe * u1 - ce[...] * (east(h2) - h2)
    v2 = on * v1 - cn[...] * (north(h2, h2_p) - h2)
    for at_west, west_col, at_south, south_row in fixes:
        u2 = jnp.where(at_west, west_col, u2)
        v2 = jnp.where(at_south, south_row, v2)
    coarse_out[0, 0], coarse_out[0, 1], coarse_out[0, 2] = h2, u2, v2

    cell = gauge[...]
    grow = cell // cols
    gcol = cell - grow * cols
    own_row = grow - me * rows
    in_block = None
    for j in range(2):
        hit = (
            (own_row >= r0[j]) & (own_row < r0[j] + bl) & (gcol >= c0[j]) & (gcol < c0[j] + bl)
        )
        in_block = hit if in_block is None else in_block | hit
    pick_col = jnp.where(iota((cols, 128), 0) == gcol, 1.0, 0.0)
    found = dot(h2, pick_col)
    value = jnp.sum(
        jnp.where((rowh == own_row) & jnp.logical_not(in_block), found, 0.0),
        axis=0, keepdims=True,
    )
    rel_col = jnp.full((1, 128), -1, jnp.int32)
    rel_row = jnp.full((1, 128), -1, jnp.int32)
    for s in range(slots):
        p = jnp.maximum(my_patch[s], 0)
        first_row = (p >> 1) * rows + anchor[0, p]
        first_col = anchor[1, p]
        hit = (
            (grow >= first_row) & (grow < first_row + bl)
            & (gcol >= first_col) & (gcol < first_col + bl) & (my_patch[s] >= 0)
        )
        rel_col = jnp.where(hit, gcol - first_col, rel_col)
        rel_row = jnp.where(hit, grow - first_row + bl * s, rel_row)
    pick_col = jnp.where(rc_i == rel_col, 1.0, 0.0)
    found = dot(mean, pick_col)
    value = value + jnp.sum(
        jnp.where(iota((bl * slots, 128), 0) == rel_row, found, 0.0), axis=0, keepdims=True
    )
    z_s[0] = value

    def send_member(k, carry):
        pltpu.make_async_remote_copy(
            src_ref=z_s.at[0], dst_ref=z_r.at[k], send_sem=send_sem.at[5],
            recv_sem=recv_sem.at[5], device_id=(lax.rem(mem + k + 1, nm), me),
            device_id_type=MESH,
        ).start()
        return carry

    lax.fori_loop(0, nm - 1, send_member, 0)
    for s in range(slots):
        tail = mean[bl * s + 24 : bl * s + 32]
        for i in range(3):
            piece = mean[bl * s + 8 * i : bl * s + 8 * i + 8]
            a2_p[s, 8 * i : 8 * i + 8, :] = jnp.where(
                lane8 < 96, piece, roll(tail, 96 - 32 * i, 1)
            )

    def send_mean(k, carry):
        a2_s[k] = a2_p[sidx[k]]
        pltpu.make_async_remote_copy(
            src_ref=a2_s.at[k], dst_ref=a2_r.at[k], send_sem=send_sem.at[4],
            recv_sem=recv_sem.at[4], device_id=(mem, lax.rem(me + k + 1, ns)),
            device_id_type=MESH,
        ).start()
        return carry

    lax.fori_loop(0, ns - 1, send_mean, 0)
    a2_r[ns - 1] = a2_p[sidx[ns - 1]]

    all_of(z_r, nm - 1, recv_sem.at[5])

    def weight(m):
        return (1.0 + 2.0 * m.astype(f32) / (nm - 1)) / (2.0 * nm)

    center = weight(mem) * value
    for k in range(nm - 1):
        center = center + weight(lax.rem(mem - k - 1 + nm, nm)) * z_r[k]
    g_s[0] = value - center

    def send_gauge(k, carry):
        pltpu.make_async_remote_copy(
            src_ref=g_s.at[0], dst_ref=g_r.at[k], send_sem=send_sem.at[6],
            recv_sem=recv_sem.at[6], device_id=(mem, lax.rem(me + k + 1, ns)),
            device_id_type=MESH,
        ).start()
        return carry

    lax.fori_loop(0, ns - 1, send_gauge, 0)

    all_of(a2_r, ns - 1, recv_sem.at[4])
    for j in range(2):
        at = owner_at[j]
        tail = jnp.zeros((8, 128), f32)
        for i in range(3):
            piece = a2_r[at, 8 * i : 8 * i + 8, :]
            pz[j, 32 + 8 * i : 40 + 8 * i, :] = piece
            here = (lane8 >= 32 * i) & (lane8 < 32 * i + 32)
            tail = jnp.where(here, roll(piece, 32 + 32 * i, 1), tail)
        pz[j, 56:64, :] = tail
        moved = pz[j, pl.ds(32 - r0[j], rows), :]
        inside = (
            (rowc >= r0[j]) & (rowc < r0[j] + bl) & (lanec >= c0[j]) & (lanec < c0[j] + bl)
        )
        for field in range(3):
            placed = roll(moved, (c0[j] - 32 * field) & 127, 1)
            placed = jnp.concatenate([placed] * (cols // 128), axis=1)
            coarse_out[0, field] = jnp.where(inside, placed, coarse_out[0, field])

    all_of(g_r, ns - 1, recv_sem.at[6])
    total = g_s[0]
    for k in range(ns - 1):
        total = total + g_r[k]
    spread_out[...] = total

    all_of(pay_r, ns - 1, send_sem.at[2])
    all_of(m1_r, ns - 1, send_sem.at[3])
    all_of(a2_r, ns - 1, send_sem.at[4])
    all_of(z_r, nm - 1, send_sem.at[5])
    all_of(g_r, ns - 1, send_sem.at[6])


def store_results(coarse, fine, spread, coarse_out, fine_out, spread_out, sem):
    pairs = ((coarse, coarse_out), (fine, fine_out), (spread, spread_out))
    copies = [pltpu.make_async_copy(a, b, sem.at[i]) for i, (a, b) in enumerate(pairs)]
    for copy in copies:
        copy.start()
    for copy in copies:
        copy.wait()


def shards(
    coarse_state, coarse_seabed, open_faces, fine_state, fine_seabed, slot_patch, patch_anchor,
    gauge_cells,
):
    ns = lax.axis_size("space")
    nm = lax.axis_size("member")
    rows, cols = coarse_seabed.shape
    slots, fl = fine_seabed.shape[0], fine_seabed.shape[-1]
    nb = 8 * slots
    vmem, hbm, smem = (
        pl.BlockSpec(memory_space=space) for space in (pltpu.VMEM, pltpu.HBM, pltpu.SMEM)
    )

    def buf(*shape):
        return pltpu.VMEM(shape, f32)

    shapes = (coarse_state.shape, fine_state.shape, (1, gauge_cells.shape[0]))
    results = pl.pallas_call(
        functools.partial(kernel, ns, nm, slots),
        out_shape=tuple(pltpu.VMEM(shape, f32) for shape in shapes),
        in_specs=[smem, smem, vmem, hbm, hbm, hbm, hbm, hbm],
        out_specs=(vmem, vmem, vmem),
        scratch_shapes=[
            buf(3, rows, cols), buf(rows, cols), pltpu.VMEM((2, rows, cols), jnp.int32),
            buf(3, rows, cols), buf(rows, cols), buf(11, cols // 128, rows, 128),
            buf(rows, cols), buf(rows, cols),
            buf(slots, fl + 16, fl), buf(slots, fl, fl), buf(slots, fl + 16, fl),
            buf(slots, fl, fl), buf(slots, fl, 128), buf(slots, fl, 128),
            buf(8, cols), buf(8, cols), buf(8, cols), buf(8, cols),
            buf(2, 4, 2, 8, 128), buf(8, 128), buf(ns, 8, 128), buf(nb, 128), buf(nb, 128),
            buf(fl, 128), buf(2 * nb, 128), buf(3, slots * fl // REFINE, 128),
            buf(slots, 128, 128),
            buf(slots, 1, 128), buf(ns, 1, 128), buf(ns, 1, 128),
            buf(slots, 24, 128), buf(ns, 24, 128), buf(ns, 24, 128),
            buf(2, 128, 128),
            buf(1, 1, 128), buf(nm, 1, 128), buf(1, 1, 128), buf(ns, 1, 128),
            pltpu.SMEM((ns,), jnp.int32),
            pltpu.SemaphoreType.DMA((7,)), pltpu.SemaphoreType.DMA((7,)),
            pltpu.SemaphoreType.DMA((7,)),
        ],
        compiler_params=pltpu.CompilerParams(
            collective_id=0, has_side_effects=True, vmem_limit_bytes=56 * 1024 * 1024
        ),
    )(
        slot_patch, patch_anchor.T, gauge_cells.reshape(1, -1),
        *(pltpu.with_memory_space_constraint(x, pltpu.HBM)
          for x in (coarse_state, coarse_seabed, open_faces, fine_state, fine_seabed)),
    )
    return pl.pallas_call(
        store_results,
        out_shape=tuple(jax.ShapeDtypeStruct(shape, f32) for shape in shapes),
        in_specs=[vmem] * 3,
        out_specs=(hbm,) * 3,
        scratch_shapes=[pltpu.SemaphoreType.DMA((3,))],
    )(*(pltpu.with_memory_space_constraint(x, pltpu.VMEM) for x in results))


def solution(mesh):
    return jax.shard_map(
        shards,
        mesh=mesh,
        in_specs=(
            P("member", None, "space", None),
            P("space", None),
            P(None, "space", None),
            P("member", None, "space", None, None),
            P("space", None, None),
            P(),
            P(),
            P(),
        ),
        out_specs=(
            P("member", None, "space", None),
            P("member", None, "space", None, None),
            P("member", None),
        ),
        check_vma=False,
    )
```

```python
import functools

import jax
import jax.numpy as jnp
from jax import lax
from jax.experimental import pallas as pl
from jax.experimental.pallas import tpu as pltpu
from jax.sharding import PartitionSpec as P

REFINE = 4
C = 0.5
MESH = pl.DeviceIdType.MESH
f32 = jnp.float32
NT = (((1,), (1,)), ((), ()))
NN = (((1,), (0,)), ((), ()))


def dot(a, b, dims=NN):
    return lax.dot_general(
        a, b, dims, precision=lax.Precision.HIGHEST, preferred_element_type=f32
    )


def dot3(a, b):
    b = b.astype(jnp.bfloat16)
    total = None
    for _ in range(3):
        part = a.astype(jnp.bfloat16)
        a = a - part.astype(f32)
        term = lax.dot_general(part, b, NN, preferred_element_type=f32)
        total = term if total is None else total + term
    return total


def iota(shape, dim):
    return lax.broadcasted_iota(jnp.int32, shape, dim)


def roll(x, shift, axis):
    return pltpu.roll(x, shift, axis)


def kernel(
    ns, nm, slots,
    slot, anchor, gauge, coarse, seabed, faces, fine, fseabed,
    coarse_out, fine_out, spread_out,
    cs, sd, op, t1, t2, ex, ce, cn, fh, fu, fv, fd, eo, ed,
    up_s, dn_s, up_r, dn_r, rs, pay_s, pay_r, xb, gx, ycol, yrow, red, tp,
    m1_p, m1_s, m1_r, a2_p, a2_s, a2_r, pz, z_s, z_r, g_s, g_r, sidx,
    in_sem, send_sem, recv_sem,
):
    me = lax.axis_index("space")
    mem = lax.axis_index("member")
    rows, cols = sd.shape
    fl = fu.shape[-1]
    bl = fl // REFINE
    nb = slots * 8

    barrier = pltpu.get_barrier_semaphore()

    def greet_space(k, carry):
        pl.semaphore_signal(
            barrier, inc=1, device_id=(mem, lax.rem(me + k, ns)), device_id_type=MESH
        )
        return carry

    def greet_member(k, carry):
        pl.semaphore_signal(
            barrier, inc=1, device_id=(lax.rem(mem + k, nm), me), device_id_type=MESH
        )
        return carry

    lax.fori_loop(1, nm, greet_member, 0)
    lax.fori_loop(1, ns, greet_space, 0)

    loads = [
        pltpu.make_async_copy(coarse.at[0], cs, in_sem.at[0]),
        pltpu.make_async_copy(seabed, sd, in_sem.at[1]),
        pltpu.make_async_copy(faces, op, in_sem.at[2]),
        pltpu.make_async_copy(fine.at[0, 0], fh.at[:, pl.ds(8, fl), :], in_sem.at[3]),
        pltpu.make_async_copy(fine.at[0, 1], fu, in_sem.at[4]),
        pltpu.make_async_copy(fine.at[0, 2], fv.at[:, pl.ds(8, fl), :], in_sem.at[5]),
        pltpu.make_async_copy(fseabed, fd, in_sem.at[6]),
    ]
    for load in loads:
        load.start()

    r0 = [jnp.clip(anchor[0, 2 * me + j], 1, rows - bl - 1) for j in range(2)]
    c0 = [jnp.clip(anchor[1, 2 * me + j], 1, cols - bl - 1) for j in range(2)]

    lane = iota((1, 128), 1)
    row8 = iota((8, 128), 0)
    lane8 = iota((8, 128), 1)
    rowc = iota((rows, cols), 0)
    lanec = iota((rows, cols), 1)
    lane1 = iota((1, cols), 1)
    block = None
    for j in range(2):
        inside = (
            (rowc >= r0[j]) & (rowc < r0[j] + bl) & (lanec >= c0[j]) & (lanec < c0[j] + bl)
        )
        block = inside if block is None else block | inside

    def west(x):
        first = iota(x.shape, 1) == 0
        return jnp.where(first, 0.0, roll(x, 1, 1))

    def east(x):
        last = iota(x.shape, 1) == cols - 1
        return jnp.where(last, 0.0, roll(x, cols - 1, 1))

    def south(x, below):
        return jnp.where(rowc == 0, below, roll(x, 1, 0))

    def north(x, above):
        return jnp.where(rowc == rows - 1, above, roll(x, rows - 1, 0))

    for load in loads[:3]:
        load.wait()
    h0, u0, v0 = cs[0], cs[1], cs[2]
    oe = op[0].astype(f32)
    on = op[1].astype(f32)
    cd = C * sd[...]
    ce[...] = cd * oe
    cn[...] = cd * on
    h1 = h0 - C * (u0 - west(u0) + v0 - south(v0, 0.0))
    t1[0] = h1
    up_s[0:1, :] = h1[rows - 1 : rows]
    up_s[1:2, :] = v0[rows - 1 : rows]
    up_s[2:3, :] = on[rows - 1 : rows]
    up_s[3:4, :] = cn[rows - 1 : rows, :]
    up_s[4:8, :] = jnp.zeros((4, cols), f32)
    dn_s[0:1, :] = h1[0:1]
    dn_s[1:2, :] = u0[0:1]
    dn_s[2:3, :] = v0[0:1]
    dn_s[3:4, :] = h1[1:2]
    dn_s[4:5, :] = oe[0:1]
    dn_s[5:6, :] = ce[0:1, :]
    dn_s[6:7, :] = on[0:1]
    dn_s[7:8, :] = cn[0:1, :]

    pl.semaphore_wait(barrier, ns + nm - 2)

    up = pltpu.make_async_remote_copy(
        src_ref=up_s, dst_ref=up_r, send_sem=send_sem.at[0], recv_sem=recv_sem.at[0],
        device_id=(mem, lax.rem(me + 1, ns)), device_id_type=MESH,
    )
    down = pltpu.make_async_remote_copy(
        src_ref=dn_s, dst_ref=dn_r, send_sem=send_sem.at[1], recv_sem=recv_sem.at[1],
        device_id=(mem, lax.rem(me + ns - 1, ns)), device_id_type=MESH,
    )
    up.start()
    down.start()

    xb[...] = jnp.zeros(xb.shape, f32)
    gx[...] = jnp.zeros(gx.shape, f32)
    tp[...] = jnp.zeros(tp.shape, f32)
    pz[...] = jnp.zeros(pz.shape, f32)
    rs[...] = jnp.zeros(rs.shape, f32)

    up.wait()
    down.wait()

    low = me > 0
    high = me < ns - 1
    h1_m = up_r[0:1, :]
    v0_m = jnp.where(low, up_r[1:2, :], 0.0)
    h1 = jnp.where(rowc == 0, h1 + C * v0_m, h1)
    h1_p = jnp.where(high, dn_r[0:1, :] + C * v0[rows - 1 : rows], 0.0)
    u1 = oe * u0 - ce[...] * (east(h1) - h1)
    v1 = on * v0 - cn[...] * (north(h1, h1_p) - h1)
    u1_p = dn_r[4:5, :] * dn_r[1:2, :] - dn_r[5:6, :] * (east(h1_p) - h1_p)
    v1_p = dn_r[6:7, :] * dn_r[2:3, :] - dn_r[7:8, :] * (dn_r[3:4, :] - h1_p)
    v1_m = jnp.where(
        low, up_r[2:3, :] * v0_m - up_r[3:4, :] * (h1[0:1] - h1_m), 0.0
    )
    h2_p = jnp.where(
        high, h1_p - C * (u1_p - west(u1_p) + v1_p - v1[rows - 1 : rows]), 0.0
    )
    h1 = jnp.where(block, 0.0, h1)
    u1 = jnp.where(block, 0.0, u1)
    v1 = jnp.where(block, 0.0, v1)
    h2 = h1 - C * (u1 - west(u1) + v1 - south(v1, v1_m))
    t1[0], t1[1], t1[2] = h1, u1, v1
    t2[...] = h2
    u2 = oe * u1 - ce[...] * (east(h2) - h2)
    v2 = on * v1 - cn[...] * (north(h2, h2_p) - h2)
    for f, held in enumerate((h0, h1, h2, u0, u1, u2, ce, v0, v1, v2, cn)):
        for tile in range(cols // 128):
            ex[f, tile] = held[:, 128 * tile : 128 * tile + 128]

    payload = None
    for j in range(2):
        cw = c0[j] - 1
        ch = c0[j] + bl
        tw = cw >> 7
        te = ch >> 7
        span = pl.ds(r0[j], bl)
        west_stack = jnp.concatenate(
            [ex[3 + t, tw, span, :] for t in range(4)], axis=0
        )
        east_stack = jnp.concatenate(
            [ex[t, te, span, :] for t in range(3)] + [jnp.full((bl, 128), -1.0, f32)],
            axis=0,
        )
        pick_w = jnp.where((row8 == 1) & (lane8 == (cw & 127)), 1.0, 0.0)
        pick_e = jnp.where((row8 == 0) & (lane8 == (ch & 127)), 1.0, 0.0)
        sides = dot(pick_w, west_stack, NT) + dot(pick_e, east_stack, NT)
        first = c0[j] >> 7
        second = jnp.minimum(first + 1, cols // 128 - 1)
        north_row = pl.ds(r0[j] + bl, 1)
        south_row = pl.ds(r0[j] - 1, 1)
        for t in range(4):
            moved = []
            for half, tile in enumerate((first, second)):
                if t < 3:
                    rs[j, t, half, 2:3, :] = ex[t, tile, north_row, :]
                else:
                    rs[j, t, half, 2:3, :] = jnp.full((1, 128), -1.0, f32)
                rs[j, t, half, 3:4, :] = ex[7 + t, tile, south_row, :]
                moved.append(roll(rs[j, t, half], (32 * t - c0[j]) & 127, 1))
            kept = lane8 - 32 * t < 128 - (c0[j] & 127)
            picked = jnp.where(kept, moved[0], moved[1])
            here = (row8 >= 2) & (row8 < 4) & (lane8 >= 32 * t) & (lane8 < 32 * t + 32)
            sides = jnp.where(here, picked, sides)
        sides = jnp.where(row8 < 4, sides, 0.0)
        payload = sides if j == 0 else payload + roll(sides, 4, 0)
    pay_s[...] = payload
    pay_r[ns - 1] = payload

    def spread_payload(k, carry):
        pltpu.make_async_remote_copy(
            src_ref=pay_s, dst_ref=pay_r.at[k], send_sem=send_sem.at[2],
            recv_sem=recv_sem.at[2], device_id=(mem, lax.rem(me + k + 1, ns)),
            device_id_type=MESH,
        ).start()
        return carry

    lax.fori_loop(0, ns - 1, spread_payload, 0)

    my_patch = [slot[me * slots + s] for s in range(slots)]
    held_parent = [p >> 1 for p in my_patch]

    def find_slot(k, carry):
        d = lax.rem(me + k + 1, ns)
        which = jnp.int32(0)
        for s in range(1, slots):
            which = jnp.where(held_parent[s] == d, s, which)
        sidx[k] = which
        return carry

    lax.fori_loop(0, ns, find_slot, 0)

    def find_owner(i, carry):
        p = slot[i]
        return tuple(
            jnp.where(p == 2 * me + j, i, carry[j]) for j in range(2)
        )

    where_held = lax.fori_loop(0, ns * slots, find_owner, (jnp.int32(0), jnp.int32(0)))
    owner_at = [lax.rem(me - w // slots - 1 + 2 * ns, ns) for w in where_held]

    def all_of(ref, count, sem):
        part = ref.at[pl.ds(0, count)]
        pltpu.make_async_copy(part, part, sem).wait()

    cell = gauge[...]
    grow = cell // cols
    gcol = cell - grow * cols
    own_row = grow - me * rows
    covered = None
    for j in range(2):
        down = own_row - r0[j]
        right = gcol - c0[j]
        hit = (
            (down >= 0) & (right >= 0) & (down <= bl) & (right <= bl)
            & ((down < bl) | (right < bl))
        )
        covered = hit if covered is None else covered | hit
    pick_col = jnp.where(iota((cols, 128), 0) == gcol, 1.0, 0.0)
    found = dot3(h2, pick_col)
    outside = jnp.sum(
        jnp.where((iota((rows, 128), 0) == own_row) & jnp.logical_not(covered), found, 0.0),
        axis=0, keepdims=True,
    )

    rc_i = iota((fl, 128), 0)
    rc_l = iota((fl, 128), 1)
    spread_rows = jnp.where((rc_l & 31) == (rc_i >> 2), 1.0, 0.0)
    spread_lanes = jnp.where((rc_i & 31) == (rc_l >> 2), 1.0, 0.0)
    mean_h = jnp.where((rc_i >> 2) == rc_l, 0.25, 0.0)
    mean_u = jnp.where(rc_i == 4 * (rc_l - 32) + 3, 1.0, 0.0)
    mean_v = jnp.where((rc_i >> 2) == rc_l - 64, 0.25, 0.0)
    lane_nb = iota((nb, 128), 1)

    def expand(old, diff):
        both = jnp.concatenate([old, diff], axis=0)
        ycol[:, 0 : 2 * nb] = dot(spread_rows, both, NT)
        yrow[...] = dot(both, spread_lanes)
        for s in range(slots):
            eo[s] = roll(ycol[...], 127 - 8 * s, 1)
            ed[s] = roll(ycol[...], (255 - 8 * s - nb) % 128, 1)

    lane_f = iota((fl, 128), 1)
    every = range(slots)

    def update(k, final):
        kf = k.astype(f32)
        wf = (2.0 * kf + 1.0) / (2.0 * REFINE)
        wl = (kf + 1.0) / REFINE
        weight_of = jnp.where(lane == fl - 1, wl, wf)
        for s in every:
            n, o = 8 * s + 2, 8 * s + 3
            fv[s, 7:8, :] = yrow[o : o + 1, :] + wf * yrow[nb + o : nb + o + 1, :]
            fh[s, 8 + fl : 9 + fl, :] = yrow[n : n + 1, :] + wl * yrow[nb + n : nb + n + 1, :]
        held = []
        for s in every:
            edge = eo[s] + weight_of * ed[s]
            u = fu[s]
            v = fv[s, 8 : 8 + fl, :]
            v_s = fv[s, 7 : 7 + fl, :]
            u_w = jnp.where(lane_f == 0, edge, roll(u, 1, 1))
            h = fh[s, 8 : 8 + fl, :] - C * (u - u_w + v - v_s)
            held.append((h, u, v, edge))
        for s in every:
            fh[s, 8 : 8 + fl, :] = held[s][0]
        for s in every:
            h, u, v, edge = held[s]
            cdf = C * fd[s]
            h_e = jnp.where(lane_f == fl - 1, edge, roll(h, fl - 1, 1))
            h_n = fh[s, 9 : 9 + fl, :]
            u = u - cdf * (h_e - h)
            v = v - cdf * (h_n - h)
            if final:
                used = my_patch[s] >= 0
                fine_out[0, 0, s] = jnp.where(used, h, 0.0)
                fine_out[0, 1, s] = jnp.where(used, u, 0.0)
                fine_out[0, 2, s] = jnp.where(used, v, 0.0)
            else:
                fu[s] = u
                fv[s, 8 : 8 + fl, :] = v

    def fine_steps(last):
        def step(k, carry):
            update(k, False)
            return carry

        lax.fori_loop(0, REFINE - 1 if last else REFINE, step, 0)
        if last:
            update(jnp.int32(REFINE - 1), True)

    def averages(held):
        for s in range(slots):
            span = slice(bl * s, bl * s + bl)
            parts = [held(0, s, i) for i in range(REFINE)]
            red[0, span, :] = 0.25 * ((parts[0] + parts[1]) + (parts[2] + parts[3]))
            parts = [held(1, s, i) for i in range(REFINE)]
            red[1, span, :] = 0.25 * ((parts[0] + parts[1]) + (parts[2] + parts[3]))
            red[2, span, :] = held(2, s, REFINE - 1)
        return dot3(red[0], mean_h) + dot3(red[1], mean_u) + dot3(red[2], mean_v)

    def inner(f, s, i):
        if f == 1:
            return fu[s, pl.ds(i, bl, stride=REFINE), :]
        return (fh, None, fv)[f][s, pl.ds(8 + i, bl, stride=REFINE), :]

    def outer(f, s, i):
        return fine_out[0, f, s, pl.ds(i, bl, stride=REFINE), :]

    for load in loads[3:]:
        load.wait()
    all_of(pay_r, ns - 1, recv_sem.at[2])

    for s in range(slots):
        p = jnp.maximum(my_patch[s], 0)
        at = lax.rem(me - (p >> 1) - 1 + 2 * ns, ns)
        got = pay_r[at, pl.ds((p & 1) * 4, 4), :]
        xb[8 * s : 8 * s + 4, :] = jnp.where(my_patch[s] >= 0, got, 0.0)

    x = xb[...]
    left = lane_nb < 32
    expand(
        jnp.where(left, x, 0.0), jnp.where(left, roll(x, 96, 1) - x, 0.0)
    )
    fine_steps(False)

    mean = averages(inner)
    pick_i = iota((16, 128), 0)
    pick_l = iota((16, 128), 1)
    pick = jnp.where((pick_i == 0) & (pick_l == 63), C, 0.0)
    pick = pick + jnp.where((pick_i == 1) & (pick_l == 0), 1.0, 0.0)
    pick = pick - jnp.where((pick_i == 1) & ((pick_l == 32) | (pick_l == 64)), C, 0.0)
    pick = pick + jnp.where((pick_i == 9) & (pick_l == 64), C, 0.0)
    for s in range(slots):
        tp[s, 64:96, :] = mean[bl * s : bl * s + bl]
    for s in range(slots):
        side = dot(pick, tp[s], NT)
        side = side[0:8] + roll(side[8:16], 1, 1)
        gx[8 * s : 8 * s + 2, :] = side[0:2]
        top = tp[s, 95:96, :]
        low_row = tp[s, 64:65, :]
        gx[8 * s + 2 : 8 * s + 3, :] = C * top
        gx[8 * s + 3 : 8 * s + 4, :] = roll(low_row, 64, 1) - C * (
            roll(low_row, 32, 1) - jnp.where(lane > 64, roll(low_row, 33, 1), 0.0) + low_row
        )
    new = x - roll(x, 96, 1) * gx[...]
    mid = (lane_nb >= 64) & (lane_nb < 96)
    expand(
        jnp.where((lane_nb >= 32) & (lane_nb < 64), x, 0.0),
        jnp.where(mid, new - roll(x, 32, 1), 0.0),
    )
    fine_steps(True)
    mean = averages(outer)

    rel_col = jnp.full((1, 128), -1, jnp.int32)
    rel_row = jnp.full((1, 128), -1, jnp.int32)
    for s in range(slots):
        p = jnp.maximum(my_patch[s], 0)
        down = jnp.where(my_patch[s] >= 0, grow - ((p >> 1) * rows + anchor[0, p]), -1)
        right = gcol - anchor[1, p]
        in_rows = (down >= 0) & (down < bl)
        in_cols = (right >= 0) & (right < bl)
        hit = in_rows & in_cols
        rel_col = jnp.where(hit, right, rel_col)
        rel_row = jnp.where(hit, down + bl * s, rel_row)
        hit = in_rows & (right == bl)
        rel_col = jnp.where(hit, 64 + down, rel_col)
        rel_row = jnp.where(hit, bl * slots + 8 * s, rel_row)
        hit = (down == bl) & in_cols
        rel_col = jnp.where(hit, 64 + right, rel_col)
        rel_row = jnp.where(hit, bl * slots + 8 * s + 2, rel_row)
    pick_col = jnp.where(rc_i == rel_col, 1.0, 0.0)
    found = dot3(jnp.concatenate([mean, new], axis=0), pick_col)
    at_row = iota((bl * slots + nb, 128), 0) == rel_row
    value = outside + jnp.sum(jnp.where(at_row, found, 0.0), axis=0, keepdims=True)
    z_s[0] = value

    def send_member(k, carry):
        pltpu.make_async_remote_copy(
            src_ref=z_s.at[0], dst_ref=z_r.at[k], send_sem=send_sem.at[5],
            recv_sem=recv_sem.at[5], device_id=(lax.rem(mem + k + 1, nm), me),
            device_id_type=MESH,
        ).start()
        return carry

    lax.fori_loop(0, nm - 1, send_member, 0)
    for s in range(slots):
        tail = mean[bl * s + 24 : bl * s + 32]
        for i in range(3):
            piece = mean[bl * s + 8 * i : bl * s + 8 * i + 8]
            a2_p[s, 8 * i : 8 * i + 8, :] = jnp.where(
                lane8 < 96, piece, roll(tail, 96 - 32 * i, 1)
            )

    def send_mean(k, carry):
        a2_s[k] = a2_p[sidx[k]]
        pltpu.make_async_remote_copy(
            src_ref=a2_s.at[k], dst_ref=a2_r.at[k], send_sem=send_sem.at[4],
            recv_sem=recv_sem.at[4], device_id=(mem, lax.rem(me + k + 1, ns)),
            device_id_type=MESH,
        ).start()
        return carry

    lax.fori_loop(0, ns - 1, send_mean, 0)
    a2_r[ns - 1] = a2_p[sidx[ns - 1]]

    packed = jnp.zeros((nb, 128), f32)
    row_nb = iota((nb, 128), 0) & 7
    for q in range(4):
        here = (row_nb == q) & (lane_nb >= 32 * q) & (lane_nb < 32 * q + 32)
        packed = jnp.where(here, roll(new, (32 * q + 64) % 128, 1), packed)
    for s in range(slots):
        m1_p[s] = jnp.sum(packed[8 * s : 8 * s + 8], axis=0, keepdims=True)

    def send_cycle(k, carry):
        m1_s[k] = m1_p[sidx[k]]
        pltpu.make_async_remote_copy(
            src_ref=m1_s.at[k], dst_ref=m1_r.at[k], send_sem=send_sem.at[3],
            recv_sem=recv_sem.at[3], device_id=(mem, lax.rem(me + k + 1, ns)),
            device_id_type=MESH,
        ).start()
        return carry

    lax.fori_loop(0, ns - 1, send_cycle, 0)
    m1_r[ns - 1] = m1_p[sidx[ns - 1]]

    all_of(z_r, nm - 1, recv_sem.at[5])

    def weight(m):
        return (1.0 + 2.0 * m.astype(f32) / (nm - 1)) / (2.0 * nm)

    center = weight(mem) * value
    for k in range(nm - 1):
        center = center + weight(lax.rem(mem - k - 1 + nm, nm)) * z_r[k]
    g_s[0] = value - center

    def send_gauge(k, carry):
        pltpu.make_async_remote_copy(
            src_ref=g_s.at[0], dst_ref=g_r.at[k], send_sem=send_sem.at[6],
            recv_sem=recv_sem.at[6], device_id=(mem, lax.rem(me + k + 1, ns)),
            device_id_type=MESH,
        ).start()
        return carry

    lax.fori_loop(0, ns - 1, send_gauge, 0)

    all_of(m1_r, ns - 1, recv_sem.at[3])
    rowh = iota((rows, 128), 0)
    laneh = iota((rows, 128), 1)
    h2 = t2[...]
    fixes = []
    for j in range(2):
        got = m1_r[owner_at[j]]
        match = (laneh & 31) == rowh - r0[j]
        rows_in = (rowc >= r0[j]) & (rowc < r0[j] + bl)
        cols_in = (lanec >= c0[j]) & (lanec < c0[j] + bl)
        east_col = jnp.sum(
            jnp.where(match & (laneh < 32), got, 0.0), axis=1, keepdims=True
        )
        west_col = jnp.sum(
            jnp.where(match & (laneh >= 32) & (laneh < 64), got, 0.0), axis=1, keepdims=True
        )
        got8 = jnp.broadcast_to(got, (8, 128))
        north_row = roll(got8, (c0[j] - 64) & 127, 1)[0:1]
        south_row = roll(got8, (c0[j] - 96) & 127, 1)[0:1]
        north_row = jnp.concatenate([north_row] * (cols // 128), axis=1)
        south_row = jnp.concatenate([south_row] * (cols // 128), axis=1)
        h2 = jnp.where(rows_in & (lanec == c0[j] + bl), east_col, h2)
        h2 = jnp.where(cols_in & (rowc == r0[j] + bl), north_row, h2)
        fixes.append((rows_in & (lanec == c0[j] - 1), west_col,
                      cols_in & (rowc == r0[j] - 1), south_row))
    u1, v1 = t1[1], t1[2]
    u2 = oe * u1 - ce[...] * (east(h2) - h2)
    v2 = on * v1 - cn[...] * (north(h2, h2_p) - h2)
    for at_west, west_col, at_south, south_row in fixes:
        u2 = jnp.where(at_west, west_col, u2)
        v2 = jnp.where(at_south, south_row, v2)
    coarse_out[0, 0], coarse_out[0, 1], coarse_out[0, 2] = h2, u2, v2

    all_of(a2_r, ns - 1, recv_sem.at[4])
    for j in range(2):
        at = owner_at[j]
        tail = jnp.zeros((8, 128), f32)
        for i in range(3):
            piece = a2_r[at, 8 * i : 8 * i + 8, :]
            pz[j, 32 + 8 * i : 40 + 8 * i, :] = piece
            here = (lane8 >= 32 * i) & (lane8 < 32 * i + 32)
            tail = jnp.where(here, roll(piece, 32 + 32 * i, 1), tail)
        pz[j, 56:64, :] = tail
        moved = pz[j, pl.ds(32 - r0[j], rows), :]
        inside = (
            (rowc >= r0[j]) & (rowc < r0[j] + bl) & (lanec >= c0[j]) & (lanec < c0[j] + bl)
        )
        for field in range(3):
            placed = roll(moved, (c0[j] - 32 * field) & 127, 1)
            placed = jnp.concatenate([placed] * (cols // 128), axis=1)
            coarse_out[0, field] = jnp.where(inside, placed, coarse_out[0, field])

    all_of(g_r, ns - 1, recv_sem.at[6])
    total = g_s[0]
    for k in range(ns - 1):
        total = total + g_r[k]
    spread_out[...] = total

    all_of(pay_r, ns - 1, send_sem.at[2])
    all_of(m1_r, ns - 1, send_sem.at[3])
    all_of(a2_r, ns - 1, send_sem.at[4])
    all_of(z_r, nm - 1, send_sem.at[5])
    all_of(g_r, ns - 1, send_sem.at[6])


def store_results(coarse, fine, spread, coarse_out, fine_out, spread_out, sem):
    pairs = ((coarse, coarse_out), (fine, fine_out), (spread, spread_out))
    copies = [pltpu.make_async_copy(a, b, sem.at[i]) for i, (a, b) in enumerate(pairs)]
    for copy in copies:
        copy.start()
    for copy in copies:
        copy.wait()


def shards(
    coarse_state, coarse_seabed, open_faces, fine_state, fine_seabed, slot_patch, patch_anchor,
    gauge_cells,
):
    ns = lax.axis_size("space")
    nm = lax.axis_size("member")
    rows, cols = coarse_seabed.shape
    slots, fl = fine_seabed.shape[0], fine_seabed.shape[-1]
    nb = 8 * slots
    vmem, hbm, smem = (
        pl.BlockSpec(memory_space=space) for space in (pltpu.VMEM, pltpu.HBM, pltpu.SMEM)
    )

    def buf(*shape):
        return pltpu.VMEM(shape, f32)

    shapes = (coarse_state.shape, fine_state.shape, (1, gauge_cells.shape[0]))
    results = pl.pallas_call(
        functools.partial(kernel, ns, nm, slots),
        out_shape=tuple(pltpu.VMEM(shape, f32) for shape in shapes),
        in_specs=[smem, smem, vmem, hbm, hbm, hbm, hbm, hbm],
        out_specs=(vmem, vmem, vmem),
        scratch_shapes=[
            buf(3, rows, cols), buf(rows, cols), pltpu.VMEM((2, rows, cols), jnp.int32),
            buf(3, rows, cols), buf(rows, cols), buf(11, cols // 128, rows, 128),
            buf(rows, cols), buf(rows, cols),
            buf(slots, fl + 16, fl), buf(slots, fl, fl), buf(slots, fl + 16, fl),
            buf(slots, fl, fl), buf(slots, fl, 128), buf(slots, fl, 128),
            buf(8, cols), buf(8, cols), buf(8, cols), buf(8, cols),
            buf(2, 4, 2, 8, 128), buf(8, 128), buf(ns, 8, 128), buf(nb, 128), buf(nb, 128),
            buf(fl, 128), buf(2 * nb, 128), buf(3, slots * fl // REFINE, 128),
            buf(slots, 128, 128),
            buf(slots, 1, 128), buf(ns, 1, 128), buf(ns, 1, 128),
            buf(slots, 24, 128), buf(ns, 24, 128), buf(ns, 24, 128),
            buf(2, 128, 128),
            buf(1, 1, 128), buf(nm, 1, 128), buf(1, 1, 128), buf(ns, 1, 128),
            pltpu.SMEM((ns,), jnp.int32),
            pltpu.SemaphoreType.DMA((7,)), pltpu.SemaphoreType.DMA((7,)),
            pltpu.SemaphoreType.DMA((7,)),
        ],
        compiler_params=pltpu.CompilerParams(
            collective_id=0, has_side_effects=True, vmem_limit_bytes=56 * 1024 * 1024
        ),
    )(
        slot_patch, patch_anchor.T, gauge_cells.reshape(1, -1),
        *(pltpu.with_memory_space_constraint(x, pltpu.HBM)
          for x in (coarse_state, coarse_seabed, open_faces, fine_state, fine_seabed)),
    )
    return pl.pallas_call(
        store_results,
        out_shape=tuple(jax.ShapeDtypeStruct(shape, f32) for shape in shapes),
        in_specs=[vmem] * 3,
        out_specs=(hbm,) * 3,
        scratch_shapes=[pltpu.SemaphoreType.DMA((3,))],
    )(*(pltpu.with_memory_space_constraint(x, pltpu.VMEM) for x in results))


def solution(mesh):
    return jax.shard_map(
        shards,
        mesh=mesh,
        in_specs=(
            P("member", None, "space", None),
            P("space", None),
            P(None, "space", None),
            P("member", None, "space", None, None),
            P("space", None, None),
            P(),
            P(),
            P(),
        ),
        out_specs=(
            P("member", None, "space", None),
            P("member", None, "space", None, None),
            P("member", None),
        ),
        check_vma=False,
    )
```

```python
import functools

import jax
import jax.numpy as jnp
from jax import lax
from jax.experimental import pallas as pl
from jax.experimental.pallas import tpu as pltpu
from jax.sharding import PartitionSpec as P

REFINE = 4
C = 0.5
MESH = pl.DeviceIdType.MESH
f32 = jnp.float32
NT = (((1,), (1,)), ((), ()))
NN = (((1,), (0,)), ((), ()))


def dot(a, b, dims=NN):
    return lax.dot_general(
        a, b, dims, precision=lax.Precision.HIGHEST, preferred_element_type=f32
    )


def terms(x):
    parts = []
    for _ in range(3):
        parts.append(x.astype(jnp.bfloat16))
        x = x - parts[-1].astype(f32)
    return parts


def dot3(a, b):
    b = b.astype(jnp.bfloat16)
    one, two, three = (
        lax.dot_general(part, b, NN, preferred_element_type=f32) for part in terms(a)
    )
    return one + (two + three)


def dot3_nt(a, b):
    a = a.astype(jnp.bfloat16)
    one, two, three = (
        lax.dot_general(a, part, NT, preferred_element_type=f32) for part in terms(b)
    )
    return one + (two + three)


def iota(shape, dim):
    return lax.broadcasted_iota(jnp.int32, shape, dim)


def roll(x, shift, axis):
    return pltpu.roll(x, shift, axis)


def kernel(
    ns, nm, slots,
    slot, anchor, gauge, coarse, seabed, faces, fine, fseabed,
    coarse_out, fine_out, spread_out,
    cs, sd, op, t1, t2, ex, ce, cn, fh, fu, fv, fd, eo, ed,
    up_s, dn_s, up_r, dn_r, rs, early_s, early_r, pay_s, pay_r, xb, gx, ycol, yrow, red, tp,
    m1_p, m1_s, m1_r, a2_p, a2_s, a2_r, pz, z_s, z_r, g_s, g_r, sidx,
    in_sem, send_sem, recv_sem,
):
    me = lax.axis_index("space")
    mem = lax.axis_index("member")
    rows, cols = sd.shape
    fl = fu.shape[-1]
    bl = fl // REFINE
    nb = slots * 8

    barrier = pltpu.get_barrier_semaphore()

    def far_first(i):
        return lax.rem(i + (5 * ns) // 8 - 1, ns - 1)

    def greet_space(i, carry):
        k = far_first(i) + 1
        pl.semaphore_signal(
            barrier, inc=1, device_id=(mem, lax.rem(me + k, ns)), device_id_type=MESH
        )
        return carry

    def greet_member(i, carry):
        k = lax.rem(i + nm // 2 - 2, nm - 1) + 1
        pl.semaphore_signal(
            barrier, inc=1, device_id=(lax.rem(mem + k, nm), me), device_id_type=MESH
        )
        return carry

    lax.fori_loop(0, nm - 1, greet_member, 0)
    lax.fori_loop(0, ns - 1, greet_space, 0)

    loads = [
        pltpu.make_async_copy(coarse.at[0], cs, in_sem.at[0]),
        pltpu.make_async_copy(seabed, sd, in_sem.at[1]),
        pltpu.make_async_copy(faces, op, in_sem.at[2]),
        pltpu.make_async_copy(fine.at[0, 0], fh.at[:, pl.ds(8, fl), :], in_sem.at[3]),
        pltpu.make_async_copy(fine.at[0, 1], fu, in_sem.at[4]),
        pltpu.make_async_copy(fine.at[0, 2], fv.at[:, pl.ds(8, fl), :], in_sem.at[5]),
        pltpu.make_async_copy(fseabed, fd, in_sem.at[6]),
    ]
    for load in loads:
        load.start()

    r0 = [jnp.clip(anchor[0, 2 * me + j], 1, rows - bl - 1) for j in range(2)]
    c0 = [jnp.clip(anchor[1, 2 * me + j], 1, cols - bl - 1) for j in range(2)]

    lane = iota((1, 128), 1)
    row8 = iota((8, 128), 0)
    lane8 = iota((8, 128), 1)
    rowc = iota((rows, cols), 0)
    lanec = iota((rows, cols), 1)
    lane1 = iota((1, cols), 1)
    block = None
    for j in range(2):
        inside = (
            (rowc >= r0[j]) & (rowc < r0[j] + bl) & (lanec >= c0[j]) & (lanec < c0[j] + bl)
        )
        block = inside if block is None else block | inside

    def west(x):
        first = iota(x.shape, 1) == 0
        return jnp.where(first, 0.0, roll(x, 1, 1))

    def east(x):
        last = iota(x.shape, 1) == cols - 1
        return jnp.where(last, 0.0, roll(x, cols - 1, 1))

    def south(x, below):
        return jnp.where(rowc == 0, below, roll(x, 1, 0))

    def north(x, above):
        return jnp.where(rowc == rows - 1, above, roll(x, rows - 1, 0))

    def cycles(full):
        total = None
        next_slab = jnp.minimum(me + 1, ns - 1)
        blank = jnp.zeros((bl, 128), f32)
        for j in range(2):
            cw = c0[j] - 1
            ch = c0[j] + bl
            tw = cw >> 7
            te = ch >> 7
            span = pl.ds(r0[j], bl)
            if full:
                west_parts = [ex[3 + t, tw, span, :] for t in range(4)]
                east_parts = [ex[t, te, span, :] for t in range(3)]
                east_parts.append(jnp.full((bl, 128), -1.0, f32))
            else:
                west_parts = [ex[3, tw, span, :], ex[4, tw, span, :], blank, blank]
                east_parts = [ex[0, te, span, :], ex[1, te, span, :], blank, blank]
            pick_w = jnp.where((row8 == 1) & (lane8 == (cw & 127)), 1.0, 0.0)
            pick_e = jnp.where((row8 == 0) & (lane8 == (ch & 127)), 1.0, 0.0)
            sides = dot(pick_w, jnp.concatenate(west_parts, axis=0), NT)
            sides = sides + dot(pick_e, jnp.concatenate(east_parts, axis=0), NT)
            for t in range(4):
                north_row = pl.ds(r0[j] + bl, 1)
                south_row = pl.ds(r0[j] - 1, 1)
                column = c0[j]
                source = 7 + t
                if t == 2 and not full:
                    column = jnp.clip(anchor[1, 2 * next_slab + j], 1, cols - bl - 1)
                    south_row = pl.ds(rows - 1, 1)
                    source = 7
                first = column >> 7
                second = jnp.minimum(first + 1, cols // 128 - 1)
                moved = []
                for half, tile in enumerate((first, second)):
                    if t < 2 or (t == 2 and full):
                        rs[j, t, half, 2:3, :] = ex[t, tile, north_row, :]
                    else:
                        rs[j, t, half, 2:3, :] = jnp.full((1, 128), -1.0, f32)
                    rs[j, t, half, 3:4, :] = ex[source, tile, south_row, :]
                    moved.append(roll(rs[j, t, half], (32 * t - column) & 127, 1))
                kept = lane8 - 32 * t < 128 - (column & 127)
                picked = jnp.where(kept, moved[0], moved[1])
                here = (row8 >= 2) & (row8 < 4) & (lane8 >= 32 * t) & (lane8 < 32 * t + 32)
                sides = jnp.where(here, picked, sides)
            sides = jnp.where(row8 < 4, sides, 0.0)
            total = sides if j == 0 else total + roll(sides, 4, 0)
        return total

    def hold(pairs):
        for f, held in pairs:
            for tile in range(cols // 128):
                ex[f, tile] = held[:, 128 * tile : 128 * tile + 128]

    rs[...] = jnp.zeros(rs.shape, f32)

    for load in loads[:3]:
        load.wait()
    h0, u0, v0 = cs[0], cs[1], cs[2]
    oe = op[0].astype(f32)
    on = op[1].astype(f32)
    cd = C * sd[...]
    ce[...] = cd * oe
    cn[...] = cd * on
    h1 = h0 - C * (u0 - west(u0) + v0 - south(v0, 0.0))
    t1[0] = h1
    up_s[0:1, :] = h1[rows - 1 : rows]
    up_s[1:2, :] = v0[rows - 1 : rows]
    up_s[2:3, :] = on[rows - 1 : rows]
    up_s[3:4, :] = cn[rows - 1 : rows, :]
    up_s[4:8, :] = jnp.zeros((4, cols), f32)
    dn_s[0:1, :] = h1[0:1]
    dn_s[1:2, :] = u0[0:1]
    dn_s[2:3, :] = v0[0:1]
    dn_s[3:4, :] = h1[1:2]
    dn_s[4:5, :] = oe[0:1]
    dn_s[5:6, :] = ce[0:1, :]
    dn_s[6:7, :] = on[0:1]
    dn_s[7:8, :] = cn[0:1, :]

    u1 = oe * u0 - ce[...] * (east(h1) - h1)
    v1 = on * v0 - cn[...] * (north(h1, 0.0) - h1)
    hold(((0, h0), (1, h1), (3, u0), (4, u1), (6, ce), (7, v0), (8, v1), (10, cn)))
    early = cycles(False)
    early_s[...] = early
    early_r[ns - 1] = early

    pl.semaphore_wait(barrier, ns + nm - 2)

    up = pltpu.make_async_remote_copy(
        src_ref=up_s, dst_ref=up_r, send_sem=send_sem.at[0], recv_sem=recv_sem.at[0],
        device_id=(mem, lax.rem(me + 1, ns)), device_id_type=MESH,
    )
    down = pltpu.make_async_remote_copy(
        src_ref=dn_s, dst_ref=dn_r, send_sem=send_sem.at[1], recv_sem=recv_sem.at[1],
        device_id=(mem, lax.rem(me + ns - 1, ns)), device_id_type=MESH,
    )
    up.start()
    down.start()

    def spread_early(i, carry):
        k = far_first(i)
        pltpu.make_async_remote_copy(
            src_ref=early_s, dst_ref=early_r.at[k], send_sem=send_sem.at[7],
            recv_sem=recv_sem.at[7], device_id=(mem, lax.rem(me + k + 1, ns)),
            device_id_type=MESH,
        ).start()
        return carry

    lax.fori_loop(0, ns - 1, spread_early, 0)

    my_patch = [slot[me * slots + s] for s in range(slots)]
    held_parent = [p >> 1 for p in my_patch]

    def find_slot(k, carry):
        d = lax.rem(me + k + 1, ns)
        which = jnp.int32(0)
        for s in range(1, slots):
            which = jnp.where(held_parent[s] == d, s, which)
        sidx[k] = which
        return carry

    lax.fori_loop(0, ns, find_slot, 0)

    xb[...] = jnp.zeros(xb.shape, f32)
    gx[...] = jnp.zeros(gx.shape, f32)
    tp[...] = jnp.zeros(tp.shape, f32)
    pz[...] = jnp.zeros(pz.shape, f32)
    up.wait()
    down.wait()

    low = me > 0
    high = me < ns - 1
    h1_m = up_r[0:1, :]
    v0_m = jnp.where(low, up_r[1:2, :], 0.0)
    h1 = jnp.where(rowc == 0, h1 + C * v0_m, h1)
    h1_p = jnp.where(high, dn_r[0:1, :] + C * v0[rows - 1 : rows], 0.0)
    u1 = oe * u0 - ce[...] * (east(h1) - h1)
    v1 = on * v0 - cn[...] * (north(h1, h1_p) - h1)
    u1_p = dn_r[4:5, :] * dn_r[1:2, :] - dn_r[5:6, :] * (east(h1_p) - h1_p)
    v1_p = dn_r[6:7, :] * dn_r[2:3, :] - dn_r[7:8, :] * (dn_r[3:4, :] - h1_p)
    v1_m = jnp.where(
        low, up_r[2:3, :] * v0_m - up_r[3:4, :] * (h1[0:1] - h1_m), 0.0
    )
    h2_p = jnp.where(
        high, h1_p - C * (u1_p - west(u1_p) + v1_p - v1[rows - 1 : rows]), 0.0
    )
    h1 = jnp.where(block, 0.0, h1)
    u1 = jnp.where(block, 0.0, u1)
    v1 = jnp.where(block, 0.0, v1)
    h2 = h1 - C * (u1 - west(u1) + v1 - south(v1, v1_m))
    t1[0], t1[1], t1[2] = h1, u1, v1
    t2[...] = h2
    u2 = oe * u1 - ce[...] * (east(h2) - h2)
    v2 = on * v1 - cn[...] * (north(h2, h2_p) - h2)
    hold(((2, h2), (5, u2), (8, v1), (9, v2)))

    payload = cycles(True)
    pay_s[...] = payload
    pay_r[ns - 1] = payload

    def spread_payload(i, carry):
        k = far_first(i)
        pltpu.make_async_remote_copy(
            src_ref=pay_s, dst_ref=pay_r.at[k], send_sem=send_sem.at[2],
            recv_sem=recv_sem.at[2], device_id=(mem, lax.rem(me + k + 1, ns)),
            device_id_type=MESH,
        ).start()
        return carry

    lax.fori_loop(0, ns - 1, spread_payload, 0)

    def all_of(ref, count, sem):
        part = ref.at[pl.ds(0, count)]
        pltpu.make_async_copy(part, part, sem).wait()

    cell = gauge[...]
    grow = cell // cols
    gcol = cell - grow * cols
    own_row = grow - me * rows
    covered = None
    for j in range(2):
        down = own_row - r0[j]
        right = gcol - c0[j]
        hit = (
            (down >= 0) & (right >= 0) & (down <= bl) & (right <= bl)
            & ((down < bl) | (right < bl))
        )
        covered = hit if covered is None else covered | hit
    pick_col = jnp.where(iota((cols, 128), 0) == gcol, 1.0, 0.0)
    found = dot3(h2, pick_col)
    outside = jnp.sum(
        jnp.where((iota((rows, 128), 0) == own_row) & jnp.logical_not(covered), found, 0.0),
        axis=0, keepdims=True,
    )

    rc_i = iota((fl, 128), 0)
    rc_l = iota((fl, 128), 1)
    spread_rows = jnp.where((rc_l & 31) == (rc_i >> 2), 1.0, 0.0)
    spread_lanes = jnp.where((rc_i & 31) == (rc_l >> 2), 1.0, 0.0)
    mean_h = jnp.where((rc_i >> 2) == rc_l, 0.25, 0.0)
    mean_u = jnp.where(rc_i == 4 * (rc_l - 32) + 3, 1.0, 0.0)
    mean_v = jnp.where((rc_i >> 2) == rc_l - 64, 0.25, 0.0)
    lane_nb = iota((nb, 128), 1)

    def expand(old, diff):
        both = jnp.concatenate([old, diff], axis=0)
        ycol[:, 0 : 2 * nb] = dot3_nt(spread_rows, both)
        yrow[...] = dot3(both, spread_lanes)
        for s in range(slots):
            eo[s] = roll(ycol[...], 127 - 8 * s, 1)
            ed[s] = roll(ycol[...], (255 - 8 * s - nb) % 128, 1)

    lane_f = iota((fl, 128), 1)
    every = range(slots)

    def update(k, final):
        kf = k.astype(f32)
        wf = (2.0 * kf + 1.0) / (2.0 * REFINE)
        wl = (kf + 1.0) / REFINE
        weight_of = jnp.where(lane == fl - 1, wl, wf)
        for s in every:
            n, o = 8 * s + 2, 8 * s + 3
            fv[s, 7:8, :] = yrow[o : o + 1, :] + wf * yrow[nb + o : nb + o + 1, :]
            fh[s, 8 + fl : 9 + fl, :] = yrow[n : n + 1, :] + wl * yrow[nb + n : nb + n + 1, :]
        held = []
        for s in every:
            edge = eo[s] + weight_of * ed[s]
            u = fu[s]
            v = fv[s, 8 : 8 + fl, :]
            v_s = fv[s, 7 : 7 + fl, :]
            u_w = jnp.where(lane_f == 0, edge, roll(u, 1, 1))
            h = fh[s, 8 : 8 + fl, :] - C * (u - u_w + v - v_s)
            held.append((h, u, v, edge))
        for s in every:
            fh[s, 8 : 8 + fl, :] = held[s][0]
        for s in every:
            h, u, v, edge = held[s]
            cdf = C * fd[s]
            h_e = jnp.where(lane_f == fl - 1, edge, roll(h, fl - 1, 1))
            h_n = fh[s, 9 : 9 + fl, :]
            u = u - cdf * (h_e - h)
            v = v - cdf * (h_n - h)
            if final:
                used = my_patch[s] >= 0
                fine_out[0, 0, s] = jnp.where(used, h, 0.0)
                fine_out[0, 1, s] = jnp.where(used, u, 0.0)
                fine_out[0, 2, s] = jnp.where(used, v, 0.0)
            else:
                fu[s] = u
                fv[s, 8 : 8 + fl, :] = v

    def fine_steps(last):
        def step(k, carry):
            update(k, False)
            return carry

        lax.fori_loop(0, REFINE - 1 if last else REFINE, step, 0)
        if last:
            update(jnp.int32(REFINE - 1), True)

    def averages(held):
        for s in range(slots):
            span = slice(bl * s, bl * s + bl)
            parts = [held(0, s, i) for i in range(REFINE)]
            red[0, span, :] = 0.25 * ((parts[0] + parts[1]) + (parts[2] + parts[3]))
            parts = [held(1, s, i) for i in range(REFINE)]
            red[1, span, :] = 0.25 * ((parts[0] + parts[1]) + (parts[2] + parts[3]))
            red[2, span, :] = held(2, s, REFINE - 1)
        return dot3(red[0], mean_h) + dot3(red[1], mean_u) + dot3(red[2], mean_v)

    def inner(f, s, i):
        if f == 1:
            return fu[s, pl.ds(i, bl, stride=REFINE), :]
        return (fh, None, fv)[f][s, pl.ds(8 + i, bl, stride=REFINE), :]

    def outer(f, s, i):
        return fine_out[0, f, s, pl.ds(i, bl, stride=REFINE), :]

    for load in loads[3:]:
        load.wait()
    def take(held, s, rows_from, count, slab):
        at = lax.rem(me - slab - 1 + 2 * ns, ns)
        p = jnp.maximum(my_patch[s], 0)
        got = held[at, pl.ds((p & 1) * 4 + rows_from, count), :]
        return jnp.where(my_patch[s] >= 0, got, 0.0)

    all_of(early_r, ns - 1, recv_sem.at[7])
    for s in range(slots):
        p = jnp.maximum(my_patch[s], 0)
        parent = p >> 1
        got = take(early_r, s, 0, 4, parent)
        lower = take(early_r, s, 3, 1, jnp.maximum(parent - 1, 0))
        mine = got[3:4]
        fix = C * roll(mine, 64, 1) * roll(lower, 96, 1)
        fixed = (lane >= 32) & (lane < 64) & (anchor[0, p] == 1) & (parent > 0)
        xb[8 * s : 8 * s + 3, :] = got[0:3]
        xb[8 * s + 3 : 8 * s + 4, :] = jnp.where(fixed, mine + fix, mine)

    x = xb[...]
    left = lane_nb < 32
    expand(
        jnp.where(left, x, 0.0), jnp.where(left, roll(x, 96, 1) - x, 0.0)
    )
    fine_steps(False)

    mean = averages(inner)
    pick_i = iota((16, 128), 0)
    pick_l = iota((16, 128), 1)
    pick = jnp.where((pick_i == 0) & (pick_l == 63), C, 0.0)
    pick = pick + jnp.where((pick_i == 1) & (pick_l == 0), 1.0, 0.0)
    pick = pick - jnp.where((pick_i == 1) & ((pick_l == 32) | (pick_l == 64)), C, 0.0)
    pick = pick + jnp.where((pick_i == 9) & (pick_l == 64), C, 0.0)
    for s in range(slots):
        tp[s, 64:96, :] = mean[bl * s : bl * s + bl]
    for s in range(slots):
        side = dot3_nt(pick, tp[s])
        side = side[0:8] + roll(side[8:16], 1, 1)
        gx[8 * s : 8 * s + 2, :] = side[0:2]
        top = tp[s, 95:96, :]
        low_row = tp[s, 64:65, :]
        gx[8 * s + 2 : 8 * s + 3, :] = C * top
        gx[8 * s + 3 : 8 * s + 4, :] = roll(low_row, 64, 1) - C * (
            roll(low_row, 32, 1) - jnp.where(lane > 64, roll(low_row, 33, 1), 0.0) + low_row
        )
    all_of(pay_r, ns - 1, recv_sem.at[2])
    for s in range(slots):
        xb[8 * s : 8 * s + 4, :] = take(pay_r, s, 0, 4, jnp.maximum(my_patch[s], 0) >> 1)
    x = xb[...]
    new = x - roll(x, 96, 1) * gx[...]
    mid = (lane_nb >= 64) & (lane_nb < 96)
    expand(
        jnp.where((lane_nb >= 32) & (lane_nb < 64), x, 0.0),
        jnp.where(mid, new - roll(x, 32, 1), 0.0),
    )
    fine_steps(True)
    mean = averages(outer)

    rel_col = jnp.full((1, 128), -1, jnp.int32)
    rel_row = jnp.full((1, 128), -1, jnp.int32)
    for s in range(slots):
        p = jnp.maximum(my_patch[s], 0)
        down = jnp.where(my_patch[s] >= 0, grow - ((p >> 1) * rows + anchor[0, p]), -1)
        right = gcol - anchor[1, p]
        in_rows = (down >= 0) & (down < bl)
        in_cols = (right >= 0) & (right < bl)
        hit = in_rows & in_cols
        rel_col = jnp.where(hit, right, rel_col)
        rel_row = jnp.where(hit, down + bl * s, rel_row)
        hit = in_rows & (right == bl)
        rel_col = jnp.where(hit, 64 + down, rel_col)
        rel_row = jnp.where(hit, bl * slots + 8 * s, rel_row)
        hit = (down == bl) & in_cols
        rel_col = jnp.where(hit, 64 + right, rel_col)
        rel_row = jnp.where(hit, bl * slots + 8 * s + 2, rel_row)
    pick_col = jnp.where(rc_i == rel_col, 1.0, 0.0)
    found = dot3(jnp.concatenate([mean, new], axis=0), pick_col)
    at_row = iota((bl * slots + nb, 128), 0) == rel_row
    value = outside + jnp.sum(jnp.where(at_row, found, 0.0), axis=0, keepdims=True)
    z_s[0] = value

    def send_member(i, carry):
        k = lax.rem(i + nm // 2 - 2, nm - 1)
        pltpu.make_async_remote_copy(
            src_ref=z_s.at[0], dst_ref=z_r.at[k], send_sem=send_sem.at[5],
            recv_sem=recv_sem.at[5], device_id=(lax.rem(mem + k + 1, nm), me),
            device_id_type=MESH,
        ).start()
        return carry

    lax.fori_loop(0, nm - 1, send_member, 0)
    for s in range(slots):
        tail = mean[bl * s + 24 : bl * s + 32]
        for i in range(3):
            piece = mean[bl * s + 8 * i : bl * s + 8 * i + 8]
            a2_p[s, 8 * i : 8 * i + 8, :] = jnp.where(
                lane8 < 96, piece, roll(tail, 96 - 32 * i, 1)
            )

    def send_mean(i, carry):
        k = far_first(i)
        a2_s[k] = a2_p[sidx[k]]
        pltpu.make_async_remote_copy(
            src_ref=a2_s.at[k], dst_ref=a2_r.at[k], send_sem=send_sem.at[4],
            recv_sem=recv_sem.at[4], device_id=(mem, lax.rem(me + k + 1, ns)),
            device_id_type=MESH,
        ).start()
        return carry

    lax.fori_loop(0, ns - 1, send_mean, 0)
    a2_r[ns - 1] = a2_p[sidx[ns - 1]]

    packed = jnp.zeros((nb, 128), f32)
    row_nb = iota((nb, 128), 0) & 7
    for q in range(4):
        here = (row_nb == q) & (lane_nb >= 32 * q) & (lane_nb < 32 * q + 32)
        packed = jnp.where(here, roll(new, (32 * q + 64) % 128, 1), packed)
    for s in range(slots):
        m1_p[s] = jnp.sum(packed[8 * s : 8 * s + 8], axis=0, keepdims=True)

    def send_cycle(i, carry):
        k = far_first(i)
        m1_s[k] = m1_p[sidx[k]]
        pltpu.make_async_remote_copy(
            src_ref=m1_s.at[k], dst_ref=m1_r.at[k], send_sem=send_sem.at[3],
            recv_sem=recv_sem.at[3], device_id=(mem, lax.rem(me + k + 1, ns)),
            device_id_type=MESH,
        ).start()
        return carry

    lax.fori_loop(0, ns - 1, send_cycle, 0)
    m1_r[ns - 1] = m1_p[sidx[ns - 1]]

    all_of(z_r, nm - 1, recv_sem.at[5])

    def weight(m):
        return (1.0 + 2.0 * m.astype(f32) / (nm - 1)) / (2.0 * nm)

    center = weight(mem) * value
    for k in range(nm - 1):
        center = center + weight(lax.rem(mem - k - 1 + nm, nm)) * z_r[k]
    g_s[0] = value - center

    def send_gauge(i, carry):
        k = far_first(i)
        pltpu.make_async_remote_copy(
            src_ref=g_s.at[0], dst_ref=g_r.at[k], send_sem=send_sem.at[6],
            recv_sem=recv_sem.at[6], device_id=(mem, lax.rem(me + k + 1, ns)),
            device_id_type=MESH,
        ).start()
        return carry

    lax.fori_loop(0, ns - 1, send_gauge, 0)

    def find_owner(i, carry):
        p = slot[i]
        return tuple(
            jnp.where(p == 2 * me + j, i, carry[j]) for j in range(2)
        )

    where_held = lax.fori_loop(0, ns * slots, find_owner, (jnp.int32(0), jnp.int32(0)))
    owner_at = [lax.rem(me - w // slots - 1 + 2 * ns, ns) for w in where_held]

    all_of(m1_r, ns - 1, recv_sem.at[3])
    rowh = iota((rows, 128), 0)
    laneh = iota((rows, 128), 1)
    h2 = t2[...]
    fixes = []
    for j in range(2):
        got = m1_r[owner_at[j]]
        match = (laneh & 31) == rowh - r0[j]
        rows_in = (rowc >= r0[j]) & (rowc < r0[j] + bl)
        cols_in = (lanec >= c0[j]) & (lanec < c0[j] + bl)
        east_col = jnp.sum(
            jnp.where(match & (laneh < 32), got, 0.0), axis=1, keepdims=True
        )
        west_col = jnp.sum(
            jnp.where(match & (laneh >= 32) & (laneh < 64), got, 0.0), axis=1, keepdims=True
        )
        got8 = jnp.broadcast_to(got, (8, 128))
        north_row = roll(got8, (c0[j] - 64) & 127, 1)[0:1]
        south_row = roll(got8, (c0[j] - 96) & 127, 1)[0:1]
        north_row = jnp.concatenate([north_row] * (cols // 128), axis=1)
        south_row = jnp.concatenate([south_row] * (cols // 128), axis=1)
        h2 = jnp.where(rows_in & (lanec == c0[j] + bl), east_col, h2)
        h2 = jnp.where(cols_in & (rowc == r0[j] + bl), north_row, h2)
        fixes.append((rows_in & (lanec == c0[j] - 1), west_col,
                      cols_in & (rowc == r0[j] - 1), south_row))
    u1, v1 = t1[1], t1[2]
    u2 = oe * u1 - ce[...] * (east(h2) - h2)
    v2 = on * v1 - cn[...] * (north(h2, h2_p) - h2)
    for at_west, west_col, at_south, south_row in fixes:
        u2 = jnp.where(at_west, west_col, u2)
        v2 = jnp.where(at_south, south_row, v2)
    coarse_out[0, 0], coarse_out[0, 1], coarse_out[0, 2] = h2, u2, v2

    all_of(a2_r, ns - 1, recv_sem.at[4])
    for j in range(2):
        at = owner_at[j]
        tail = jnp.zeros((8, 128), f32)
        for i in range(3):
            piece = a2_r[at, 8 * i : 8 * i + 8, :]
            pz[j, 32 + 8 * i : 40 + 8 * i, :] = piece
            here = (lane8 >= 32 * i) & (lane8 < 32 * i + 32)
            tail = jnp.where(here, roll(piece, 32 + 32 * i, 1), tail)
        pz[j, 56:64, :] = tail
        moved = pz[j, pl.ds(32 - r0[j], rows), :]
        inside = (
            (rowc >= r0[j]) & (rowc < r0[j] + bl) & (lanec >= c0[j]) & (lanec < c0[j] + bl)
        )
        for field in range(3):
            placed = roll(moved, (c0[j] - 32 * field) & 127, 1)
            placed = jnp.concatenate([placed] * (cols // 128), axis=1)
            coarse_out[0, field] = jnp.where(inside, placed, coarse_out[0, field])

    all_of(g_r, ns - 1, recv_sem.at[6])
    total = g_s[0]
    for k in range(ns - 1):
        total = total + g_r[k]
    spread_out[...] = total

    all_of(early_r, ns - 1, send_sem.at[7])
    all_of(pay_r, ns - 1, send_sem.at[2])
    all_of(m1_r, ns - 1, send_sem.at[3])
    all_of(a2_r, ns - 1, send_sem.at[4])
    all_of(z_r, nm - 1, send_sem.at[5])
    all_of(g_r, ns - 1, send_sem.at[6])


def store_results(coarse, fine, spread, coarse_out, fine_out, spread_out, sem):
    pairs = ((coarse, coarse_out), (fine, fine_out), (spread, spread_out))
    copies = [pltpu.make_async_copy(a, b, sem.at[i]) for i, (a, b) in enumerate(pairs)]
    for copy in copies:
        copy.start()
    for copy in copies:
        copy.wait()


def shards(
    coarse_state, coarse_seabed, open_faces, fine_state, fine_seabed, slot_patch, patch_anchor,
    gauge_cells,
):
    ns = lax.axis_size("space")
    nm = lax.axis_size("member")
    rows, cols = coarse_seabed.shape
    slots, fl = fine_seabed.shape[0], fine_seabed.shape[-1]
    nb = 8 * slots
    vmem, hbm, smem = (
        pl.BlockSpec(memory_space=space) for space in (pltpu.VMEM, pltpu.HBM, pltpu.SMEM)
    )

    def buf(*shape):
        return pltpu.VMEM(shape, f32)

    shapes = (coarse_state.shape, fine_state.shape, (1, gauge_cells.shape[0]))
    results = pl.pallas_call(
        functools.partial(kernel, ns, nm, slots),
        out_shape=tuple(pltpu.VMEM(shape, f32) for shape in shapes),
        in_specs=[smem, smem, vmem, hbm, hbm, hbm, hbm, hbm],
        out_specs=(vmem, vmem, vmem),
        scratch_shapes=[
            buf(3, rows, cols), buf(rows, cols), pltpu.VMEM((2, rows, cols), jnp.int32),
            buf(3, rows, cols), buf(rows, cols), buf(11, cols // 128, rows, 128),
            buf(rows, cols), buf(rows, cols),
            buf(slots, fl + 16, fl), buf(slots, fl, fl), buf(slots, fl + 16, fl),
            buf(slots, fl, fl), buf(slots, fl, 128), buf(slots, fl, 128),
            buf(8, cols), buf(8, cols), buf(8, cols), buf(8, cols),
            buf(2, 4, 2, 8, 128), buf(8, 128), buf(ns, 8, 128),
            buf(8, 128), buf(ns, 8, 128), buf(nb, 128), buf(nb, 128),
            buf(fl, 128), buf(2 * nb, 128), buf(3, slots * fl // REFINE, 128),
            buf(slots, 128, 128),
            buf(slots, 1, 128), buf(ns, 1, 128), buf(ns, 1, 128),
            buf(slots, 24, 128), buf(ns, 24, 128), buf(ns, 24, 128),
            buf(2, 128, 128),
            buf(1, 1, 128), buf(nm, 1, 128), buf(1, 1, 128), buf(ns, 1, 128),
            pltpu.SMEM((ns,), jnp.int32),
            pltpu.SemaphoreType.DMA((7,)), pltpu.SemaphoreType.DMA((8,)),
            pltpu.SemaphoreType.DMA((8,)),
        ],
        compiler_params=pltpu.CompilerParams(
            collective_id=0, has_side_effects=True, vmem_limit_bytes=56 * 1024 * 1024
        ),
    )(
        slot_patch, patch_anchor.T, gauge_cells.reshape(1, -1),
        *(pltpu.with_memory_space_constraint(x, pltpu.HBM)
          for x in (coarse_state, coarse_seabed, open_faces, fine_state, fine_seabed)),
    )
    return pl.pallas_call(
        store_results,
        out_shape=tuple(jax.ShapeDtypeStruct(shape, f32) for shape in shapes),
        in_specs=[vmem] * 3,
        out_specs=(hbm,) * 3,
        scratch_shapes=[pltpu.SemaphoreType.DMA((3,))],
    )(*(pltpu.with_memory_space_constraint(x, pltpu.VMEM) for x in results))


def solution(mesh):
    return jax.shard_map(
        shards,
        mesh=mesh,
        in_specs=(
            P("member", None, "space", None),
            P("space", None),
            P(None, "space", None),
            P("member", None, "space", None, None),
            P("space", None, None),
            P(),
            P(),
            P(),
        ),
        out_specs=(
            P("member", None, "space", None),
            P("member", None, "space", None, None),
            P("member", None),
        ),
        check_vma=False,
    )
```

```python
import functools

import jax
import jax.numpy as jnp
from jax import lax
from jax.experimental import pallas as pl
from jax.experimental.pallas import tpu as pltpu
from jax.sharding import PartitionSpec as P

REFINE = 4
C = 0.5
MESH = pl.DeviceIdType.MESH
f32 = jnp.float32
NT = (((1,), (1,)), ((), ()))
NN = (((1,), (0,)), ((), ()))


def terms(x):
    parts = []
    for _ in range(3):
        parts.append(x.astype(jnp.bfloat16))
        x = x - parts[-1].astype(f32)
    return parts


def dot3(a, b):
    b = b.astype(jnp.bfloat16)
    one, two, three = (
        lax.dot_general(part, b, NN, preferred_element_type=f32) for part in terms(a)
    )
    return one + (two + three)


def dot3_nt(a, b):
    a = a.astype(jnp.bfloat16)
    one, two, three = (
        lax.dot_general(a, part, NT, preferred_element_type=f32) for part in terms(b)
    )
    return one + (two + three)


def iota(shape, dim):
    return lax.broadcasted_iota(jnp.int32, shape, dim)


def roll(x, shift, axis):
    return pltpu.roll(x, shift, axis)


def kernel(
    ns, nm, slots,
    slot, anchor, gauge, coarse, seabed, faces, fine, fseabed,
    coarse_out, fine_out, spread_out,
    cs, sd, op, t1, t2, ex, ce, cn, fh, fu, fv, fd, eo, ed,
    up_s, dn_s, up_r, dn_r, rs, early_s, early_r, pay_s, pay_r, xb, gx, ycol, yrow, red, tp,
    m1_p, m1_s, m1_r, a2_p, a2_s, a2_r, pz, z_s, z_r, g_s, g_r, sidx,
    in_sem, send_sem, recv_sem,
):
    me = lax.axis_index("space")
    mem = lax.axis_index("member")
    rows, cols = sd.shape
    fl = fu.shape[-1]
    bl = fl // REFINE
    nb = slots * 8

    barrier = pltpu.get_barrier_semaphore()

    def far_first(i):
        return lax.rem(i + (5 * ns) // 8 - 1, ns - 1)

    def greet_space(i, carry):
        k = far_first(i) + 1
        pl.semaphore_signal(
            barrier, inc=1, device_id=(mem, lax.rem(me + k, ns)), device_id_type=MESH
        )
        return carry

    def greet_member(i, carry):
        k = lax.rem(i + nm // 2 - 2, nm - 1) + 1
        pl.semaphore_signal(
            barrier, inc=1, device_id=(lax.rem(mem + k, nm), me), device_id_type=MESH
        )
        return carry

    lax.fori_loop(0, nm - 1, greet_member, 0)
    lax.fori_loop(0, ns - 1, greet_space, 0)

    loads = [
        pltpu.make_async_copy(coarse.at[0], cs, in_sem.at[0]),
        pltpu.make_async_copy(seabed, sd, in_sem.at[1]),
        pltpu.make_async_copy(faces, op, in_sem.at[2]),
        pltpu.make_async_copy(fine.at[0, 0], fh.at[:, pl.ds(8, fl), :], in_sem.at[3]),
        pltpu.make_async_copy(fine.at[0, 1], fu, in_sem.at[4]),
        pltpu.make_async_copy(fine.at[0, 2], fv.at[:, pl.ds(8, fl), :], in_sem.at[5]),
        pltpu.make_async_copy(fseabed, fd, in_sem.at[6]),
    ]
    for load in loads[:3]:
        load.start()

    r0 = [jnp.clip(anchor[0, 2 * me + j], 1, rows - bl - 1) for j in range(2)]
    c0 = [jnp.clip(anchor[1, 2 * me + j], 1, cols - bl - 1) for j in range(2)]

    lane = iota((1, 128), 1)
    row8 = iota((8, 128), 0)
    lane8 = iota((8, 128), 1)
    rowc = iota((rows, cols), 0)
    lanec = iota((rows, cols), 1)
    lane1 = iota((1, cols), 1)
    block = None
    for j in range(2):
        inside = (
            (rowc >= r0[j]) & (rowc < r0[j] + bl) & (lanec >= c0[j]) & (lanec < c0[j] + bl)
        )
        block = inside if block is None else block | inside

    def west(x):
        first = iota(x.shape, 1) == 0
        return jnp.where(first, 0.0, roll(x, 1, 1))

    def east(x):
        last = iota(x.shape, 1) == cols - 1
        return jnp.where(last, 0.0, roll(x, cols - 1, 1))

    def south(x, below):
        return jnp.where(rowc == 0, below, roll(x, 1, 0))

    def north(x, above):
        return jnp.where(rowc == rows - 1, above, roll(x, rows - 1, 0))

    pick_row = iota((16, 256), 0)
    pick_lane = iota((16, 256), 1)

    def cycles(times):
        total = None
        next_slab = jnp.minimum(me + 1, ns - 1)
        blank = jnp.zeros((bl, 128), f32)
        for j in range(2):
            cw = c0[j] - 1
            ch = c0[j] + bl
            tw = cw >> 7
            te = ch >> 7
            span = pl.ds(r0[j], bl)
            level = jnp.full((bl, 128), -1.0, f32)
            west_parts = [ex[3 + t, tw, span, :] if t in times else blank for t in range(4)]
            east_parts = [ex[t, te, span, :] if t in times else blank for t in range(3)]
            east_parts.append(level if 3 in times else blank)
            at_west = (pick_row == 1) & (pick_lane == (cw & 127))
            at_east = (pick_row == 0) & (pick_lane == 128 + (ch & 127))
            both = jnp.concatenate(
                [jnp.concatenate(parts, axis=0) for parts in (west_parts, east_parts)], axis=1
            )
            sides = dot3_nt(jnp.where(at_west | at_east, 1.0, 0.0), both)[0:8]
            for t in range(4):
                if t not in times and 2 in times:
                    continue
                north_row = pl.ds(r0[j] + bl, 1)
                south_row = pl.ds(r0[j] - 1, 1)
                column = c0[j]
                source = 7 + t
                if t not in times:
                    column = jnp.clip(anchor[1, 2 * next_slab + j], 1, cols - bl - 1)
                    south_row = pl.ds(rows - 1, 1)
                    source = 7
                first = column >> 7
                second = jnp.minimum(first + 1, cols // 128 - 1)
                moved = []
                for half, tile in enumerate((first, second)):
                    if t in times and t < 3:
                        rs[j, t, half, 2:3, :] = ex[t, tile, north_row, :]
                    else:
                        rs[j, t, half, 2:3, :] = jnp.full((1, 128), -1.0, f32)
                    rs[j, t, half, 3:4, :] = ex[source, tile, south_row, :]
                    moved.append(roll(rs[j, t, half], (32 * t - column) & 127, 1))
                kept = lane8 - 32 * t < 128 - (column & 127)
                picked = jnp.where(kept, moved[0], moved[1])
                here = (row8 >= 2) & (row8 < 4) & (lane8 >= 32 * t) & (lane8 < 32 * t + 32)
                sides = jnp.where(here, picked, sides)
            sides = jnp.where(row8 < 4, sides, 0.0)
            total = sides if j == 0 else total + roll(sides, 4, 0)
        return total

    def hold(pairs):
        for f, held in pairs:
            for tile in range(cols // 128):
                ex[f, tile] = held[:, 128 * tile : 128 * tile + 128]

    rs[...] = jnp.zeros(rs.shape, f32)

    for load in loads[:3]:
        load.wait()
    for load in loads[3:]:
        load.start()
    h0, u0, v0 = cs[0], cs[1], cs[2]
    oe = op[0].astype(f32)
    on = op[1].astype(f32)
    cd = C * sd[...]
    ce[...] = cd * oe
    cn[...] = cd * on
    h1 = h0 - C * (u0 - west(u0) + v0 - south(v0, 0.0))
    up_s[0:1, :] = h1[rows - 1 : rows]
    up_s[1:2, :] = v0[rows - 1 : rows]
    up_s[2:3, :] = on[rows - 1 : rows]
    up_s[3:4, :] = cn[rows - 1 : rows, :]
    up_s[4:8, :] = jnp.zeros((4, cols), f32)
    dn_s[0:1, :] = h1[0:1]
    dn_s[1:2, :] = u0[0:1]
    dn_s[2:3, :] = v0[0:1]
    dn_s[3:4, :] = h1[1:2]
    dn_s[4:5, :] = oe[0:1]
    dn_s[5:6, :] = ce[0:1, :]
    dn_s[6:7, :] = on[0:1]
    dn_s[7:8, :] = cn[0:1, :]

    u1 = oe * u0 - ce[...] * (east(h1) - h1)
    v1 = on * v0 - cn[...] * (north(h1, 0.0) - h1)
    t1[0] = h1
    h1 = jnp.where(block, 0.0, h1)
    u1 = jnp.where(block, 0.0, u1)
    v1 = jnp.where(block, 0.0, v1)
    h2 = h1 - C * (u1 - west(u1) + v1 - south(v1, 0.0))
    t1[1], t1[2], t2[...] = u1, v1, h2
    u2 = oe * u1 - ce[...] * (east(h2) - h2)
    v2 = on * v1 - cn[...] * (north(h2, 0.0) - h2)
    hold(((0, h0), (1, h1), (2, h2), (3, u0), (4, u1), (5, u2), (6, ce)))
    hold(((7, v0), (8, v1), (9, v2), (10, cn)))
    early = cycles((0, 1, 3))
    early_s[...] = early
    early_r[ns - 1] = early

    pl.semaphore_wait(barrier, ns + nm - 2)

    up = pltpu.make_async_remote_copy(
        src_ref=up_s, dst_ref=up_r, send_sem=send_sem.at[0], recv_sem=recv_sem.at[0],
        device_id=(mem, lax.rem(me + 1, ns)), device_id_type=MESH,
    )
    down = pltpu.make_async_remote_copy(
        src_ref=dn_s, dst_ref=dn_r, send_sem=send_sem.at[1], recv_sem=recv_sem.at[1],
        device_id=(mem, lax.rem(me + ns - 1, ns)), device_id_type=MESH,
    )
    up.start()
    down.start()

    def spread_early(i, carry):
        k = far_first(i)
        pltpu.make_async_remote_copy(
            src_ref=early_s, dst_ref=early_r.at[k], send_sem=send_sem.at[7],
            recv_sem=recv_sem.at[7], device_id=(mem, lax.rem(me + k + 1, ns)),
            device_id_type=MESH,
        ).start()
        return carry

    lax.fori_loop(0, ns - 1, spread_early, 0)

    my_patch = [slot[me * slots + s] for s in range(slots)]
    held_parent = [p >> 1 for p in my_patch]

    def find_slot(k, carry):
        d = lax.rem(me + k + 1, ns)
        which = jnp.int32(0)
        for s in range(1, slots):
            which = jnp.where(held_parent[s] == d, s, which)
        sidx[k] = which
        return carry

    lax.fori_loop(0, ns, find_slot, 0)

    xb[...] = jnp.zeros(xb.shape, f32)
    gx[...] = jnp.zeros(gx.shape, f32)
    tp[...] = jnp.zeros(tp.shape, f32)
    pz[...] = jnp.zeros(pz.shape, f32)
    up.wait()
    down.wait()

    strip_row = iota((8, cols), 0)
    strip_lane = iota((8, cols), 1)

    def strip(o):
        inside = None
        for j in range(2):
            hit = (
                (strip_row + o >= r0[j]) & (strip_row + o < r0[j] + bl)
                & (strip_lane >= c0[j]) & (strip_lane < c0[j] + bl)
            )
            inside = hit if inside is None else inside | hit
        part = slice(o, o + 8)
        faces_here = (op[0, part, :].astype(f32), op[1, part, :].astype(f32))
        return inside, part, faces_here

    def strip_south(x, below):
        return jnp.where(strip_row == 0, below, roll(x, 1, 0))

    def strip_north(x, above):
        return jnp.where(strip_row == 7, above, roll(x, 7, 0))

    def renew(o, h, below_of, above, above2_of):
        inside, part, (oe_s, on_s) = strip(o)
        ce_s, cn_s = ce[part, :], cn[part, :]
        u = oe_s * cs[1, part, :] - ce_s * (east(h) - h)
        v = on_s * cs[2, part, :] - cn_s * (strip_north(h, above) - h)
        below = below_of(h)
        above2 = above2_of(v)
        hm = jnp.where(inside, 0.0, h)
        um = jnp.where(inside, 0.0, u)
        vm = jnp.where(inside, 0.0, v)
        second = hm - C * (um - west(um) + vm - strip_south(vm, below))
        u2 = oe_s * um - ce_s * (east(second) - second)
        v2 = on_s * vm - cn_s * (strip_north(second, above2) - second)
        t1[1, part, :], t1[2, part, :], t2[part, :] = um, vm, second
        for f, held in ((2, second), (5, u2), (8, vm), (9, v2)):
            for tile in range(cols // 128):
                ex[f, tile, part, :] = held[:, 128 * tile : 128 * tile + 128]
        return above2

    low = me > 0
    high = me < ns - 1
    h1_m = up_r[0:1, :]
    v0_m = jnp.where(low, up_r[1:2, :], 0.0)
    v0_top = cs[2, rows - 1 : rows, :]
    h1_p = jnp.where(high, dn_r[0:1, :] + C * v0_top, 0.0)
    u1_p = dn_r[4:5, :] * dn_r[1:2, :] - dn_r[5:6, :] * (east(h1_p) - h1_p)
    v1_p = dn_r[6:7, :] * dn_r[2:3, :] - dn_r[7:8, :] * (dn_r[3:4, :] - h1_p)

    def below_first(h):
        return jnp.where(low, up_r[2:3, :] * v0_m - up_r[3:4, :] * (h[0:1] - h1_m), 0.0)

    def above_last(v):
        return jnp.where(high, h1_p - C * (u1_p - west(u1_p) + v1_p - v[7:8]), 0.0)

    h_low = t1[0, 0:8, :]
    h_low = jnp.where(strip_row == 0, h_low + C * v0_m, h_low)
    above_low = t1[0, 8:9, :]
    second_above_low = t2[8:9, :]
    below_high = t1[2, rows - 9 : rows - 8, :]
    renew(0, h_low, below_first, above_low, lambda v: second_above_low)
    h2_p = renew(rows - 8, t1[0, rows - 8 : rows, :], lambda h: below_high, h1_p, above_last)

    payload = cycles((2,))
    pay_s[...] = payload
    pay_r[ns - 1] = payload

    def spread_payload(i, carry):
        k = far_first(i)
        pltpu.make_async_remote_copy(
            src_ref=pay_s, dst_ref=pay_r.at[k], send_sem=send_sem.at[2],
            recv_sem=recv_sem.at[2], device_id=(mem, lax.rem(me + k + 1, ns)),
            device_id_type=MESH,
        ).start()
        return carry

    lax.fori_loop(0, ns - 1, spread_payload, 0)

    def all_of(ref, count, sem):
        part = ref.at[pl.ds(0, count)]
        pltpu.make_async_copy(part, part, sem).wait()

    cell = gauge[...]
    grow = cell // cols
    gcol = cell - grow * cols
    own_row = grow - me * rows
    covered = None
    for j in range(2):
        down = own_row - r0[j]
        right = gcol - c0[j]
        hit = (
            (down >= 0) & (right >= 0) & (down <= bl) & (right <= bl)
            & ((down < bl) | (right < bl))
        )
        covered = hit if covered is None else covered | hit
    pick_col = jnp.where(iota((cols, 128), 0) == gcol, 1.0, 0.0)
    found = dot3(t2[...], pick_col)
    outside = jnp.sum(
        jnp.where((iota((rows, 128), 0) == own_row) & jnp.logical_not(covered), found, 0.0),
        axis=0, keepdims=True,
    )

    rc_i = iota((fl, 128), 0)
    rc_l = iota((fl, 128), 1)
    spread_rows = jnp.where((rc_l & 31) == (rc_i >> 2), 1.0, 0.0)
    spread_lanes = jnp.where((rc_i & 31) == (rc_l >> 2), 1.0, 0.0)
    mean_h = jnp.where((rc_i >> 2) == rc_l, 0.25, 0.0)
    mean_u = jnp.where(rc_i == 4 * (rc_l - 32) + 3, 1.0, 0.0)
    mean_v = jnp.where((rc_i >> 2) == rc_l - 64, 0.25, 0.0)
    lane_nb = iota((nb, 128), 1)

    def expand(old, diff):
        both = jnp.concatenate([old, diff], axis=0)
        ycol[:, 0 : 2 * nb] = dot3_nt(spread_rows, both)
        yrow[...] = dot3(both, spread_lanes)
        for s in range(slots):
            eo[s] = roll(ycol[...], 127 - 8 * s, 1)
            ed[s] = roll(ycol[...], (255 - 8 * s - nb) % 128, 1)

    lane_f = iota((fl, 128), 1)
    every = range(slots)

    def update(k, final):
        kf = k.astype(f32)
        wf = (2.0 * kf + 1.0) / (2.0 * REFINE)
        wl = (kf + 1.0) / REFINE
        weight_of = jnp.where(lane == fl - 1, wl, wf)
        for s in every:
            n, o = 8 * s + 2, 8 * s + 3
            fv[s, 7:8, :] = yrow[o : o + 1, :] + wf * yrow[nb + o : nb + o + 1, :]
            fh[s, 8 + fl : 9 + fl, :] = yrow[n : n + 1, :] + wl * yrow[nb + n : nb + n + 1, :]
        held = []
        for s in every:
            edge = eo[s] + weight_of * ed[s]
            u = fu[s]
            v = fv[s, 8 : 8 + fl, :]
            v_s = fv[s, 7 : 7 + fl, :]
            u_w = jnp.where(lane_f == 0, edge, roll(u, 1, 1))
            h = fh[s, 8 : 8 + fl, :] - C * (u - u_w + v - v_s)
            held.append((h, u, v, edge))
        for s in every:
            fh[s, 8 : 8 + fl, :] = held[s][0]
        for s in every:
            h, u, v, edge = held[s]
            cdf = C * fd[s]
            h_e = jnp.where(lane_f == fl - 1, edge, roll(h, fl - 1, 1))
            h_n = fh[s, 9 : 9 + fl, :]
            u = u - cdf * (h_e - h)
            v = v - cdf * (h_n - h)
            if final:
                used = my_patch[s] >= 0
                fine_out[0, 0, s] = jnp.where(used, h, 0.0)
                fine_out[0, 1, s] = jnp.where(used, u, 0.0)
                fine_out[0, 2, s] = jnp.where(used, v, 0.0)
            else:
                fu[s] = u
                fv[s, 8 : 8 + fl, :] = v

    def fine_steps(last):
        def step(k, carry):
            update(k, False)
            return carry

        lax.fori_loop(0, REFINE - 1 if last else REFINE, step, 0, unroll=True)
        if last:
            update(jnp.int32(REFINE - 1), True)

    def averages(held):
        for s in range(slots):
            span = slice(bl * s, bl * s + bl)
            parts = [held(0, s, i) for i in range(REFINE)]
            red[0, span, :] = 0.25 * ((parts[0] + parts[1]) + (parts[2] + parts[3]))
            parts = [held(1, s, i) for i in range(REFINE)]
            red[1, span, :] = 0.25 * ((parts[0] + parts[1]) + (parts[2] + parts[3]))
            red[2, span, :] = held(2, s, REFINE - 1)
        return dot3(red[0], mean_h) + dot3(red[1], mean_u) + dot3(red[2], mean_v)

    def inner(f, s, i):
        if f == 1:
            return fu[s, pl.ds(i, bl, stride=REFINE), :]
        return (fh, None, fv)[f][s, pl.ds(8 + i, bl, stride=REFINE), :]

    def outer(f, s, i):
        return fine_out[0, f, s, pl.ds(i, bl, stride=REFINE), :]

    for load in loads[3:]:
        load.wait()
    def take(held, s, rows_from, count, slab):
        at = lax.rem(me - slab - 1 + 2 * ns, ns)
        p = jnp.maximum(my_patch[s], 0)
        got = held[at, pl.ds((p & 1) * 4 + rows_from, count), :]
        return jnp.where(my_patch[s] >= 0, got, 0.0)

    all_of(early_r, ns - 1, recv_sem.at[7])
    for s in range(slots):
        p = jnp.maximum(my_patch[s], 0)
        parent = p >> 1
        got = take(early_r, s, 0, 4, parent)
        lower = take(early_r, s, 3, 1, jnp.maximum(parent - 1, 0))
        mine = got[3:4]
        fix = C * roll(mine, 64, 1) * roll(lower, 96, 1)
        fixed = (lane >= 32) & (lane < 64) & (anchor[0, p] == 1) & (parent > 0)
        xb[8 * s : 8 * s + 3, :] = got[0:3]
        xb[8 * s + 3 : 8 * s + 4, :] = jnp.where(fixed, mine + fix, mine)

    x = xb[...]
    left = lane_nb < 32
    expand(
        jnp.where(left, x, 0.0), jnp.where(left, roll(x, 96, 1) - x, 0.0)
    )
    fine_steps(False)

    mean = averages(inner)
    pick_i = iota((16, 128), 0)
    pick_l = iota((16, 128), 1)
    pick = jnp.where((pick_i == 0) & (pick_l == 63), C, 0.0)
    pick = pick + jnp.where((pick_i == 1) & (pick_l == 0), 1.0, 0.0)
    pick = pick - jnp.where((pick_i == 1) & ((pick_l == 32) | (pick_l == 64)), C, 0.0)
    pick = pick + jnp.where((pick_i == 9) & (pick_l == 64), C, 0.0)
    for s in range(slots):
        tp[s, 64:96, :] = mean[bl * s : bl * s + bl]
    for s in range(slots):
        side = dot3_nt(pick, tp[s])
        side = side[0:8] + roll(side[8:16], 1, 1)
        gx[8 * s : 8 * s + 2, :] = side[0:2]
        top = tp[s, 95:96, :]
        low_row = tp[s, 64:65, :]
        gx[8 * s + 2 : 8 * s + 3, :] = C * top
        gx[8 * s + 3 : 8 * s + 4, :] = roll(low_row, 64, 1) - C * (
            roll(low_row, 32, 1) - jnp.where(lane > 64, roll(low_row, 33, 1), 0.0) + low_row
        )
    all_of(pay_r, ns - 1, recv_sem.at[2])
    mid = (lane_nb >= 64) & (lane_nb < 96)
    for s in range(slots):
        xb[8 * s : 8 * s + 4, :] = take(pay_r, s, 0, 4, jnp.maximum(my_patch[s], 0) >> 1)
    x = jnp.where(mid, xb[...], x)
    new = x - roll(x, 96, 1) * gx[...]
    expand(
        jnp.where((lane_nb >= 32) & (lane_nb < 64), x, 0.0),
        jnp.where(mid, new - roll(x, 32, 1), 0.0),
    )
    fine_steps(True)
    mean = averages(outer)

    rel_col = jnp.full((1, 128), -1, jnp.int32)
    rel_row = jnp.full((1, 128), -1, jnp.int32)
    for s in range(slots):
        p = jnp.maximum(my_patch[s], 0)
        down = jnp.where(my_patch[s] >= 0, grow - ((p >> 1) * rows + anchor[0, p]), -1)
        right = gcol - anchor[1, p]
        in_rows = (down >= 0) & (down < bl)
        in_cols = (right >= 0) & (right < bl)
        hit = in_rows & in_cols
        rel_col = jnp.where(hit, right, rel_col)
        rel_row = jnp.where(hit, down + bl * s, rel_row)
        hit = in_rows & (right == bl)
        rel_col = jnp.where(hit, 64 + down, rel_col)
        rel_row = jnp.where(hit, bl * slots + 8 * s, rel_row)
        hit = (down == bl) & in_cols
        rel_col = jnp.where(hit, 64 + right, rel_col)
        rel_row = jnp.where(hit, bl * slots + 8 * s + 2, rel_row)
    pick_col = jnp.where(rc_i == rel_col, 1.0, 0.0)
    found = dot3(jnp.concatenate([mean, new], axis=0), pick_col)
    at_row = iota((bl * slots + nb, 128), 0) == rel_row
    value = outside + jnp.sum(jnp.where(at_row, found, 0.0), axis=0, keepdims=True)
    z_s[0] = value

    def send_member(i, carry):
        k = lax.rem(i + nm // 2 - 2, nm - 1)
        pltpu.make_async_remote_copy(
            src_ref=z_s.at[0], dst_ref=z_r.at[k], send_sem=send_sem.at[5],
            recv_sem=recv_sem.at[5], device_id=(lax.rem(mem + k + 1, nm), me),
            device_id_type=MESH,
        ).start()
        return carry

    lax.fori_loop(0, nm - 1, send_member, 0)
    for s in range(slots):
        tail = mean[bl * s + 24 : bl * s + 32]
        for i in range(3):
            piece = mean[bl * s + 8 * i : bl * s + 8 * i + 8]
            a2_p[s, 8 * i : 8 * i + 8, :] = jnp.where(
                lane8 < 96, piece, roll(tail, 96 - 32 * i, 1)
            )

    def send_mean(i, carry):
        k = far_first(i)
        a2_s[k] = a2_p[sidx[k]]
        pltpu.make_async_remote_copy(
            src_ref=a2_s.at[k], dst_ref=a2_r.at[k], send_sem=send_sem.at[4],
            recv_sem=recv_sem.at[4], device_id=(mem, lax.rem(me + k + 1, ns)),
            device_id_type=MESH,
        ).start()
        return carry

    lax.fori_loop(0, ns - 1, send_mean, 0)
    a2_r[ns - 1] = a2_p[sidx[ns - 1]]

    packed = jnp.zeros((nb, 128), f32)
    row_nb = iota((nb, 128), 0) & 7
    for q in range(4):
        here = (row_nb == q) & (lane_nb >= 32 * q) & (lane_nb < 32 * q + 32)
        packed = jnp.where(here, roll(new, (32 * q + 64) % 128, 1), packed)
    for s in range(slots):
        m1_p[s] = jnp.sum(packed[8 * s : 8 * s + 8], axis=0, keepdims=True)

    def send_cycle(i, carry):
        k = far_first(i)
        m1_s[k] = m1_p[sidx[k]]
        pltpu.make_async_remote_copy(
            src_ref=m1_s.at[k], dst_ref=m1_r.at[k], send_sem=send_sem.at[3],
            recv_sem=recv_sem.at[3], device_id=(mem, lax.rem(me + k + 1, ns)),
            device_id_type=MESH,
        ).start()
        return carry

    lax.fori_loop(0, ns - 1, send_cycle, 0)
    m1_r[ns - 1] = m1_p[sidx[ns - 1]]

    all_of(z_r, nm - 1, recv_sem.at[5])

    def weight(m):
        return (1.0 + 2.0 * m.astype(f32) / (nm - 1)) / (2.0 * nm)

    center = weight(mem) * value
    for k in range(nm - 1):
        center = center + weight(lax.rem(mem - k - 1 + nm, nm)) * z_r[k]
    g_s[0] = value - center

    def send_gauge(i, carry):
        k = far_first(i)
        pltpu.make_async_remote_copy(
            src_ref=g_s.at[0], dst_ref=g_r.at[k], send_sem=send_sem.at[6],
            recv_sem=recv_sem.at[6], device_id=(mem, lax.rem(me + k + 1, ns)),
            device_id_type=MESH,
        ).start()
        return carry

    lax.fori_loop(0, ns - 1, send_gauge, 0)

    def find_owner(i, carry):
        p = slot[i]
        return tuple(
            jnp.where(p == 2 * me + j, i, carry[j]) for j in range(2)
        )

    where_held = lax.fori_loop(0, ns * slots, find_owner, (jnp.int32(0), jnp.int32(0)))
    owner_at = [lax.rem(me - w // slots - 1 + 2 * ns, ns) for w in where_held]

    all_of(m1_r, ns - 1, recv_sem.at[3])
    rowh = iota((rows, 128), 0)
    laneh = iota((rows, 128), 1)
    h2 = t2[...]
    fixes = []
    for j in range(2):
        got = m1_r[owner_at[j]]
        match = (laneh & 31) == rowh - r0[j]
        rows_in = (rowc >= r0[j]) & (rowc < r0[j] + bl)
        cols_in = (lanec >= c0[j]) & (lanec < c0[j] + bl)
        east_col = jnp.sum(
            jnp.where(match & (laneh < 32), got, 0.0), axis=1, keepdims=True
        )
        west_col = jnp.sum(
            jnp.where(match & (laneh >= 32) & (laneh < 64), got, 0.0), axis=1, keepdims=True
        )
        got8 = jnp.broadcast_to(got, (8, 128))
        north_row = roll(got8, (c0[j] - 64) & 127, 1)[0:1]
        south_row = roll(got8, (c0[j] - 96) & 127, 1)[0:1]
        north_row = jnp.concatenate([north_row] * (cols // 128), axis=1)
        south_row = jnp.concatenate([south_row] * (cols // 128), axis=1)
        h2 = jnp.where(rows_in & (lanec == c0[j] + bl), east_col, h2)
        h2 = jnp.where(cols_in & (rowc == r0[j] + bl), north_row, h2)
        fixes.append((rows_in & (lanec == c0[j] - 1), west_col,
                      cols_in & (rowc == r0[j] - 1), south_row))
    u1, v1 = t1[1], t1[2]
    u2 = oe * u1 - ce[...] * (east(h2) - h2)
    v2 = on * v1 - cn[...] * (north(h2, h2_p) - h2)
    for at_west, west_col, at_south, south_row in fixes:
        u2 = jnp.where(at_west, west_col, u2)
        v2 = jnp.where(at_south, south_row, v2)
    coarse_out[0, 0], coarse_out[0, 1], coarse_out[0, 2] = h2, u2, v2

    all_of(a2_r, ns - 1, recv_sem.at[4])
    for j in range(2):
        at = owner_at[j]
        tail = jnp.zeros((8, 128), f32)
        for i in range(3):
            piece = a2_r[at, 8 * i : 8 * i + 8, :]
            pz[j, 32 + 8 * i : 40 + 8 * i, :] = piece
            here = (lane8 >= 32 * i) & (lane8 < 32 * i + 32)
            tail = jnp.where(here, roll(piece, 32 + 32 * i, 1), tail)
        pz[j, 56:64, :] = tail
        moved = pz[j, pl.ds(32 - r0[j], rows), :]
        inside = (
            (rowc >= r0[j]) & (rowc < r0[j] + bl) & (lanec >= c0[j]) & (lanec < c0[j] + bl)
        )
        for field in range(3):
            placed = roll(moved, (c0[j] - 32 * field) & 127, 1)
            placed = jnp.concatenate([placed] * (cols // 128), axis=1)
            coarse_out[0, field] = jnp.where(inside, placed, coarse_out[0, field])

    all_of(g_r, ns - 1, recv_sem.at[6])
    total = g_s[0]
    for k in range(ns - 1):
        total = total + g_r[k]
    spread_out[...] = total

    all_of(early_r, ns - 1, send_sem.at[7])
    all_of(pay_r, ns - 1, send_sem.at[2])
    all_of(m1_r, ns - 1, send_sem.at[3])
    all_of(a2_r, ns - 1, send_sem.at[4])
    all_of(z_r, nm - 1, send_sem.at[5])
    all_of(g_r, ns - 1, send_sem.at[6])


def store_results(coarse, fine, spread, coarse_out, fine_out, spread_out, sem):
    pairs = ((coarse, coarse_out), (fine, fine_out), (spread, spread_out))
    copies = [pltpu.make_async_copy(a, b, sem.at[i]) for i, (a, b) in enumerate(pairs)]
    for copy in copies:
        copy.start()
    for copy in copies:
        copy.wait()


def shards(
    coarse_state, coarse_seabed, open_faces, fine_state, fine_seabed, slot_patch, patch_anchor,
    gauge_cells,
):
    ns = lax.axis_size("space")
    nm = lax.axis_size("member")
    rows, cols = coarse_seabed.shape
    slots, fl = fine_seabed.shape[0], fine_seabed.shape[-1]
    nb = 8 * slots
    vmem, hbm, smem = (
        pl.BlockSpec(memory_space=space) for space in (pltpu.VMEM, pltpu.HBM, pltpu.SMEM)
    )

    def buf(*shape):
        return pltpu.VMEM(shape, f32)

    shapes = (coarse_state.shape, fine_state.shape, (1, gauge_cells.shape[0]))
    results = pl.pallas_call(
        functools.partial(kernel, ns, nm, slots),
        out_shape=tuple(pltpu.VMEM(shape, f32) for shape in shapes),
        in_specs=[smem, smem, vmem, hbm, hbm, hbm, hbm, hbm],
        out_specs=(vmem, vmem, vmem),
        scratch_shapes=[
            buf(3, rows, cols), buf(rows, cols), pltpu.VMEM((2, rows, cols), jnp.int32),
            buf(3, rows, cols), buf(rows, cols), buf(11, cols // 128, rows, 128),
            buf(rows, cols), buf(rows, cols),
            buf(slots, fl + 16, fl), buf(slots, fl, fl), buf(slots, fl + 16, fl),
            buf(slots, fl, fl), buf(slots, fl, 128), buf(slots, fl, 128),
            buf(8, cols), buf(8, cols), buf(8, cols), buf(8, cols),
            buf(2, 4, 2, 8, 128), buf(8, 128), buf(ns, 8, 128),
            buf(8, 128), buf(ns, 8, 128), buf(nb, 128), buf(nb, 128),
            buf(fl, 128), buf(2 * nb, 128), buf(3, slots * fl // REFINE, 128),
            buf(slots, 128, 128),
            buf(slots, 1, 128), buf(ns, 1, 128), buf(ns, 1, 128),
            buf(slots, 24, 128), buf(ns, 24, 128), buf(ns, 24, 128),
            buf(2, 128, 128),
            buf(1, 1, 128), buf(nm, 1, 128), buf(1, 1, 128), buf(ns, 1, 128),
            pltpu.SMEM((ns,), jnp.int32),
            pltpu.SemaphoreType.DMA((7,)), pltpu.SemaphoreType.DMA((8,)),
            pltpu.SemaphoreType.DMA((8,)),
        ],
        compiler_params=pltpu.CompilerParams(
            collective_id=0, has_side_effects=True, vmem_limit_bytes=56 * 1024 * 1024
        ),
    )(
        slot_patch, patch_anchor.T, gauge_cells.reshape(1, -1),
        *(pltpu.with_memory_space_constraint(x, pltpu.HBM)
          for x in (coarse_state, coarse_seabed, open_faces, fine_state, fine_seabed)),
    )
    return pl.pallas_call(
        store_results,
        out_shape=tuple(jax.ShapeDtypeStruct(shape, f32) for shape in shapes),
        in_specs=[vmem] * 3,
        out_specs=(hbm,) * 3,
        scratch_shapes=[pltpu.SemaphoreType.DMA((3,))],
    )(*(pltpu.with_memory_space_constraint(x, pltpu.VMEM) for x in results))


def solution(mesh):
    return jax.shard_map(
        shards,
        mesh=mesh,
        in_specs=(
            P("member", None, "space", None),
            P("space", None),
            P(None, "space", None),
            P("member", None, "space", None, None),
            P("space", None, None),
            P(),
            P(),
            P(),
        ),
        out_specs=(
            P("member", None, "space", None),
            P("member", None, "space", None, None),
            P("member", None),
        ),
        check_vma=False,
    )
```

```python
import functools

import jax
import jax.numpy as jnp
from jax import lax
from jax.experimental import pallas as pl
from jax.experimental.pallas import tpu as pltpu
from jax.sharding import PartitionSpec as P

REFINE = 4
C = 0.5
MESH = pl.DeviceIdType.MESH
f32 = jnp.float32
NT = (((1,), (1,)), ((), ()))
NN = (((1,), (0,)), ((), ()))


def terms(x):
    parts = []
    for _ in range(3):
        parts.append(x.astype(jnp.bfloat16))
        x = x - parts[-1].astype(f32)
    return parts


def dot3(a, b):
    b = b.astype(jnp.bfloat16)
    one, two, three = (
        lax.dot_general(part, b, NN, preferred_element_type=f32) for part in terms(a)
    )
    return one + (two + three)


def dot3_nt(a, b):
    a = a.astype(jnp.bfloat16)
    one, two, three = (
        lax.dot_general(a, part, NT, preferred_element_type=f32) for part in terms(b)
    )
    return one + (two + three)


def iota(shape, dim):
    return lax.broadcasted_iota(jnp.int32, shape, dim)


def roll(x, shift, axis):
    return pltpu.roll(x, shift, axis)


def kernel(
    ns, nm, slots,
    slot, anchor, gauge, coarse, seabed, faces, fine, fseabed,
    coarse_out, fine_out, spread_out,
    cs, sd, op, t1, t2, ex, ce, cn, fh, fu, fv, fd, eo, ed,
    up_s, dn_s, up_r, dn_r, rs, early_s, early_r, pay_s, pay_r, xb, gx, ycol, yrow, red, tp,
    m1_p, m1_s, m1_r, a2_p, a2_s, a2_r, pz, z_s, z_r, g_s, g_r, sidx,
    in_sem, send_sem, recv_sem,
):
    me = lax.axis_index("space")
    mem = lax.axis_index("member")
    rows, cols = sd.shape
    fl = fu.shape[-1]
    bl = fl // REFINE
    nb = slots * 8

    barrier = pltpu.get_barrier_semaphore()

    def far_first(i):
        return lax.rem(i + (5 * ns) // 8 - 1, ns - 1)

    def greet_space(i, carry):
        k = far_first(i) + 1
        pl.semaphore_signal(
            barrier, inc=1, device_id=(mem, lax.rem(me + k, ns)), device_id_type=MESH
        )
        return carry

    def greet_member(i, carry):
        k = lax.rem(i + nm // 2 - 2, nm - 1) + 1
        pl.semaphore_signal(
            barrier, inc=1, device_id=(lax.rem(mem + k, nm), me), device_id_type=MESH
        )
        return carry

    lax.fori_loop(0, nm - 1, greet_member, 0, unroll=True)
    lax.fori_loop(0, ns - 1, greet_space, 0, unroll=True)

    loads = [
        pltpu.make_async_copy(coarse.at[0], cs, in_sem.at[0]),
        pltpu.make_async_copy(seabed, sd, in_sem.at[1]),
        pltpu.make_async_copy(faces, op, in_sem.at[2]),
        pltpu.make_async_copy(fine.at[0, 0], fh.at[:, pl.ds(8, fl), :], in_sem.at[3]),
        pltpu.make_async_copy(fine.at[0, 1], fu, in_sem.at[4]),
        pltpu.make_async_copy(fine.at[0, 2], fv.at[:, pl.ds(8, fl), :], in_sem.at[5]),
        pltpu.make_async_copy(fseabed, fd, in_sem.at[6]),
    ]
    for load in loads[:3]:
        load.start()

    r0 = [jnp.clip(anchor[0, 2 * me + j], 1, rows - bl - 1) for j in range(2)]
    c0 = [jnp.clip(anchor[1, 2 * me + j], 1, cols - bl - 1) for j in range(2)]

    lane = iota((1, 128), 1)
    row8 = iota((8, 128), 0)
    lane8 = iota((8, 128), 1)
    rowc = iota((rows, cols), 0)
    lanec = iota((rows, cols), 1)
    lane1 = iota((1, cols), 1)
    block = None
    for j in range(2):
        inside = (
            (rowc >= r0[j]) & (rowc < r0[j] + bl) & (lanec >= c0[j]) & (lanec < c0[j] + bl)
        )
        block = inside if block is None else block | inside

    def west(x):
        first = iota(x.shape, 1) == 0
        return jnp.where(first, 0.0, roll(x, 1, 1))

    def east(x):
        last = iota(x.shape, 1) == cols - 1
        return jnp.where(last, 0.0, roll(x, cols - 1, 1))

    def south(x, below):
        return jnp.where(rowc == 0, below, roll(x, 1, 0))

    def north(x, above):
        return jnp.where(rowc == rows - 1, above, roll(x, rows - 1, 0))

    pick_row = iota((16, 256), 0)
    pick_lane = iota((16, 256), 1)

    def cycles(times):
        total = None
        next_slab = jnp.minimum(me + 1, ns - 1)
        blank = jnp.zeros((bl, 128), f32)
        for j in range(2):
            cw = c0[j] - 1
            ch = c0[j] + bl
            tw = cw >> 7
            te = ch >> 7
            span = pl.ds(r0[j], bl)
            level = jnp.full((bl, 128), -1.0, f32)
            west_parts = [ex[3 + t, tw, span, :] if t in times else blank for t in range(4)]
            east_parts = [ex[t, te, span, :] if t in times else blank for t in range(3)]
            east_parts.append(level if 3 in times else blank)
            at_west = (pick_row == 1) & (pick_lane == (cw & 127))
            at_east = (pick_row == 0) & (pick_lane == 128 + (ch & 127))
            both = jnp.concatenate(
                [jnp.concatenate(parts, axis=0) for parts in (west_parts, east_parts)], axis=1
            )
            sides = dot3_nt(jnp.where(at_west | at_east, 1.0, 0.0), both)[0:8]
            for t in range(4):
                if t not in times and 2 in times:
                    continue
                north_row = pl.ds(r0[j] + bl, 1)
                south_row = pl.ds(r0[j] - 1, 1)
                column = c0[j]
                source = 7 + t
                if t not in times:
                    column = jnp.clip(anchor[1, 2 * next_slab + j], 1, cols - bl - 1)
                    south_row = pl.ds(rows - 1, 1)
                    source = 7
                first = column >> 7
                second = jnp.minimum(first + 1, cols // 128 - 1)
                moved = []
                for half, tile in enumerate((first, second)):
                    if t in times and t < 3:
                        rs[j, t, half, 2:3, :] = ex[t, tile, north_row, :]
                    else:
                        rs[j, t, half, 2:3, :] = jnp.full((1, 128), -1.0, f32)
                    rs[j, t, half, 3:4, :] = ex[source, tile, south_row, :]
                    moved.append(roll(rs[j, t, half], (32 * t - column) & 127, 1))
                kept = lane8 - 32 * t < 128 - (column & 127)
                picked = jnp.where(kept, moved[0], moved[1])
                here = (row8 >= 2) & (row8 < 4) & (lane8 >= 32 * t) & (lane8 < 32 * t + 32)
                sides = jnp.where(here, picked, sides)
            sides = jnp.where(row8 < 4, sides, 0.0)
            total = sides if j == 0 else total + roll(sides, 4, 0)
        return total

    def hold(pairs):
        for f, held in pairs:
            for tile in range(cols // 128):
                ex[f, tile] = held[:, 128 * tile : 128 * tile + 128]

    rs[...] = jnp.zeros(rs.shape, f32)

    for load in loads[:3]:
        load.wait()
    for load in loads[3:]:
        load.start()
    h0, u0, v0 = cs[0], cs[1], cs[2]
    oe = op[0].astype(f32)
    on = op[1].astype(f32)
    cd = C * sd[...]
    ce[...] = cd * oe
    cn[...] = cd * on
    h1 = h0 - C * (u0 - west(u0) + v0 - south(v0, 0.0))
    up_s[0:1, :] = h1[rows - 1 : rows]
    up_s[1:2, :] = v0[rows - 1 : rows]
    up_s[2:3, :] = on[rows - 1 : rows]
    up_s[3:4, :] = cn[rows - 1 : rows, :]
    up_s[4:8, :] = jnp.zeros((4, cols), f32)
    dn_s[0:1, :] = h1[0:1]
    dn_s[1:2, :] = u0[0:1]
    dn_s[2:3, :] = v0[0:1]
    dn_s[3:4, :] = h1[1:2]
    dn_s[4:5, :] = oe[0:1]
    dn_s[5:6, :] = ce[0:1, :]
    dn_s[6:7, :] = on[0:1]
    dn_s[7:8, :] = cn[0:1, :]

    u1 = oe * u0 - ce[...] * (east(h1) - h1)
    v1 = on * v0 - cn[...] * (north(h1, 0.0) - h1)
    t1[0] = h1
    h1 = jnp.where(block, 0.0, h1)
    u1 = jnp.where(block, 0.0, u1)
    v1 = jnp.where(block, 0.0, v1)
    h2 = h1 - C * (u1 - west(u1) + v1 - south(v1, 0.0))
    t1[1], t1[2], t2[...] = u1, v1, h2
    u2 = oe * u1 - ce[...] * (east(h2) - h2)
    v2 = on * v1 - cn[...] * (north(h2, 0.0) - h2)
    hold(((0, h0), (1, h1), (2, h2), (3, u0), (4, u1), (5, u2), (6, ce)))
    hold(((7, v0), (8, v1), (9, v2), (10, cn)))
    early = cycles((0, 1, 3))
    early_s[...] = early
    early_r[ns - 1] = early

    pl.semaphore_wait(barrier, ns + nm - 2)

    up = pltpu.make_async_remote_copy(
        src_ref=up_s, dst_ref=up_r, send_sem=send_sem.at[0], recv_sem=recv_sem.at[0],
        device_id=(mem, lax.rem(me + 1, ns)), device_id_type=MESH,
    )
    down = pltpu.make_async_remote_copy(
        src_ref=dn_s, dst_ref=dn_r, send_sem=send_sem.at[1], recv_sem=recv_sem.at[1],
        device_id=(mem, lax.rem(me + ns - 1, ns)), device_id_type=MESH,
    )
    up.start()
    down.start()

    def spread_early(i, carry):
        k = far_first(i)
        pltpu.make_async_remote_copy(
            src_ref=early_s, dst_ref=early_r.at[k], send_sem=send_sem.at[7],
            recv_sem=recv_sem.at[7], device_id=(mem, lax.rem(me + k + 1, ns)),
            device_id_type=MESH,
        ).start()
        return carry

    lax.fori_loop(0, ns - 1, spread_early, 0, unroll=True)

    my_patch = [slot[me * slots + s] for s in range(slots)]
    held_parent = [p >> 1 for p in my_patch]

    def find_slot(k, carry):
        d = lax.rem(me + k + 1, ns)
        which = jnp.int32(0)
        for s in range(1, slots):
            which = jnp.where(held_parent[s] == d, s, which)
        sidx[k] = which
        return carry

    lax.fori_loop(0, ns, find_slot, 0)

    xb[...] = jnp.zeros(xb.shape, f32)
    gx[...] = jnp.zeros(gx.shape, f32)
    tp[...] = jnp.zeros(tp.shape, f32)
    pz[...] = jnp.zeros(pz.shape, f32)
    up.wait()
    down.wait()

    strip_row = iota((8, cols), 0)
    strip_lane = iota((8, cols), 1)

    def strip(o):
        inside = None
        for j in range(2):
            hit = (
                (strip_row + o >= r0[j]) & (strip_row + o < r0[j] + bl)
                & (strip_lane >= c0[j]) & (strip_lane < c0[j] + bl)
            )
            inside = hit if inside is None else inside | hit
        part = slice(o, o + 8)
        faces_here = (op[0, part, :].astype(f32), op[1, part, :].astype(f32))
        return inside, part, faces_here

    def strip_south(x, below):
        return jnp.where(strip_row == 0, below, roll(x, 1, 0))

    def strip_north(x, above):
        return jnp.where(strip_row == 7, above, roll(x, 7, 0))

    def renew(o, h, below_of, above, above2_of):
        inside, part, (oe_s, on_s) = strip(o)
        ce_s, cn_s = ce[part, :], cn[part, :]
        u = oe_s * cs[1, part, :] - ce_s * (east(h) - h)
        v = on_s * cs[2, part, :] - cn_s * (strip_north(h, above) - h)
        below = below_of(h)
        above2 = above2_of(v)
        hm = jnp.where(inside, 0.0, h)
        um = jnp.where(inside, 0.0, u)
        vm = jnp.where(inside, 0.0, v)
        second = hm - C * (um - west(um) + vm - strip_south(vm, below))
        u2 = oe_s * um - ce_s * (east(second) - second)
        v2 = on_s * vm - cn_s * (strip_north(second, above2) - second)
        t1[1, part, :], t1[2, part, :], t2[part, :] = um, vm, second
        for f, held in ((2, second), (5, u2), (8, vm), (9, v2)):
            for tile in range(cols // 128):
                ex[f, tile, part, :] = held[:, 128 * tile : 128 * tile + 128]
        return above2

    low = me > 0
    high = me < ns - 1
    h1_m = up_r[0:1, :]
    v0_m = jnp.where(low, up_r[1:2, :], 0.0)
    v0_top = cs[2, rows - 1 : rows, :]
    h1_p = jnp.where(high, dn_r[0:1, :] + C * v0_top, 0.0)
    u1_p = dn_r[4:5, :] * dn_r[1:2, :] - dn_r[5:6, :] * (east(h1_p) - h1_p)
    v1_p = dn_r[6:7, :] * dn_r[2:3, :] - dn_r[7:8, :] * (dn_r[3:4, :] - h1_p)

    def below_first(h):
        return jnp.where(low, up_r[2:3, :] * v0_m - up_r[3:4, :] * (h[0:1] - h1_m), 0.0)

    def above_last(v):
        return jnp.where(high, h1_p - C * (u1_p - west(u1_p) + v1_p - v[7:8]), 0.0)

    h_low = t1[0, 0:8, :]
    h_low = jnp.where(strip_row == 0, h_low + C * v0_m, h_low)
    above_low = t1[0, 8:9, :]
    second_above_low = t2[8:9, :]
    below_high = t1[2, rows - 9 : rows - 8, :]
    renew(0, h_low, below_first, above_low, lambda v: second_above_low)
    h2_p = renew(rows - 8, t1[0, rows - 8 : rows, :], lambda h: below_high, h1_p, above_last)

    payload = cycles((2,))
    pay_s[...] = payload
    pay_r[ns - 1] = payload

    def spread_payload(i, carry):
        k = far_first(i)
        pltpu.make_async_remote_copy(
            src_ref=pay_s, dst_ref=pay_r.at[k], send_sem=send_sem.at[2],
            recv_sem=recv_sem.at[2], device_id=(mem, lax.rem(me + k + 1, ns)),
            device_id_type=MESH,
        ).start()
        return carry

    lax.fori_loop(0, ns - 1, spread_payload, 0, unroll=True)

    def all_of(ref, count, sem):
        part = ref.at[pl.ds(0, count)]
        pltpu.make_async_copy(part, part, sem).wait()

    cell = gauge[...]
    grow = cell // cols
    gcol = cell - grow * cols
    own_row = grow - me * rows
    covered = None
    for j in range(2):
        down = own_row - r0[j]
        right = gcol - c0[j]
        hit = (
            (down >= 0) & (right >= 0) & (down <= bl) & (right <= bl)
            & ((down < bl) | (right < bl))
        )
        covered = hit if covered is None else covered | hit
    pick_col = jnp.where(iota((cols, 128), 0) == gcol, 1.0, 0.0)
    found = dot3(t2[...], pick_col)
    outside = jnp.sum(
        jnp.where((iota((rows, 128), 0) == own_row) & jnp.logical_not(covered), found, 0.0),
        axis=0, keepdims=True,
    )

    rc_i = iota((fl, 128), 0)
    rc_l = iota((fl, 128), 1)
    spread_rows = jnp.where((rc_l & 31) == (rc_i >> 2), 1.0, 0.0)
    spread_lanes = jnp.where((rc_i & 31) == (rc_l >> 2), 1.0, 0.0)
    mean_h = jnp.where((rc_i >> 2) == rc_l, 0.25, 0.0)
    mean_u = jnp.where(rc_i == 4 * (rc_l - 32) + 3, 1.0, 0.0)
    mean_v = jnp.where((rc_i >> 2) == rc_l - 64, 0.25, 0.0)
    lane_nb = iota((nb, 128), 1)

    def expand(old, diff):
        both = jnp.concatenate([old, diff], axis=0)
        ycol[:, 0 : 2 * nb] = dot3_nt(spread_rows, both)
        yrow[...] = dot3(both, spread_lanes)
        for s in range(slots):
            eo[s] = roll(ycol[...], 127 - 8 * s, 1)
            ed[s] = roll(ycol[...], (255 - 8 * s - nb) % 128, 1)

    lane_f = iota((fl, 128), 1)
    every = range(slots)

    def update(k, final):
        kf = k.astype(f32)
        wf = (2.0 * kf + 1.0) / (2.0 * REFINE)
        wl = (kf + 1.0) / REFINE
        weight_of = jnp.where(lane == fl - 1, wl, wf)
        for s in every:
            n, o = 8 * s + 2, 8 * s + 3
            fv[s, 7:8, :] = yrow[o : o + 1, :] + wf * yrow[nb + o : nb + o + 1, :]
            fh[s, 8 + fl : 9 + fl, :] = yrow[n : n + 1, :] + wl * yrow[nb + n : nb + n + 1, :]
        held = []
        for s in every:
            edge = eo[s] + weight_of * ed[s]
            u = fu[s]
            v = fv[s, 8 : 8 + fl, :]
            v_s = fv[s, 7 : 7 + fl, :]
            u_w = jnp.where(lane_f == 0, edge, roll(u, 1, 1))
            h = fh[s, 8 : 8 + fl, :] - C * (u - u_w + v - v_s)
            held.append((h, u, v, edge))
        for s in every:
            fh[s, 8 : 8 + fl, :] = held[s][0]
        for s in every:
            h, u, v, edge = held[s]
            cdf = C * fd[s]
            h_e = jnp.where(lane_f == fl - 1, edge, roll(h, fl - 1, 1))
            h_n = fh[s, 9 : 9 + fl, :]
            u = u - cdf * (h_e - h)
            v = v - cdf * (h_n - h)
            if final:
                used = my_patch[s] >= 0
                fine_out[0, 0, s] = jnp.where(used, h, 0.0)
                fine_out[0, 1, s] = jnp.where(used, u, 0.0)
                fine_out[0, 2, s] = jnp.where(used, v, 0.0)
            else:
                fu[s] = u
                fv[s, 8 : 8 + fl, :] = v

    def fine_steps(last):
        def step(k, carry):
            update(k, False)
            return carry

        lax.fori_loop(0, REFINE - 1 if last else REFINE, step, 0, unroll=True)
        if last:
            update(jnp.int32(REFINE - 1), True)

    def averages(held):
        for s in range(slots):
            span = slice(bl * s, bl * s + bl)
            parts = [held(0, s, i) for i in range(REFINE)]
            red[0, span, :] = 0.25 * ((parts[0] + parts[1]) + (parts[2] + parts[3]))
            parts = [held(1, s, i) for i in range(REFINE)]
            red[1, span, :] = 0.25 * ((parts[0] + parts[1]) + (parts[2] + parts[3]))
            red[2, span, :] = held(2, s, REFINE - 1)
        return dot3(red[0], mean_h) + dot3(red[1], mean_u) + dot3(red[2], mean_v)

    def inner(f, s, i):
        if f == 1:
            return fu[s, pl.ds(i, bl, stride=REFINE), :]
        return (fh, None, fv)[f][s, pl.ds(8 + i, bl, stride=REFINE), :]

    def outer(f, s, i):
        return fine_out[0, f, s, pl.ds(i, bl, stride=REFINE), :]

    for load in loads[3:]:
        load.wait()
    def take(held, s, rows_from, count, slab):
        at = lax.rem(me - slab - 1 + 2 * ns, ns)
        p = jnp.maximum(my_patch[s], 0)
        got = held[at, pl.ds((p & 1) * 4 + rows_from, count), :]
        return jnp.where(my_patch[s] >= 0, got, 0.0)

    all_of(early_r, ns - 1, recv_sem.at[7])
    for s in range(slots):
        p = jnp.maximum(my_patch[s], 0)
        parent = p >> 1
        got = take(early_r, s, 0, 4, parent)
        lower = take(early_r, s, 3, 1, jnp.maximum(parent - 1, 0))
        mine = got[3:4]
        fix = C * roll(mine, 64, 1) * roll(lower, 96, 1)
        fixed = (lane >= 32) & (lane < 64) & (anchor[0, p] == 1) & (parent > 0)
        xb[8 * s : 8 * s + 3, :] = got[0:3]
        xb[8 * s + 3 : 8 * s + 4, :] = jnp.where(fixed, mine + fix, mine)

    x = xb[...]
    left = lane_nb < 32
    expand(
        jnp.where(left, x, 0.0), jnp.where(left, roll(x, 96, 1) - x, 0.0)
    )
    fine_steps(False)

    mean = averages(inner)
    pick_i = iota((16, 128), 0)
    pick_l = iota((16, 128), 1)
    pick = jnp.where((pick_i == 0) & (pick_l == 63), C, 0.0)
    pick = pick + jnp.where((pick_i == 1) & (pick_l == 0), 1.0, 0.0)
    pick = pick - jnp.where((pick_i == 1) & ((pick_l == 32) | (pick_l == 64)), C, 0.0)
    pick = pick + jnp.where((pick_i == 9) & (pick_l == 64), C, 0.0)
    for s in range(slots):
        tp[s, 64:96, :] = mean[bl * s : bl * s + bl]
    for s in range(slots):
        side = dot3_nt(pick, tp[s])
        side = side[0:8] + roll(side[8:16], 1, 1)
        gx[8 * s : 8 * s + 2, :] = side[0:2]
        top = tp[s, 95:96, :]
        low_row = tp[s, 64:65, :]
        gx[8 * s + 2 : 8 * s + 3, :] = C * top
        gx[8 * s + 3 : 8 * s + 4, :] = roll(low_row, 64, 1) - C * (
            roll(low_row, 32, 1) - jnp.where(lane > 64, roll(low_row, 33, 1), 0.0) + low_row
        )
    all_of(pay_r, ns - 1, recv_sem.at[2])
    mid = (lane_nb >= 64) & (lane_nb < 96)
    for s in range(slots):
        xb[8 * s : 8 * s + 4, :] = take(pay_r, s, 0, 4, jnp.maximum(my_patch[s], 0) >> 1)
    x = jnp.where(mid, xb[...], x)
    new = x - roll(x, 96, 1) * gx[...]
    expand(
        jnp.where((lane_nb >= 32) & (lane_nb < 64), x, 0.0),
        jnp.where(mid, new - roll(x, 32, 1), 0.0),
    )
    fine_steps(True)
    mean = averages(outer)

    rel_col = jnp.full((1, 128), -1, jnp.int32)
    rel_row = jnp.full((1, 128), -1, jnp.int32)
    for s in range(slots):
        p = jnp.maximum(my_patch[s], 0)
        down = jnp.where(my_patch[s] >= 0, grow - ((p >> 1) * rows + anchor[0, p]), -1)
        right = gcol - anchor[1, p]
        in_rows = (down >= 0) & (down < bl)
        in_cols = (right >= 0) & (right < bl)
        hit = in_rows & in_cols
        rel_col = jnp.where(hit, right, rel_col)
        rel_row = jnp.where(hit, down + bl * s, rel_row)
        hit = in_rows & (right == bl)
        rel_col = jnp.where(hit, 64 + down, rel_col)
        rel_row = jnp.where(hit, bl * slots + 8 * s, rel_row)
        hit = (down == bl) & in_cols
        rel_col = jnp.where(hit, 64 + right, rel_col)
        rel_row = jnp.where(hit, bl * slots + 8 * s + 2, rel_row)
    pick_col = jnp.where(rc_i == rel_col, 1.0, 0.0)
    found = dot3(jnp.concatenate([mean, new], axis=0), pick_col)
    at_row = iota((bl * slots + nb, 128), 0) == rel_row
    value = outside + jnp.sum(jnp.where(at_row, found, 0.0), axis=0, keepdims=True)
    z_s[0] = value

    def send_member(i, carry):
        k = lax.rem(i + nm // 2 - 2, nm - 1)
        pltpu.make_async_remote_copy(
            src_ref=z_s.at[0], dst_ref=z_r.at[k], send_sem=send_sem.at[5],
            recv_sem=recv_sem.at[5], device_id=(lax.rem(mem + k + 1, nm), me),
            device_id_type=MESH,
        ).start()
        return carry

    lax.fori_loop(0, nm - 1, send_member, 0, unroll=True)
    for s in range(slots):
        tail = mean[bl * s + 24 : bl * s + 32]
        for i in range(3):
            piece = mean[bl * s + 8 * i : bl * s + 8 * i + 8]
            a2_p[s, 8 * i : 8 * i + 8, :] = jnp.where(
                lane8 < 96, piece, roll(tail, 96 - 32 * i, 1)
            )

    def send_mean(i, carry):
        k = far_first(i)
        a2_s[k] = a2_p[sidx[k]]
        pltpu.make_async_remote_copy(
            src_ref=a2_s.at[k], dst_ref=a2_r.at[k], send_sem=send_sem.at[4],
            recv_sem=recv_sem.at[4], device_id=(mem, lax.rem(me + k + 1, ns)),
            device_id_type=MESH,
        ).start()
        return carry

    lax.fori_loop(0, ns - 1, send_mean, 0)
    a2_r[ns - 1] = a2_p[sidx[ns - 1]]

    packed = jnp.zeros((nb, 128), f32)
    row_nb = iota((nb, 128), 0) & 7
    for q in range(4):
        here = (row_nb == q) & (lane_nb >= 32 * q) & (lane_nb < 32 * q + 32)
        packed = jnp.where(here, roll(new, (32 * q + 64) % 128, 1), packed)
    for s in range(slots):
        m1_p[s] = jnp.sum(packed[8 * s : 8 * s + 8], axis=0, keepdims=True)

    def send_cycle(i, carry):
        k = far_first(i)
        m1_s[k] = m1_p[sidx[k]]
        pltpu.make_async_remote_copy(
            src_ref=m1_s.at[k], dst_ref=m1_r.at[k], send_sem=send_sem.at[3],
            recv_sem=recv_sem.at[3], device_id=(mem, lax.rem(me + k + 1, ns)),
            device_id_type=MESH,
        ).start()
        return carry

    lax.fori_loop(0, ns - 1, send_cycle, 0)
    m1_r[ns - 1] = m1_p[sidx[ns - 1]]

    def weight(m):
        return (1.0 + 2.0 * m.astype(f32) / (nm - 1)) / (2.0 * nm)

    weights = [weight(lax.rem(mem - k - 1 + nm, nm)) for k in range(nm - 1)]
    center = weight(mem) * value
    all_of(z_r, nm - 1, recv_sem.at[5])

    for k in range(nm - 1):
        center = center + weights[k] * z_r[k]
    g_s[0] = value - center

    def send_gauge(i, carry):
        k = far_first(i)
        pltpu.make_async_remote_copy(
            src_ref=g_s.at[0], dst_ref=g_r.at[k], send_sem=send_sem.at[6],
            recv_sem=recv_sem.at[6], device_id=(mem, lax.rem(me + k + 1, ns)),
            device_id_type=MESH,
        ).start()
        return carry

    lax.fori_loop(0, ns - 1, send_gauge, 0, unroll=True)

    def find_owner(i, carry):
        p = slot[i]
        return tuple(
            jnp.where(p == 2 * me + j, i, carry[j]) for j in range(2)
        )

    where_held = lax.fori_loop(0, ns * slots, find_owner, (jnp.int32(0), jnp.int32(0)))
    owner_at = [lax.rem(me - w // slots - 1 + 2 * ns, ns) for w in where_held]

    all_of(m1_r, ns - 1, recv_sem.at[3])
    rowh = iota((rows, 128), 0)
    laneh = iota((rows, 128), 1)
    h2 = t2[...]
    fixes = []
    for j in range(2):
        got = m1_r[owner_at[j]]
        match = (laneh & 31) == rowh - r0[j]
        rows_in = (rowc >= r0[j]) & (rowc < r0[j] + bl)
        cols_in = (lanec >= c0[j]) & (lanec < c0[j] + bl)
        east_col = jnp.sum(
            jnp.where(match & (laneh < 32), got, 0.0), axis=1, keepdims=True
        )
        west_col = jnp.sum(
            jnp.where(match & (laneh >= 32) & (laneh < 64), got, 0.0), axis=1, keepdims=True
        )
        got8 = jnp.broadcast_to(got, (8, 128))
        north_row = roll(got8, (c0[j] - 64) & 127, 1)[0:1]
        south_row = roll(got8, (c0[j] - 96) & 127, 1)[0:1]
        north_row = jnp.concatenate([north_row] * (cols // 128), axis=1)
        south_row = jnp.concatenate([south_row] * (cols // 128), axis=1)
        h2 = jnp.where(rows_in & (lanec == c0[j] + bl), east_col, h2)
        h2 = jnp.where(cols_in & (rowc == r0[j] + bl), north_row, h2)
        fixes.append((rows_in & (lanec == c0[j] - 1), west_col,
                      cols_in & (rowc == r0[j] - 1), south_row))
    u1, v1 = t1[1], t1[2]
    u2 = oe * u1 - ce[...] * (east(h2) - h2)
    v2 = on * v1 - cn[...] * (north(h2, h2_p) - h2)
    for at_west, west_col, at_south, south_row in fixes:
        u2 = jnp.where(at_west, west_col, u2)
        v2 = jnp.where(at_south, south_row, v2)
    coarse_out[0, 0], coarse_out[0, 1], coarse_out[0, 2] = h2, u2, v2

    all_of(a2_r, ns - 1, recv_sem.at[4])
    for j in range(2):
        at = owner_at[j]
        tail = jnp.zeros((8, 128), f32)
        for i in range(3):
            piece = a2_r[at, 8 * i : 8 * i + 8, :]
            pz[j, 32 + 8 * i : 40 + 8 * i, :] = piece
            here = (lane8 >= 32 * i) & (lane8 < 32 * i + 32)
            tail = jnp.where(here, roll(piece, 32 + 32 * i, 1), tail)
        pz[j, 56:64, :] = tail
        moved = pz[j, pl.ds(32 - r0[j], rows), :]
        inside = (
            (rowc >= r0[j]) & (rowc < r0[j] + bl) & (lanec >= c0[j]) & (lanec < c0[j] + bl)
        )
        for field in range(3):
            placed = roll(moved, (c0[j] - 32 * field) & 127, 1)
            placed = jnp.concatenate([placed] * (cols // 128), axis=1)
            coarse_out[0, field] = jnp.where(inside, placed, coarse_out[0, field])

    all_of(g_r, ns - 1, recv_sem.at[6])
    total = g_s[0]
    for k in range(ns - 1):
        total = total + g_r[k]
    spread_out[...] = total

    all_of(early_r, ns - 1, send_sem.at[7])
    all_of(pay_r, ns - 1, send_sem.at[2])
    all_of(m1_r, ns - 1, send_sem.at[3])
    all_of(a2_r, ns - 1, send_sem.at[4])
    all_of(z_r, nm - 1, send_sem.at[5])
    all_of(g_r, ns - 1, send_sem.at[6])


def store_results(coarse, fine, spread, coarse_out, fine_out, spread_out, sem):
    pairs = ((coarse, coarse_out), (fine, fine_out), (spread, spread_out))
    copies = [pltpu.make_async_copy(a, b, sem.at[i]) for i, (a, b) in enumerate(pairs)]
    for copy in copies:
        copy.start()
    for copy in copies:
        copy.wait()


def shards(
    coarse_state, coarse_seabed, open_faces, fine_state, fine_seabed, slot_patch, patch_anchor,
    gauge_cells,
):
    ns = lax.axis_size("space")
    nm = lax.axis_size("member")
    rows, cols = coarse_seabed.shape
    slots, fl = fine_seabed.shape[0], fine_seabed.shape[-1]
    nb = 8 * slots
    vmem, hbm, smem = (
        pl.BlockSpec(memory_space=space) for space in (pltpu.VMEM, pltpu.HBM, pltpu.SMEM)
    )

    def buf(*shape):
        return pltpu.VMEM(shape, f32)

    shapes = (coarse_state.shape, fine_state.shape, (1, gauge_cells.shape[0]))
    results = pl.pallas_call(
        functools.partial(kernel, ns, nm, slots),
        out_shape=tuple(pltpu.VMEM(shape, f32) for shape in shapes),
        in_specs=[smem, smem, vmem, hbm, hbm, hbm, hbm, hbm],
        out_specs=(vmem, vmem, vmem),
        scratch_shapes=[
            buf(3, rows, cols), buf(rows, cols), pltpu.VMEM((2, rows, cols), jnp.int32),
            buf(3, rows, cols), buf(rows, cols), buf(11, cols // 128, rows, 128),
            buf(rows, cols), buf(rows, cols),
            buf(slots, fl + 16, fl), buf(slots, fl, fl), buf(slots, fl + 16, fl),
            buf(slots, fl, fl), buf(slots, fl, 128), buf(slots, fl, 128),
            buf(8, cols), buf(8, cols), buf(8, cols), buf(8, cols),
            buf(2, 4, 2, 8, 128), buf(8, 128), buf(ns, 8, 128),
            buf(8, 128), buf(ns, 8, 128), buf(nb, 128), buf(nb, 128),
            buf(fl, 128), buf(2 * nb, 128), buf(3, slots * fl // REFINE, 128),
            buf(slots, 128, 128),
            buf(slots, 1, 128), buf(ns, 1, 128), buf(ns, 1, 128),
            buf(slots, 24, 128), buf(ns, 24, 128), buf(ns, 24, 128),
            buf(2, 128, 128),
            buf(1, 1, 128), buf(nm, 1, 128), buf(1, 1, 128), buf(ns, 1, 128),
            pltpu.SMEM((ns,), jnp.int32),
            pltpu.SemaphoreType.DMA((7,)), pltpu.SemaphoreType.DMA((8,)),
            pltpu.SemaphoreType.DMA((8,)),
        ],
        compiler_params=pltpu.CompilerParams(
            collective_id=0, has_side_effects=True, vmem_limit_bytes=56 * 1024 * 1024
        ),
    )(
        slot_patch, patch_anchor.T, gauge_cells.reshape(1, -1),
        *(pltpu.with_memory_space_constraint(x, pltpu.HBM)
          for x in (coarse_state, coarse_seabed, open_faces, fine_state, fine_seabed)),
    )
    return pl.pallas_call(
        store_results,
        out_shape=tuple(jax.ShapeDtypeStruct(shape, f32) for shape in shapes),
        in_specs=[vmem] * 3,
        out_specs=(hbm,) * 3,
        scratch_shapes=[pltpu.SemaphoreType.DMA((3,))],
    )(*(pltpu.with_memory_space_constraint(x, pltpu.VMEM) for x in results))


def solution(mesh):
    return jax.shard_map(
        shards,
        mesh=mesh,
        in_specs=(
            P("member", None, "space", None),
            P("space", None),
            P(None, "space", None),
            P("member", None, "space", None, None),
            P("space", None, None),
            P(),
            P(),
            P(),
        ),
        out_specs=(
            P("member", None, "space", None),
            P("member", None, "space", None, None),
            P("member", None),
        ),
        check_vma=False,
    )
```
